32 devices in a mesh: dp: 8 (over y, x, core), expert: 4 (over z).
Axes of the slice: x: 2, y: 2, z: 4, core: 2. Of those that a mesh axis runs over, the one named last changes fastest.
Arguments:
- tokens: bfloat16 [8192, 768], P(('dp', 'expert')), may hold values from -6 to 6
- timestep: int32 [32], P(('dp', 'expert')), may hold values from 0 to 999
- labels: int32 [32], P(('dp', 'expert')), may hold values from 0 to 999
- routes: int32 [8192, 2], P(('dp', 'expert')), may hold values from 0 to 7, all different within a row; in each aligned block of 256 rows (0 to 255, 256 to 511, ...) at most 128 rows name the same one
- expert_gates: float32 [8192, 2], P(('dp', 'expert')), may hold values from 0.2 to 0.8
- grad_out: bfloat16 [8192, 768], P(('dp', 'expert')), may hold values from -6 to 6
- ada_weight: bfloat16 [768, 4608], P(None, ('dp', 'expert')), may hold values from -0.21875 to 0.21875
- ada_bias: bfloat16 [4608], P(('dp', 'expert')), may hold values from -2 to 2
- qkv_weight: bfloat16 [768, 2304], P(None, ('dp', 'expert')), may hold values from -0.21875 to 0.21875
- proj_weight: bfloat16 [768, 768], P(None, ('dp', 'expert')), may hold values from -0.875 to 0.875
- shared_up: bfloat16 [768, 3072], P(None, ('dp', 'expert')), may hold values from -0.21875 to 0.21875
- shared_down: bfloat16 [3072, 768], P(None, ('dp', 'expert')), may hold values from -0.109375 to 0.109375
- expert_up: bfloat16 [8, 768, 3072], P('expert', None, 'dp'), may hold values from -0.21875 to 0.21875
- expert_down: bfloat16 [8, 3072, 768], P('expert', None, 'dp'), may hold values from -0.109375 to 0.109375
- time_table: bfloat16 [1000, 768], P(None, ('dp', 'expert')), may hold values from -5 to 5
- class_table: bfloat16 [1000, 768], P(None, ('dp', 'expert')), may hold values from -5 to 5
Outputs:
- block_out: bfloat16 [8192, 768], P(('dp', 'expert'))
- tokens_grad: float32 [8192, 768], P(('dp', 'expert'))
- cond_grad: float32 [32, 768], P(('dp', 'expert'))
- gates_grad: float32 [8192, 2], P(('dp', 'expert'))
- ada_weight_grad: float32 [768, 4608], P(None, ('dp', 'expert'))
- ada_bias_grad: float32 [4608], P(('dp', 'expert'))
- qkv_weight_grad: float32 [768, 2304], P(None, ('dp', 'expert'))
- proj_weight_grad: float32 [768, 768], P(None, ('dp', 'expert'))
- shared_up_grad: float32 [768, 3072], P(None, ('dp', 'expert'))
- shared_down_grad: float32 [3072, 768], P(None, ('dp', 'expert'))
- expert_up_grad: float32 [8, 768, 3072], P('expert', None, 'dp')
- expert_down_grad: float32 [8, 3072, 768], P('expert', None, 'dp')
- time_table_grad: float32 [1000, 768], P(None, ('dp', 'expert'))
- class_table_grad: float32 [1000, 768], P(None, ('dp', 'expert'))
The draws below stay inside these ranges and needn't reach their ends.
Inputs may be any that keep to these rules, and one draw needn't show every extreme that they name: `routes`: the two experts of a patch differ. Among the pairs of one device's 256 patches, no expert is named more than 128 times, a bound that some block reaches.
All inputs are finite; a program needn't handle non-finite values.
Results may differ from the reference program's by a relative error of at most 0.028.
Values may be sent and summed in bfloat16 or wider, within the bound.
No kernel may reach another device: no remote copies, remote signals or barrier semaphores. Data moves between devices by JAX's collectives and lax.ppermute only.
A program may use at most 256 MiB of HBM per device.

```python
import math
import jax
import jax.numpy as jnp
import numpy as np
from jax import lax

D = 768
H = 12
HD = 64
FF = 3072
NT = 1000
NC = 1000
EXPERTS = 8
SEQ = 256
TOK_DEV = 256
CAP = 128
LATENTS = 32
TOKENS = 8192
N_DP = 8
N_EXPERT = 4


def place_ends(values, stream_key, smallest, top_value):
    dims = values.shape
    place = [jax.random.randint(jax.random.fold_in(stream_key, axis), (), 0, dims[axis]) for axis in range(len(dims))]
    values = values.at[tuple(place)].set(smallest)
    longest = dims.index(max(dims))
    place[longest] = (place[longest] + 1) % dims[longest]
    return values.at[tuple(place)].set(top_value)


def strengthened(array, stream_key, source, target, blocks, factor):
    def block_of(axis_at):
        return (jnp.arange(array.shape[axis_at]) // (array.shape[axis_at] // blocks)).reshape((-1,) + (1,) * (array.ndim - 1 - axis_at))

    first = jax.random.permutation(stream_key, blocks)[block_of(target)]
    far = (block_of(target) + blocks // 2) % blocks
    return jnp.where((block_of(source) == first) | (block_of(source) == far), factor * array, array)


def block_scale(rng, dims, cuts, least, largest):
    level = 1.0
    for axis_at, parts in cuts:
        steps = jax.random.uniform(jax.random.fold_in(jax.random.fold_in(rng, 6), axis_at), (parts,), jnp.float32, least / len(cuts), largest / len(cuts))
        level = level * jnp.repeat(jnp.exp(steps), dims[axis_at] // parts).reshape((-1,) + (1,) * (len(dims) - 1 - axis_at))
    return level


def rank_table(number_of, skew):
    loads = [(1 << 20) // math.isqrt(standing ** skew) + 1 for standing in range(1, number_of + 1)]
    scale = 1 + sum(loads) // (1 << 30)
    return np.cumsum(np.array([max(1, weight // scale) for weight in loads]))


def skewed_ids(rng, dims, number_of, skew):
    listing = rank_table(number_of, skew)
    pick = jax.random.randint(jax.random.fold_in(rng, 1), dims, 0, int(listing[number_of - 1]))
    standing = jnp.searchsorted(jnp.asarray(listing, jnp.int32), pick, side="right")
    return jax.random.permutation(jax.random.fold_in(rng, 2), number_of)[standing].astype(jnp.int32)


def routed_block(rng, own, number, rows, amount, top, reach, skew):
    sequence = jax.random.permutation(rng, amount)
    crowded, usual = portions_of(amount, rows * top, reach, skew, True), portions_of(amount, rows * top, reach, skew, False)
    places = jnp.arange(amount)

    def named(tallies, rotation):
        used = int((tallies > 0).sum())
        fixed = max(1, used // 4)
        moved = fixed + (places - fixed + rotation * (used - fixed)) % max(1, amount - fixed)
        return jnp.zeros((amount,), jnp.int32).at[sequence[jnp.where(places < fixed, places, moved)]].set(jnp.asarray(tallies, jnp.int32))

    tallies = jnp.where(number % 4 == 0, named(crowded, number // 4), named(usual, number - number // 4 - 1))
    mixed = jax.random.permutation(jax.random.fold_in(own, 3), amount)
    donor, receiver = mixed[0:amount // 2 * 2:2], mixed[1:amount // 2 * 2:2]
    room = jnp.minimum(tallies[donor] - 1, reach - tallies[receiver]) // 2
    room = jnp.where((donor == sequence[0]) | (receiver == sequence[0]) | (tallies[receiver] == 0), 0, jnp.maximum(room, 0))
    moved = jax.random.randint(jax.random.fold_in(own, 4), (amount // 2,), 0, 1 << 20) % (room + 1)
    tallies = tallies.at[donor].add(-moved).at[receiver].add(moved)
    items = jnp.searchsorted(jnp.cumsum(tallies), jnp.arange(rows * top), side="right").astype(jnp.int32)
    table = items.reshape(top, rows).T
    table = table[jax.random.permutation(jax.random.fold_in(own, 1), rows)]
    rotation = jax.random.randint(jax.random.fold_in(own, 2), (rows, 1), 0, top)
    return jnp.take_along_axis(table, (jnp.arange(top)[None, :] + rotation) % top, axis=1)


def portions_of(count, total, reach, skew, full):
    loads = [(1 << 20) // math.isqrt(grade ** skew) + 1 for grade in range(1, count + 1)]
    largest = reach if full else min(reach, max(-(-total // count), total * loads[0] // sum(loads)))
    least = 1 if total - largest >= count - 1 else 0
    given, surplus = [largest] + [least] * (count - 1), total - largest - least * (count - 1)
    while surplus > 0:
        free = [i for i in range(1, count) if given[i] < largest] or [i for i in range(1, count) if given[i] < reach]
        whole, remaining = sum([loads[i] for i in free]), surplus
        for i in free:
            more = min(reach - given[i], max(1, remaining * loads[i] // whole), surplus)
            given[i] = given[i] + more
            surplus = surplus - more
    return np.array(given)


def bell_draw(key, dims, spread, limit, cuts=(), dtype=jnp.bfloat16):
    factor_of = block_scale(key, dims, cuts, -0.22, 0.18) if cuts else 1.0
    array = jax.random.normal(key, dims, jnp.float32) * spread * factor_of
    return jnp.minimum(jnp.maximum(array, -limit), limit).astype(dtype)


def gaussian_with(stream_key, extent, deviation, bound, shards, heavy, held_as=jnp.bfloat16):
    entries = deviation * jax.random.normal(stream_key, extent, jnp.float32)
    if shards:
        entries = entries * block_scale(stream_key, extent, shards, -0.22, 0.18)
    return jnp.clip(strengthened(entries, jax.random.fold_in(stream_key, 3), *heavy), -bound, bound).astype(held_as)


def setup_inputs(seed: int = 0) -> dict:
    streams_of = jax.random.split(jax.random.key(seed), 17)
    tokens = bell_draw(streams_of[0], (TOKENS, D), 1.0, 6.0, ((0, 32),))
    timestep = place_ends(skewed_ids(streams_of[1], (LATENTS,), NT, 2), jax.random.fold_in(streams_of[1], 3), 0, NT - 1).astype(jnp.int32)
    labels = place_ends(jax.random.randint(streams_of[2], (LATENTS,), 0, NC), jax.random.fold_in(streams_of[2], 1), 0, NC - 1).astype(jnp.int32)
    routes_keys = jax.random.split(jax.random.fold_in(streams_of[3], 1), TOKENS // TOK_DEV)
    routes_turns = jax.random.permutation(jax.random.fold_in(streams_of[3], 3), TOKENS // TOK_DEV)
    routes = jax.vmap(lambda own, number: routed_block(jax.random.fold_in(streams_of[3], 2), own, number, TOK_DEV, EXPERTS, 2, CAP, 2))(routes_keys, routes_turns).reshape((TOKENS, 2))
    expert_gates = jnp.clip(0.2 + 0.6 * jax.random.uniform(streams_of[4], (TOKENS, 2), jnp.float32) ** block_scale(streams_of[4], (TOKENS, 2), ((0, 32),), -0.2, 0.2), 0.2, 0.8)
    grad_out = gaussian_with(streams_of[5], (TOKENS, D), 1.0, 6.0, ((0, 32),), (0, 1, 32, 2.75))
    ada_weight = bell_draw(streams_of[6], (D, 6 * D), D ** -0.5, 0.21875, ((1, 32),))
    ada_bias = bell_draw(streams_of[7], (6 * D,), 0.3, 2.0, ((0, 32),))
    qkv_weight = bell_draw(streams_of[8], (D, 3 * D), D ** -0.5, 0.21875, ((1, 32),))
    proj_weight = bell_draw(streams_of[9], (D, D), (D // 16) ** -0.5, 0.875, ((1, 32),))
    shared_up = bell_draw(streams_of[10], (D, FF), D ** -0.5, 0.21875, ((1, 32),))
    shared_down = bell_draw(streams_of[11], (FF, D), FF ** -0.5, 0.109375, ((1, 32),))
    expert_up = bell_draw(streams_of[12], (EXPERTS, D, FF), D ** -0.5, 0.21875, ((0, 4), (2, 8)))
    expert_down = bell_draw(streams_of[13], (EXPERTS, FF, D), FF ** -0.5, 0.109375, ((0, 4), (2, 8)))
    time_table = bell_draw(streams_of[14], (NT, D), 1.0, 5.0, ((1, 32),))
    class_table = bell_draw(streams_of[15], (NC, D), 1.0, 5.0, ((1, 32),))
    return {"tokens": tokens, "timestep": timestep, "labels": labels, "routes": routes, "expert_gates": expert_gates, "grad_out": grad_out, "ada_weight": ada_weight, "ada_bias": ada_bias, "qkv_weight": qkv_weight, "proj_weight": proj_weight, "shared_up": shared_up, "shared_down": shared_down, "expert_up": expert_up, "expert_down": expert_down, "time_table": time_table, "class_table": class_table}


@jax.custom_vjp
def low(v):
    return lax.optimization_barrier(v.astype(jnp.bfloat16)).astype(jnp.float32)

@jax.custom_vjp
def low_back(v):
    return v

def low_keep(v):
    return (low(v), None)

def low_pass(kept, grad):
    return (grad,)

def back_keep(v):
    return (v, None)

def back_low(kept, grad):
    return (low(grad),)
low.defvjp(low_keep, low_pass)
low_back.defvjp(back_keep, back_low)

def matmul(left, right):
    return jnp.dot(left, right, precision=lax.Precision.HIGHEST, preferred_element_type=jnp.float32)

def layer_norm(values):
    center = values - lax.optimization_barrier(jnp.mean(values, axis=-1, keepdims=True))
    return center * lax.rsqrt(lax.optimization_barrier(jnp.mean(center * center, axis=-1, keepdims=True)) + 1e-06)

def attend(pieces):
    queries, keys_in, values_in = pieces
    scores = low_back(jnp.einsum('gqhe,gkhe->ghqk', queries, keys_in, precision=lax.Precision.HIGHEST) / math.sqrt(HD))
    shifted = jnp.exp(scores - lax.optimization_barrier(jnp.max(scores, axis=-1, keepdims=True)))
    probs = low(shifted / lax.optimization_barrier(jnp.sum(shifted, axis=-1, keepdims=True)))
    return jnp.einsum('ghqk,gkhe->gqhe', probs, values_in, precision=lax.Precision.HIGHEST)

def reference(tokens, timestep, labels, routes, expert_gates, grad_out, ada_weight, ada_bias, qkv_weight, proj_weight, shared_up, shared_down, expert_up, expert_down, time_table, class_table):
    latents = timestep.shape[0]
    flat_routes = routes.reshape(-1)
    pairs = flat_routes.shape[0]
    row_cap = N_DP * N_EXPERT * CAP
    picks = jnp.stack([jnp.nonzero(flat_routes == number, size=row_cap, fill_value=pairs)[0].astype(jnp.int32) for number in range(EXPERTS)])
    group = math.gcd(latents, max(1, 4096 // SEQ))

    def lookup(times_tab, class_tab):
        return times_tab[timestep] + class_tab[labels]
    condition, pull_cond = jax.vjp(lookup, time_table.astype(jnp.float32), class_table.astype(jnp.float32))

    def forward(resid, gate_vals, cond_vals, ada_w, ada_b, qkv_w, proj_w, up_w, down_w, exp_up, exp_down):
        modulation = low_back(matmul(low(jax.nn.silu(cond_vals)), ada_w) + ada_b)
        blocks = modulation.reshape(latents, 6, 1, D)
        shift_one, scale_one, gate_one = (blocks[:, 0], blocks[:, 1], blocks[:, 2])
        shift_two, scale_two, gate_two = (blocks[:, 3], blocks[:, 4], blocks[:, 5])
        resid3 = resid.reshape(latents, SEQ, D)
        normed_one = low(layer_norm(resid3) * (1.0 + scale_one) + shift_one).reshape(-1, D)
        qkv_all = low(low_back(matmul(normed_one, qkv_w))).reshape(latents // group, group, SEQ, 3, H, HD)
        mixed = lax.map(jax.checkpoint(attend), (qkv_all[:, :, :, 0], qkv_all[:, :, :, 1], qkv_all[:, :, :, 2]))
        attn_rows = low(low_back(mixed.reshape(-1, D)))
        projected = low_back(matmul(attn_rows, proj_w)).reshape(latents, SEQ, D)
        middle = resid3 + gate_one * projected
        normed_two = low(layer_norm(middle) * (1.0 + scale_two) + shift_two).reshape(-1, D)
        shared = low_back(matmul(low(jax.nn.gelu(low_back(matmul(normed_two, up_w)))), down_w))
        slot_rows = jnp.stack([low_back(normed_two), low_back(normed_two)], axis=1).reshape(-1, D)

        def run_expert(pieces):
            index, up_mat, down_mat = pieces
            taken = jnp.take(slot_rows, index, axis=0, mode='fill', fill_value=0.0)
            hidden = low(jax.nn.gelu(low_back(matmul(taken, up_mat))))
            return low(low_back(matmul(hidden, down_mat)))
        results = lax.map(jax.checkpoint(run_expert), (picks, exp_up, exp_down))
        routed = jnp.zeros((pairs, D), jnp.float32).at[picks.reshape(-1)].set(results.reshape(-1, D), mode='drop').reshape(-1, 2, D)
        branch = shared + lax.optimization_barrier(jnp.sum(gate_vals[:, :, None] * routed, axis=1))
        return middle + gate_two * branch.reshape(latents, SEQ, D)
    primals = (tokens.astype(jnp.float32), expert_gates.astype(jnp.float32), condition, ada_weight.astype(jnp.float32), ada_bias.astype(jnp.float32), qkv_weight.astype(jnp.float32), proj_weight.astype(jnp.float32), shared_up.astype(jnp.float32), shared_down.astype(jnp.float32), expert_up.astype(jnp.float32), expert_down.astype(jnp.float32))
    result, pull = jax.vjp(forward, *primals)
    grads = pull(grad_out.astype(jnp.float32).reshape(latents, SEQ, D))
    time_grad, class_grad = pull_cond(grads[2])
    return (result.reshape(-1, D).astype(jnp.bfloat16), grads[0], grads[2], grads[1], grads[3], grads[4], grads[5], grads[6], grads[7], grads[8], grads[9], grads[10], time_grad, class_grad)
```

```python
import math

import jax
import jax.numpy as jnp
from jax import lax
from jax.sharding import PartitionSpec as P

H = 12
HD = 64
SEQ = 256
CAP = 128
TP = 4
AXES = ("dp", "expert")
F32 = jnp.float32
BF16 = jnp.bfloat16


def layer_norm(values):
    center = values - jnp.mean(values, axis=-1, keepdims=True)
    inverse = lax.rsqrt(jnp.mean(center * center, axis=-1, keepdims=True) + 1e-06)
    return (center * inverse, inverse)


def norm_back(upstream, normed, inverse):
    mean_grad = jnp.mean(upstream, axis=-1, keepdims=True)
    mean_mix = jnp.mean(upstream * normed, axis=-1, keepdims=True)
    return inverse * (upstream - mean_grad - normed * mean_mix)


def dot_nn(left, right):
    return jnp.dot(left, right, preferred_element_type=F32)


def dot_tn(left, right):
    return lax.dot_general(left, right, (((0,), (0,)), ((), ())), preferred_element_type=F32)


def dot_nt(left, right):
    return lax.dot_general(left, right, (((1,), (1,)), ((), ())), preferred_element_type=F32)


def einsum(spec, left, right):
    return jnp.einsum(spec, left, right, preferred_element_type=F32)


def local_grad(function, inputs, upstream):
    unused, pull = jax.vjp(function, inputs)
    return pull(upstream)[0]


def swap(value, move):
    ndp, nz = lax.axis_size("dp"), lax.axis_size("expert")
    pairs = []
    for a in range(ndp):
        for b in range(nz):
            c, d = move(a, b)
            pairs.append((a * nz + b, c * nz + d))
    return lax.ppermute(value, AXES, pairs)


def swap_core(value):
    return swap(value, lambda a, b: (a ^ 1, b))


def swap_chip(value):
    return swap(value, lambda a, b: (a ^ 2, b))


def from_plane(value, step):
    nz = lax.axis_size("expert")
    return swap(value, lambda a, b: (a, (b - step) % nz))


def to_plane(value, step):
    nz = lax.axis_size("expert")
    return swap(value, lambda a, b: (a, (b + step) % nz))


def row_bit(bit):
    return (lax.axis_index("dp") // TP >> bit) & 1


def row_bits():
    return (lax.axis_size("dp") // TP).bit_length() - 1


def gather_rows(value):
    out = value[None]
    for bit in range(row_bits()):
        got = swap(out, lambda a, b, s=TP << bit: (a ^ s, b))
        high = row_bit(bit) == 1
        out = jnp.where(high, jnp.concatenate([got, out]), jnp.concatenate([out, got]))
    return out


def reduce_rows(value):
    for bit in reversed(range(row_bits())):
        half = value.shape[0] // 2
        high = row_bit(bit) == 1
        mine = jnp.where(high, value[half:], value[:half])
        other = jnp.where(high, value[:half], value[half:]).astype(BF16)
        value = mine + swap(other, lambda a, b, s=TP << bit: (a ^ s, b)).astype(F32)
    return value[0]


def exchange_tp(value):
    ndp = lax.axis_size("dp")
    groups = [list(range(i, i + TP)) for i in range(0, ndp, TP)]
    return lax.all_to_all(value, "dp", 0, 0, tiled=True, axis_index_groups=groups)


def gather_group(block):
    nz = lax.axis_size("expert")
    stack = jnp.stack([block] + [from_plane(block, s) for s in range(1, nz)])
    stack = jnp.stack([stack, swap_chip(stack)])
    return jnp.stack([stack, swap_core(stack)])


def reduce_group(parts):
    nz = lax.axis_size("expert")
    half = parts[0] + swap_core(parts[1].astype(BF16)).astype(F32)
    half = half[0] + swap_chip(half[1].astype(BF16)).astype(F32)
    total = half[0]
    for step in range(1, nz):
        total = total + to_plane(half[step].astype(BF16), step).astype(F32)
    return total


def two_parts(value):
    high = value.astype(BF16)
    return high, (value - high.astype(F32)).astype(BF16)


def local(
    tokens,
    timestep,
    labels,
    routes,
    expert_gates,
    grad_out,
    ada_weight,
    ada_bias,
    qkv_weight,
    proj_weight,
    shared_up,
    shared_down,
    expert_up,
    expert_down,
    time_table,
    class_table,
):
    rows, feat = tokens.shape
    ndp, nz = lax.axis_size("dp"), lax.axis_size("expert")
    reps = ndp // TP
    ndev = ndp * nz
    members = TP * nz
    local_experts = expert_up.shape[0]
    wide = expert_up.shape[2]
    down_cols = expert_down.shape[2]
    shared_wide = shared_up.shape[1]
    shared_cols = shared_down.shape[1]
    qkv_cols = qkv_weight.shape[1]
    proj_cols = proj_weight.shape[1]
    table_cols = time_table.shape[1]
    plane = lax.axis_index("expert")
    scale = math.sqrt(HD)

    def exchange(value):
        return lax.all_to_all(value, AXES, 0, 0, tiled=True)

    ids = jnp.concatenate([timestep, labels])[None]
    all_ids = exchange(jnp.broadcast_to(ids, (ndev, 2)))
    pick_time = all_ids[:, :1] == jnp.arange(time_table.shape[0], dtype=jnp.int32)[None]
    pick_class = all_ids[:, 1:] == jnp.arange(class_table.shape[0], dtype=jnp.int32)[None]
    cond_cols = dot_nn(pick_time.astype(BF16), time_table) + dot_nn(
        pick_class.astype(BF16), class_table
    )
    cond_all = exchange(jnp.broadcast_to(cond_cols[None], (ndev, ndev, table_cols)))
    cond_all = cond_all.transpose(1, 0, 2).reshape(ndev, feat)
    silu_all = jax.nn.silu(cond_all).astype(BF16)
    my_index = lax.axis_index(AXES)
    cond_own = lax.dynamic_slice_in_dim(cond_all, my_index, 1, 0)
    mod_cols = dot_nn(silu_all, ada_weight) + ada_bias.astype(F32)[None]
    mod = exchange(mod_cols).reshape(6, feat)
    shift_one, scale_one, gate_one = mod[0:1], mod[1:2], mod[2:3]
    shift_two, scale_two, gate_two = mod[3:4], mod[4:5], mod[5:6]

    small = jnp.concatenate([qkv_weight.T, proj_weight.T])
    small_full = lax.all_gather(small, AXES)
    qkv_t = small_full[:, :qkv_cols].reshape(ndev * qkv_cols, feat)
    proj_t = small_full[:, qkv_cols:].reshape(ndev * proj_cols, feat)

    ups = jnp.concatenate(
        [expert_up.transpose(0, 2, 1).reshape(local_experts * wide, feat), shared_up.T]
    )
    ups = gather_rows(ups)
    up_t = (
        ups[:, : local_experts * wide]
        .reshape(reps, local_experts, wide, feat)
        .transpose(1, 0, 2, 3)
        .reshape(local_experts, reps * wide, feat)
    )
    sup_t = ups[:, local_experts * wide :].reshape(reps * shared_wide, feat)
    downs = (
        expert_down.transpose(0, 2, 1)
        .reshape(local_experts, down_cols, reps, TP, wide)
        .transpose(3, 0, 1, 2, 4)
        .reshape(TP, local_experts * down_cols, reps * wide)
    )
    downs = gather_rows(exchange_tp(downs))
    down_t = (
        downs.reshape(ndp, local_experts, down_cols, reps * wide)
        .transpose(1, 0, 2, 3)
        .reshape(local_experts, feat, reps * wide)
    )
    sdowns = (
        shared_down.T.reshape(shared_cols, reps, TP, nz, shared_wide)
        .transpose(2, 3, 0, 1, 4)
        .reshape(TP, nz, shared_cols, reps * shared_wide)
    )
    sdowns = exchange_tp(sdowns)
    sdowns = lax.all_to_all(sdowns, "expert", 1, 1, tiled=True)
    sdown_t = gather_rows(sdowns).reshape(feat, reps * shared_wide)

    gate_high, gate_low = two_parts(expert_gates)
    meta = jnp.stack([routes[:, 0].astype(BF16), routes[:, 1].astype(BF16), gate_high[:, 0], gate_high[:, 1], gate_low[:, 0], gate_low[:, 1]])
    meta = jnp.pad(meta.reshape(-1, feat), ((0, 8 - meta.size // feat), (0, 0)))
    early = gather_group(jnp.concatenate([grad_out, meta])).reshape(members, rows + 8, feat)
    grads_all = early[:, :rows]
    meta_all = early[:, rows : rows + 6 * rows // feat].reshape(members, 6, rows).astype(F32)
    routes_all = meta_all[:, 0:2].astype(jnp.int32)
    gates_all = meta_all[:, 2:4] + meta_all[:, 4:6]

    resid_in = tokens.astype(F32)
    norm_one, inverse_one = layer_norm(resid_in)
    normed_one = (norm_one * (1.0 + scale_one) + shift_one).astype(BF16)
    qkv_all = dot_nt(normed_one, qkv_t).astype(BF16).reshape(rows, 3, H, HD)
    query, key, value = qkv_all[:, 0], qkv_all[:, 1], qkv_all[:, 2]
    scores = einsum("qhe,khe->hqk", query, key) / scale
    row_max = jnp.max(scores, axis=-1, keepdims=True)
    exp_scores = jnp.exp(scores - row_max)
    probs = exp_scores / jnp.sum(exp_scores, axis=-1, keepdims=True)
    probs_low = probs.astype(BF16)
    attn = einsum("hqk,khe->qhe", probs_low, value).astype(BF16).reshape(rows, feat)
    projected = dot_nt(attn, proj_t)
    middle = resid_in + gate_one * projected
    norm_two, inverse_two = layer_norm(middle)
    normed_two = (norm_two * (1.0 + scale_two) + shift_two).astype(BF16)

    gate_rows = jnp.concatenate(list(two_parts(gate_two)) + [jnp.zeros((6, feat), BF16)])
    late = gather_group(jnp.concatenate([normed_two, gate_rows])).reshape(members, rows + 8, feat)
    hidden_all = late[:, :rows]
    gate_two_all = late[:, rows : rows + 1].astype(F32) + late[:, rows + 1 : rows + 2].astype(F32)
    d_moe_all = (gate_two_all * grads_all.astype(F32)).astype(BF16)
    names = plane * local_experts + jnp.arange(local_experts, dtype=jnp.int32)
    named = routes_all[:, None] == names[None, :, None, None]
    has = named[:, :, 0] | named[:, :, 1]
    gate_of = jnp.sum(jnp.where(named, gates_all[:, None], 0.0), axis=2)
    count = jnp.cumsum(has.astype(jnp.int32), axis=2) - 1
    slots = jnp.arange(CAP, dtype=jnp.int32)
    select = (has[:, :, None] & (count[:, :, None] == slots[None, None, :, None])).astype(BF16)
    hid_rows = einsum("best,btd->ebsd", select, hidden_all).astype(BF16)
    hid_rows = hid_rows.reshape(local_experts, members * CAP, feat)
    dm_rows = einsum("best,btd->ebsd", select, d_moe_all).reshape(
        local_experts, members * CAP, feat
    )
    gate_slot = jnp.sum(select.astype(F32) * gate_of[:, :, None], axis=3)
    gate_slot = gate_slot.transpose(1, 0, 2).reshape(local_experts, members * CAP, 1)
    dy_rows = (gate_slot * dm_rows).astype(BF16)
    pre = einsum("erd,efd->erf", hid_rows, up_t)
    act = jax.nn.gelu(pre).astype(BF16)
    res = einsum("erf,edf->erd", act, down_t)
    d_act = einsum("erd,edf->erf", dy_rows, down_t)
    d_pre = local_grad(jax.nn.gelu, pre, d_act).astype(BF16)
    d_rows = einsum("erf,efd->erd", d_pre, up_t).astype(BF16)
    gg_rows = jnp.sum(dm_rows * res, axis=2).reshape(local_experts, members, CAP)
    y_rows = (gate_slot * res).astype(BF16)
    hid_flat = hidden_all.reshape(members * rows, feat)
    dm_flat = d_moe_all.reshape(members * rows, feat)
    pre_s = dot_nt(hid_flat, sup_t)
    act_s = jax.nn.gelu(pre_s).astype(BF16)
    res_s = dot_nt(act_s, sdown_t)
    d_pre_s = local_grad(jax.nn.gelu, pre_s, dot_nn(dm_flat, sdown_t)).astype(BF16)
    d_hid_s = dot_nn(d_pre_s, sup_t)
    shape4 = (local_experts, members, CAP, feat)
    d_hid = einsum("best,ebsd->btd", select, d_rows.reshape(shape4)) + d_hid_s.reshape(
        members, rows, feat
    )
    branch = einsum("best,ebsd->btd", select, y_rows.reshape(shape4)) + res_s.reshape(
        members, rows, feat
    )
    gg_tok = jnp.sum(select.astype(F32) * gg_rows.transpose(1, 0, 2)[..., None], axis=2)
    gg = jnp.sum(jnp.where(named, gg_tok[:, :, None], 0.0), axis=1)
    gg = jnp.pad(gg.reshape(members, 1, 2 * rows), ((0, 0), (0, 7), (0, feat - 2 * rows)))
    group = (2, 2, nz)
    d_normed_two = reduce_group(d_hid.reshape(group + d_hid.shape[1:]))
    branch = jnp.concatenate([branch, gg], axis=1)
    branch = reduce_group(branch.reshape(group + branch.shape[1:]))
    gates_grad = branch[rows, : 2 * rows].reshape(2, rows).T
    branch = branch[:rows]

    g_up = einsum("erf,erd->efd", d_pre, hid_rows)
    g_sup = dot_tn(d_pre_s, hid_flat)
    g_ups = jnp.concatenate(
        [
            g_up.reshape(local_experts, reps, wide, feat)
            .transpose(1, 0, 2, 3)
            .reshape(reps, local_experts * wide, feat),
            g_sup.reshape(reps, shared_wide, feat),
        ],
        axis=1,
    )
    g_ups = reduce_rows(g_ups)
    up_part = g_ups[: local_experts * wide].reshape(local_experts, wide, feat).transpose(0, 2, 1)
    sup_part = g_ups[local_experts * wide :].T
    g_down = einsum("erd,erf->edf", dy_rows, act)
    g_down = (
        g_down.reshape(local_experts, reps, TP, down_cols, reps * wide)
        .transpose(1, 2, 0, 3, 4)
        .reshape(reps, TP, local_experts * down_cols, reps * wide)
    )
    g_down = exchange_tp(reduce_rows(g_down).astype(BF16)).astype(F32)
    down_part = (
        g_down.reshape(TP, local_experts, down_cols, reps, wide)
        .transpose(1, 3, 0, 4, 2)
        .reshape(local_experts, reps * TP * wide, down_cols)
    )
    g_sdown = dot_tn(dm_flat, act_s).reshape(reps, TP, nz, shared_cols, reps * shared_wide)
    g_sdown = exchange_tp(reduce_rows(g_sdown).astype(BF16))
    g_sdown = lax.all_to_all(g_sdown, "expert", 1, 1, tiled=True).astype(F32)
    sdown_part = (
        g_sdown.reshape(TP, nz, shared_cols, reps, shared_wide)
        .transpose(3, 0, 1, 4, 2)
        .reshape(reps * TP * nz * shared_wide, shared_cols)
    )

    block_out = (middle + gate_two * branch).astype(BF16)
    upstream = grad_out.astype(F32)
    d_gate_two = jnp.sum(upstream * branch, axis=0)
    d_shift_two = jnp.sum(d_normed_two, axis=0)
    d_scale_two = jnp.sum(d_normed_two * norm_two, axis=0)
    d_middle = upstream + norm_back(d_normed_two * (1.0 + scale_two), norm_two, inverse_two)
    d_gate_one = jnp.sum(d_middle * projected, axis=0)
    d_projected = (gate_one * d_middle).astype(BF16)
    g_proj = dot_tn(d_projected, attn)
    d_attn = dot_nn(d_projected, proj_t).astype(BF16).reshape(rows, H, HD)
    d_value = einsum("hqk,qhe->khe", probs_low, d_attn)
    d_probs = einsum("qhe,khe->hqk", d_attn, value)
    row_delta = jnp.sum(probs * d_probs, axis=-1, keepdims=True)
    d_scores = (probs * (d_probs - row_delta)).astype(BF16)
    d_query = einsum("hqk,khe->qhe", d_scores, key) / scale
    d_key = einsum("hqk,qhe->khe", d_scores, query) / scale
    d_qkv = jnp.stack([d_query, d_key, d_value], axis=1).astype(BF16).reshape(rows, 3 * feat)
    g_qkv = dot_tn(d_qkv, normed_one)
    d_normed_one = dot_nn(d_qkv, qkv_t)
    d_shift_one = jnp.sum(d_normed_one, axis=0)
    d_scale_one = jnp.sum(d_normed_one * norm_one, axis=0)
    tokens_grad = d_middle + norm_back(d_normed_one * (1.0 + scale_one), norm_one, inverse_one)

    d_mod = jnp.stack([d_shift_one, d_scale_one, d_gate_one, d_shift_two, d_scale_two, d_gate_two])
    d_mod = exchange(d_mod.astype(BF16).reshape(ndev, -1))
    ada_part = dot_tn(silu_all, d_mod)
    bias_part = jnp.sum(d_mod.astype(F32), axis=0)
    d_cond = dot_nt(d_mod, ada_weight)
    d_cond_own = jnp.sum(exchange(d_cond), axis=0, keepdims=True)
    cond_grad = local_grad(jax.nn.silu, cond_own, d_cond_own)
    d_cond_cols = exchange(d_cond.reshape(ndev, ndev, table_cols).transpose(1, 0, 2))
    d_cond_cols = local_grad(jax.nn.silu, cond_cols, jnp.sum(d_cond_cols, axis=0))

    def table_grad(pick):
        return lax.dot_general(
            pick.astype(F32),
            d_cond_cols,
            (((0,), (0,)), ((), ())),
            precision=lax.Precision.HIGHEST,
            preferred_element_type=F32,
        )

    time_part, class_part = table_grad(pick_time), table_grad(pick_class)

    g_small = jnp.concatenate(
        [g_qkv.reshape(ndev, qkv_cols, feat), g_proj.reshape(ndev, proj_cols, feat)], axis=1
    ).astype(BF16)
    g_small = lax.psum_scatter(g_small, AXES).astype(F32)
    qkv_part = g_small[:qkv_cols].T
    proj_part = g_small[qkv_cols:].T
    return (
        block_out,
        tokens_grad,
        cond_grad,
        gates_grad,
        ada_part,
        bias_part,
        qkv_part,
        proj_part,
        sup_part,
        sdown_part,
        up_part,
        down_part,
        time_part,
        class_part,
    )


def solution(mesh):
    both = ("dp", "expert")
    by_rows, by_cols, by_first = P(both, None), P(None, both), P(both)
    by_expert = P("expert", None, "dp")
    return jax.shard_map(
        local,
        mesh=mesh,
        in_specs=(
            by_rows,
            by_first,
            by_first,
            by_rows,
            by_rows,
            by_rows,
            by_cols,
            by_first,
            by_cols,
            by_cols,
            by_cols,
            by_cols,
            by_expert,
            by_expert,
            by_cols,
            by_cols,
        ),
        out_specs=(
            by_rows,
            by_rows,
            by_rows,
            by_rows,
            by_cols,
            by_first,
            by_cols,
            by_cols,
            by_cols,
            by_cols,
            by_expert,
            by_expert,
            by_cols,
            by_cols,
        ),
        check_vma=False,
    )
```

```python
import functools
import math

import jax
import jax.numpy as jnp
from jax import lax
from jax.experimental import pallas as pl
from jax.experimental.pallas import tpu as pltpu
from jax.sharding import PartitionSpec as P

H = 12
HD = 64
SEQ = 256
CAP = 128
TP = 2
AXES = ("dp", "expert")
F32 = jnp.float32
BF16 = jnp.bfloat16

HEAD = 16
BLOCKS = 4
GELU_A = math.sqrt(2.0 / math.pi)
GELU_B = 0.044715


def gelu_both(x):
    square = x * x
    t = jnp.tanh(GELU_A * x * (1.0 + GELU_B * square))
    half = 0.5 * (1.0 + t)
    slope = half + 0.5 * x * (1.0 - t * t) * (GELU_A + 3.0 * GELU_A * GELU_B * square)
    return x * half, slope


def mix_kernel(count, more, first_ref, h_own, h_core, g_own, g_core, sup_ref, sdown_ref, *refs):
    ups, downs, refs = refs[:count], refs[count : 2 * count], refs[2 * count :]
    before, refs = refs[:3] if more else None, refs[3:] if more else refs
    keep, send, grads, gsup_out, gsdown_out = refs[:5]
    rows_out, act_out, dpre_out, dy_out, hid_out, ds_out, meta, acc_y, acc_d, gg_acc, up_ref, down_ref = refs[5:]
    e = pl.program_id(0)
    seq, feat = SEQ, h_own.shape[2]
    step = 256

    @pl.when(e == 0)
    def _():
        hs = [h_own.at[0], h_own.at[1], h_core.at[0], h_core.at[1]]
        gs = [g_own.at[0], g_own.at[1], g_core.at[0], g_core.at[1]]
        for b in range(BLOCKS):
            hid_out[b] = hs[b][0:seq, :]
            tail = hs[b][seq : seq + HEAD, :].astype(F32)
            gate_two = tail[0:1] + tail[1:2]
            ds_out[b] = (gate_two * gs[b][0:seq, :].astype(F32)).astype(BF16)
            meta[b] = gs[b][seq : seq + HEAD, :].astype(F32)
        gg_acc[...] = jnp.zeros_like(gg_acc)
        acc_y[...] = jnp.zeros_like(acc_y)
        acc_d[...] = jnp.zeros_like(acc_d)

    if count == 1:
        part = ups[0].shape[2]
        for i in range(ups[0].shape[0]):
            up_ref[:, i * part : (i + 1) * part] = ups[0][i]
        down_ref[...] = downs[0][:, :, 0].reshape(down_ref.shape)
    else:
        part, per = ups[0].shape[1], feat // count
        for i in range(count):
            place = first_ref[1] ^ i
            up_ref[:, pl.ds(pl.multiple_of(place * part, 128), part)] = ups[i][...]
            down_ref[pl.ds(pl.multiple_of(place * per, 16), per), :] = downs[i][:, 0].reshape(per, -1)
    name = (first_ref[0] + e).astype(F32)
    up_down = (lax.broadcasted_iota(jnp.int32, (seq, seq), 0) <= lax.broadcasted_iota(jnp.int32, (seq, seq), 1))
    ones_tri = up_down.astype(F32).astype(BF16)
    slot = lax.broadcasted_iota(jnp.int32, (CAP, seq), 0).astype(F32)
    selects, gates = [], []
    for b in range(BLOCKS):
        m = meta[b]
        in0 = (m[0:1, 0:seq] == name).astype(F32)
        in1 = (m[0:1, seq : 2 * seq] == name).astype(F32)
        gate = in0 * (m[0:1, 2 * seq : 3 * seq] + m[1:2, seq : 2 * seq]) + in1 * (
            m[1:2, 0:seq] + m[1:2, 2 * seq : 3 * seq]
        )
        has = in0 + in1
        count = dot_nn(jnp.broadcast_to(has, (16, seq)).astype(BF16), ones_tri)[0:1] * has - 1.0
        select = (count == slot).astype(F32)
        gates.append(jnp.sum(select * gate, axis=1, keepdims=True))
        select = select.astype(BF16)
        selects.append(select)
        at = pl.ds(b * CAP, CAP)
        rows_out[at, :] = dot_nn(select, hid_out[b]).astype(BF16)
        dy_out[at, :] = (gates[b] * dot_nn(select, ds_out[b])).astype(BF16)

    rows = rows_out[...]
    dy = dy_out[...]
    wide = down_ref.shape[1]
    for c in range(0, wide, step):
        at = pl.ds(c, step)
        act, slope = gelu_both(dot_nn(rows, up_ref[:, at]))
        act_out[:, at] = act.astype(BF16)
        dpre_out[:, at] = (slope * dot_nn(dy, down_ref[:, at])).astype(BF16)
    act = act_out[...]
    dpre = dpre_out[...]
    gg = [jnp.zeros((CAP, 1), F32)] * BLOCKS
    for c in range(0, feat, step):
        at = pl.ds(c, step)
        res = dot_nt(act, down_ref[at, :])
        dx = dot_nt(dpre, up_ref[at, :]).astype(BF16)
        for b in range(BLOCKS):
            part = res[b * CAP : (b + 1) * CAP]
            spread = dot_nn(selects[b], ds_out[b, :, at])
            gg[b] = gg[b] + jnp.sum(part * spread, axis=1, keepdims=True)
            acc_y[b, :, at] += dot_tn(selects[b], (gates[b] * part).astype(BF16))
            acc_d[b, :, at] += dot_tn(selects[b], dx[b * CAP : (b + 1) * CAP])
    for b in range(BLOCKS):
        m = meta[b]
        token = jnp.sum(selects[b].astype(F32) * gg[b], axis=0, keepdims=True)
        in0 = (m[0:1, 0:seq] == name).astype(F32)
        in1 = (m[0:1, seq : 2 * seq] == name).astype(F32)
        gg_acc[b, 0:1, 0:seq] += in0 * token
        gg_acc[b, 0:1, seq : 2 * seq] += in1 * token

    blocks, part = grads.shape[0], grads.shape[4]
    per = feat // blocks

    def put(i, kind, start, value):
        at = pl.ds(start, value.shape[0])
        if more:
            value = value + before[0][i, kind, 0, at, :].astype(F32)
        grads[i, kind, 0, at, :] = value.astype(BF16)

    for c in range(0, feat, step):
        total = dot_tn(rows_out[:, c : c + step], dpre)
        for i in range(blocks):
            put(i, 0, c, total[:, i * part : (i + 1) * part])
    chunk = 2 * per if blocks > 1 else step
    for c in range(0, feat, chunk):
        total = dot_tn(dy_out[:, c : c + chunk], act)
        if blocks == 1:
            put(0, 1, c, total)
            continue
        for i in range(2):
            for q in range(blocks):
                value = total[i * per : (i + 1) * per, q * part : (q + 1) * part]
                put(c // per + i, 1, q * per, value)

    half = BLOCKS // 2
    hid = hid_out[pl.ds(e * half, half)].reshape(half * seq, feat)
    ds = ds_out[pl.ds(e * half, half)].reshape(half * seq, feat)
    act, slope = gelu_both(dot_nt(hid, sup_ref[...]))
    act = act.astype(BF16)
    dpre = (slope * dot_nn(ds, sdown_ref[...])).astype(BF16)

    @pl.when(e == 0)
    def _():
        gsup_out[...] = before[1][...] if more else jnp.zeros_like(gsup_out)
        gsdown_out[...] = before[2][...] if more else jnp.zeros_like(gsdown_out)

    gsup_out[...] += dot_tn(dpre, hid)
    gsdown_out[...] += dot_tn(ds, act)
    for c in range(0, feat, step):
        at = pl.ds(c, step)
        acc_y[pl.ds(e * half, half), :, at] += dot_nt(act, sdown_ref[at, :]).reshape(half, seq, step)
        acc_d[pl.ds(e * half, half), :, at] += dot_nn(dpre, sup_ref[:, at]).reshape(half, seq, step)

    @pl.when(e == pl.num_programs(0) - 1)
    def _():
        for b in range(BLOCKS):
            out = keep if b < half else send
            out[b % half, 0:seq, :] = acc_d[b].astype(BF16)
            out[b % half, seq : 2 * seq, :] = acc_y[b].astype(BF16)
            out[b % half, 2 * seq : 2 * seq + HEAD, :] = gg_acc[b].astype(BF16)


def mix(first, hid, grads, ups, downs, sup, sdown, *before):
    rows, feat = hid[0].shape[1] - HEAD, hid[0].shape[2]
    experts, wide = downs[0].shape[-3], downs[0].shape[-1]
    half, count = BLOCKS // 2, BLOCKS * CAP
    whole = lambda *shape: pl.BlockSpec(shape, lambda e: (0,) * len(shape))
    once = lambda *shape: pl.BlockSpec(
        shape, lambda e: (0,) * len(shape), pipeline_mode=pl.Buffered(1)
    )
    swide = sup.shape[0]
    full = rows + HEAD
    sds = jax.ShapeDtypeStruct
    blocks, part = ups[0].shape[0] if len(ups) == 1 else len(ups), ups[0].shape[-1]
    by_expert = lambda e: (0, 0, e, 0, 0)
    part_shape = (blocks, 2, 1, feat, part)
    outs = [pl.BlockSpec(part_shape, by_expert), whole(swide, feat), whole(feat, swide)]
    earlier = [
        pl.BlockSpec(part_shape, by_expert, pipeline_mode=pl.Buffered(1)),
        once(swide, feat),
        once(feat, swide),
    ]
    return pl.pallas_call(
        functools.partial(mix_kernel, len(ups), bool(before)),
        grid=(experts,),
        in_specs=[SMEM_SPEC]
        + [once(half, full, feat)] * 4
        + [
            once(swide, feat),
            once(feat, swide),
        ]
        + [
            pl.BlockSpec((feat, part), lambda e: (e, 0))
            if len(ups) > 1
            else pl.BlockSpec((blocks, feat, part), lambda e: (0, e, 0))
            for up in ups
        ]
        + [
            pl.BlockSpec(
                down.shape[:-3] + (1,) + down.shape[-2:],
                lambda e, n=len(down.shape) - 3: (0,) * n + (e, 0, 0),
                pipeline_mode=pl.Buffered(1),
            )
            for down in downs
        ]
        + (earlier if before else []),
        out_specs=[whole(half, rows + full, feat), whole(half, rows + full, feat)] + outs,
        out_shape=[
            sds((half, rows + full, feat), BF16),
            sds((half, rows + full, feat), BF16),
            sds((blocks, 2, experts, feat, part), BF16),
            sds((swide, feat), F32),
            sds((feat, swide), F32),
        ],
        scratch_shapes=[
            pltpu.VMEM((count, feat), BF16),
            pltpu.VMEM((count, wide), BF16),
            pltpu.VMEM((count, wide), BF16),
            pltpu.VMEM((count, feat), BF16),
            pltpu.VMEM((BLOCKS, rows, feat), BF16),
            pltpu.VMEM((BLOCKS, rows, feat), BF16),
            pltpu.VMEM((BLOCKS, HEAD, feat), F32),
            pltpu.VMEM((BLOCKS, rows, feat), F32),
            pltpu.VMEM((BLOCKS, rows, feat), F32),
            pltpu.VMEM((BLOCKS, HEAD, feat), F32),
            pltpu.VMEM((feat, wide), BF16),
            pltpu.VMEM((feat, wide), BF16),
        ],
        compiler_params=pltpu.CompilerParams(vmem_limit_bytes=58 * 2**20),
        cost_estimate=CHEAP,
    )(first, *hid, *grads, sup, sdown, *ups, *downs, *before)


def norm_back(upstream, normed, inverse):
    mean_grad = jnp.mean(upstream, axis=-1, keepdims=True)
    mean_mix = jnp.mean(upstream * normed, axis=-1, keepdims=True)
    return inverse * (upstream - mean_grad - normed * mean_mix)


def dot_nn(left, right):
    return jnp.dot(left, right, preferred_element_type=F32)


def dot_tn(left, right):
    return lax.dot_general(left, right, (((0,), (0,)), ((), ())), preferred_element_type=F32)


def dot_nt(left, right):
    return lax.dot_general(left, right, (((1,), (1,)), ((), ())), preferred_element_type=F32)


def local_grad(function, inputs, upstream):
    unused, pull = jax.vjp(function, inputs)
    return pull(upstream)[0]


def row_norm(values):
    center = values - jnp.mean(values, axis=-1, keepdims=True)
    inverse = lax.rsqrt(jnp.mean(center * center, axis=-1, keepdims=True) + 1e-06)
    return center * inverse, inverse


def load_weights(where_ref, pieces, spots, wq, wp, sem):
    copies = []
    for ref, blocks, lane in spots:
        piece = pieces[ref]
        rq = wq.shape[0] // where_ref.shape[0]
        rp = wp.shape[0] // where_ref.shape[0]
        width = piece.shape[2]
        for j, block in enumerate(blocks):
            at = where_ref[block]
            lanes = pl.ds(lane, width)
            to_q = wq.at[pl.ds(pl.multiple_of(at * rq, 16), rq), lanes]
            to_p = wp.at[pl.ds(pl.multiple_of(at * rp, 16), rp), lanes]
            copies.append(pltpu.make_async_copy(piece.at[j, pl.ds(0, rq), :], to_q, sem))
            copies.append(pltpu.make_async_copy(piece.at[j, pl.ds(rq, rp), :], to_p, sem))
    for copy in copies:
        copy.start()
    return copies


def pair_masks():
    lane = lax.broadcasted_iota(jnp.int32, (1, 2 * HD), 1)
    return [(lane < HD).astype(F32).astype(BF16), (lane >= HD).astype(F32).astype(BF16)]


def head_probs(query, key, mask):
    scores = dot_nt(query * mask, key) * (1.0 / math.sqrt(HD))
    exp_scores = jnp.exp(scores - jnp.max(scores, axis=-1, keepdims=True))
    return exp_scores / jnp.sum(exp_scores, axis=-1, keepdims=True)


def attend_kernel(spots, where_ref, tok_ref, mod_ref, *refs):
    count = len({spot[0] for spot in spots})
    pieces = refs[:count]
    late_ref, x1_ref, projected_ref, h1_ref, qkv_ref, attn_ref, wq, wp, sem = refs[count:]
    copies = load_weights(where_ref, pieces, spots, wq, wp, sem)
    rows, feat = tok_ref.shape
    tokens = tok_ref[...].astype(F32)
    norm, unused = row_norm(tokens)
    h1_ref[...] = (norm * (1.0 + mod_ref[1:2, :]) + mod_ref[0:1, :]).astype(BF16)
    for copy in copies:
        copy.wait()
    h1 = h1_ref[...]
    for c in range(0, 3 * feat, 256):
        at = pl.ds(c, 256)
        qkv_ref[:, at] = dot_nt(h1, wq[at, :]).astype(BF16)
    low, high = pair_masks()
    for c in range(0, feat, 2 * HD):
        at = pl.ds(c, 2 * HD)
        query, key = qkv_ref[:, at], qkv_ref[:, pl.ds(feat + c, 2 * HD)]
        value = qkv_ref[:, pl.ds(2 * feat + c, 2 * HD)]
        first = head_probs(query, key, low).astype(BF16)
        second = head_probs(query, key, high).astype(BF16)
        attn_ref[:, at] = (dot_nn(first, value * low) + dot_nn(second, value * high)).astype(BF16)
    attn = attn_ref[...]
    for c in range(0, feat, 256):
        at = pl.ds(c, 256)
        projected_ref[:, at] = dot_nt(attn, wp[at, :])
    x1 = tokens + mod_ref[2:3, :] * projected_ref[...]
    x1_ref[...] = x1
    norm, unused = row_norm(x1)
    late_ref[0:rows, :] = (norm * (1.0 + mod_ref[4:5, :]) + mod_ref[3:4, :]).astype(BF16)
    gate = mod_ref[5:6, :]
    gate_high = gate.astype(BF16).astype(F32)
    line = lax.broadcasted_iota(jnp.int32, (HEAD, feat), 0)
    late_ref[rows : rows + HEAD, :] = jnp.where(
        line == 0, gate_high, jnp.where(line == 1, gate - gate_high, 0.0)
    ).astype(BF16)


VMEM_SPEC = pl.BlockSpec(memory_space=pltpu.VMEM)
SMEM_SPEC = pl.BlockSpec(memory_space=pltpu.SMEM)
HBM_SPEC = pl.BlockSpec(memory_space=pl.ANY)
CHEAP = pl.CostEstimate(flops=10**6, bytes_accessed=10**5, transcendentals=0)


def attend(tokens, mod, where, pieces, spots):
    rows, feat = tokens.shape
    sds = jax.ShapeDtypeStruct
    return pl.pallas_call(
        functools.partial(attend_kernel, spots),
        in_specs=[SMEM_SPEC, VMEM_SPEC, VMEM_SPEC] + [HBM_SPEC] * len(pieces),
        out_specs=[VMEM_SPEC] * 6,
        out_shape=[
            sds((rows + HEAD, feat), BF16),
            sds((rows, feat), F32),
            sds((rows, feat), F32),
            sds((rows, feat), BF16),
            sds((rows, 3 * feat), BF16),
            sds((rows, feat), BF16),
        ],
        scratch_shapes=[
            pltpu.VMEM((3 * feat, feat), BF16),
            pltpu.VMEM((feat, feat), BF16),
            pltpu.SemaphoreType.DMA,
        ],
        compiler_params=pltpu.CompilerParams(vmem_limit_bytes=40 * 2**20),
        cost_estimate=CHEAP,
    )(where, tokens, mod, *pieces)


def back_kernel(spots, blocks, where_ref, dh2_ref, grad_ref, tok_ref, mod_ref, x1_ref, projected_ref, h1_ref, qkv_ref, attn_ref, *refs):
    count = len({spot[0] for spot in spots})
    pieces = refs[:count]
    outs = refs[count:]
    tokens_out, sums_out = outs[0], outs[1]
    wq, wp, dqkv, dattn, sem = outs[-5:]
    grads = outs[2:-5]
    copies = load_weights(where_ref, pieces, spots, wq, wp, sem)
    rows, feat = tok_ref.shape
    norm_two, inverse_two = row_norm(x1_ref[...])
    dh2 = dh2_ref[...]
    d_x1 = grad_ref[...].astype(F32) + norm_back(dh2 * (1.0 + mod_ref[4:5, :]), norm_two, inverse_two)
    sums_out[3:4, :] = jnp.sum(dh2, axis=0, keepdims=True)
    sums_out[4:5, :] = jnp.sum(dh2 * norm_two, axis=0, keepdims=True)
    sums_out[2:3, :] = jnp.sum(d_x1 * projected_ref[...], axis=0, keepdims=True)
    sums_out[5:8, :] = jnp.zeros((3, feat), F32)
    dp = (mod_ref[2:3, :] * d_x1).astype(BF16)
    for copy in copies:
        copy.wait()

    def put(kind, start, size, value):
        if len(grads) == 2:
            grads[kind][start : start + size, :] = value.astype(BF16)
            return
        per = (3 * feat if kind == 0 else feat) // blocks
        base = 0 if kind == 0 else 3 * feat // blocks
        done = 0
        while done < size:
            block, inside = (start + done) // per, (start + done) % per
            take = min(size - done, per - inside)
            grads[0][block, base + inside : base + inside + take, :] = value[done : done + take].astype(BF16)
            done += take

    attn = attn_ref[...]
    for c in range(0, feat, 256):
        dattn[:, c : c + 256] = dot_nn(dp, wp[:, c : c + 256]).astype(BF16)
        put(1, c, 256, dot_tn(dp[:, c : c + 256], attn))
    low, high = pair_masks()
    scale = 1.0 / math.sqrt(HD)
    for c in range(0, feat, 2 * HD):
        at, at_key, at_value = pl.ds(c, 2 * HD), pl.ds(feat + c, 2 * HD), pl.ds(2 * feat + c, 2 * HD)
        query, key, value, d_out = qkv_ref[:, at], qkv_ref[:, at_key], qkv_ref[:, at_value], dattn[:, at]
        d_query, d_key, d_value = 0.0, 0.0, 0.0
        for mask in (low, high):
            probs = head_probs(query, key, mask)
            d_part = d_out * mask
            d_value = d_value + dot_tn(probs.astype(BF16), d_part)
            d_probs = dot_nt(d_part, value)
            delta = jnp.sum(probs * d_probs, axis=-1, keepdims=True)
            d_scores = (probs * (d_probs - delta)).astype(BF16)
            d_query = d_query + dot_nn(d_scores, key * mask)
            d_key = d_key + dot_tn(d_scores, query * mask)
        dqkv[:, at] = (d_query * scale).astype(BF16)
        dqkv[:, at_key] = (d_key * scale).astype(BF16)
        dqkv[:, at_value] = d_value.astype(BF16)
    h1 = h1_ref[...]
    d_all = dqkv[...]
    parts = []
    for c in range(0, feat, 256):
        parts.append(dot_nn(d_all, wq[:, c : c + 256]))
    d_h1 = jnp.concatenate(parts, axis=1)
    norm_one, inverse_one = row_norm(tok_ref[...].astype(F32))
    sums_out[0:1, :] = jnp.sum(d_h1, axis=0, keepdims=True)
    sums_out[1:2, :] = jnp.sum(d_h1 * norm_one, axis=0, keepdims=True)
    tokens_out[...] = d_x1 + norm_back(d_h1 * (1.0 + mod_ref[1:2, :]), norm_one, inverse_one)
    for c in range(0, 3 * feat, 256):
        put(0, c, 256, dot_tn(dqkv[:, c : c + 256], h1))


def attend_back(d_hid, grad_out, tokens, mod, saved, where, pieces, spots, blocks):
    rows, feat = tokens.shape
    sds = jax.ShapeDtypeStruct
    if blocks:
        shapes = [sds((blocks, 4 * feat // blocks, feat), BF16)]
    else:
        shapes = [sds((3 * feat, feat), BF16), sds((feat, feat), BF16)]
    return pl.pallas_call(
        functools.partial(back_kernel, spots, blocks),
        in_specs=[SMEM_SPEC] + [VMEM_SPEC] * (4 + len(saved)) + [HBM_SPEC] * len(pieces),
        out_specs=[VMEM_SPEC] * (2 + len(shapes)),
        out_shape=[sds((rows, feat), F32), sds((8, feat), F32)] + shapes,
        scratch_shapes=[
            pltpu.VMEM((3 * feat, feat), BF16),
            pltpu.VMEM((feat, feat), BF16),
            pltpu.VMEM((rows, 3 * feat), BF16),
            pltpu.VMEM((rows, feat), BF16),
            pltpu.SemaphoreType.DMA,
        ],
        compiler_params=pltpu.CompilerParams(vmem_limit_bytes=48 * 2**20),
        cost_estimate=CHEAP,
    )(where, d_hid, grad_out, tokens, mod, *saved, *pieces)


def swap(value, move):
    ndp, nz = lax.axis_size("dp"), lax.axis_size("expert")
    pairs = []
    for a in range(ndp):
        for b in range(nz):
            c, d = move(a, b)
            pairs.append((a * nz + b, c * nz + d))
    return lax.ppermute(value, AXES, pairs)


def swap_row(value):
    return swap(value, lambda a, b: (a ^ 4, b))


def swap_core(value):
    return swap(value, lambda a, b: (a ^ 1, b))


def swap_chip(value):
    return swap(value, lambda a, b: (a ^ 2, b))


def from_plane(value, step):
    nz = lax.axis_size("expert")
    return swap(value, lambda a, b: (a, (b - step) % nz))


def to_plane(value, step):
    nz = lax.axis_size("expert")
    return swap(value, lambda a, b: (a, (b + step) % nz))


def row_bits():
    return (lax.axis_size("dp") // TP).bit_length() - 1


def row_groups():
    ndp = lax.axis_size("dp")
    return [list(range(i, ndp, TP)) for i in range(TP)]


def gather_rows(value):
    return lax.all_gather(value, "dp", axis_index_groups=row_groups())


def reduce_rows(value):
    flat = value.astype(BF16).reshape(-1, value.shape[-1])
    flat = lax.psum_scatter(flat, "dp", tiled=True, axis_index_groups=row_groups())
    return flat.reshape(value.shape[1:])


def tie(*values):
    return lax.optimization_barrier(values)


def plane_steps():
    nz = lax.axis_size("expert")
    return sorted(range(1, nz), key=lambda step: (min(step, nz - step), step))


def gather_planes(block):
    return [block] + [from_plane(block, step) for step in plane_steps()]


def run_mixture(planes, early, weights, first):
    steps = plane_steps()
    rows = SEQ
    near = jnp.stack(planes[:2])
    near_core = swap_core(near)
    far = jnp.stack(planes[2:])
    far, near_core = tie(far, near_core)
    far_core = swap_core(far)
    keep, send, *saved = mix(first, (near, near_core), early[0], *weights)
    far_core, keep = tie(far_core, keep)
    near = keep.astype(F32) + swap_core(send).astype(F32)
    near_sent, far = tie(near[1].astype(BF16), far)
    near_moved = to_plane(near_sent, steps[0])
    keep, send, *grads = mix(first, (far, far_core), early[1], *weights, *saved)
    near_moved, keep, send, *grads = tie(near_moved, keep, send, *grads)
    far = keep.astype(F32) + swap_core(send).astype(F32)
    moved = [to_plane(far[i, :rows].astype(BF16), step) for i, step in enumerate(steps[1:])]
    y_moved = [to_plane(far[i, rows:].astype(BF16), step) for i, step in enumerate(steps[1:])]
    d_hid = near[0][:rows] + near_moved[:rows].astype(F32)
    for m in moved:
        d_hid = d_hid + m.astype(F32)
    branch = near[0][rows:] + near_moved[rows:].astype(F32)
    return d_hid, branch, y_moved, grads


def fold_bit(part, axis, bit):
    at = (lax.axis_index("dp") >> bit) & 1
    send = lax.dynamic_index_in_dim(part, 1 - at, axis, False).astype(BF16)
    keep = lax.dynamic_index_in_dim(part, at, axis, False)
    return keep, swap(send, lambda a, b: (a ^ (1 << bit), b))


def add(pair):
    return pair[0].astype(F32) + pair[1].astype(F32)


def scatter_planes(part, split):
    nz = lax.axis_size("expert")
    z = lax.axis_index("expert")
    cut_q = split * nz
    cut_p = (part.shape[0] - cut_q) // nz

    def rows_of(plane):
        return jnp.concatenate(
            [
                lax.dynamic_slice_in_dim(part, plane * split, split, 0),
                lax.dynamic_slice_in_dim(part, cut_q + plane * cut_p, cut_p, 0),
            ]
        )

    total = rows_of(z)
    for step in range(1, nz):
        total = total + to_plane(rows_of((z + step) % nz).astype(BF16), step).astype(F32)
    return total


def two_parts(value):
    high = value.astype(BF16)
    return high, (value - high.astype(F32)).astype(BF16)


def local(
    tokens,
    timestep,
    labels,
    routes,
    expert_gates,
    grad_out,
    ada_weight,
    ada_bias,
    qkv_weight,
    proj_weight,
    shared_up,
    shared_down,
    expert_up,
    expert_down,
    time_table,
    class_table,
):
    rows, feat = tokens.shape
    ndp, nz = lax.axis_size("dp"), lax.axis_size("expert")
    reps = ndp // TP
    ndev = ndp * nz
    members = TP * nz
    local_experts = expert_up.shape[0]
    wide = expert_up.shape[2]
    down_cols = expert_down.shape[2]
    shared_wide = shared_up.shape[1]
    shared_cols = shared_down.shape[1]
    qkv_cols = qkv_weight.shape[1]
    proj_cols = proj_weight.shape[1]
    table_cols = time_table.shape[1]
    plane = lax.axis_index("expert")

    def exchange(value):
        return lax.all_to_all(value, AXES, 0, 0, tiled=True)

    ups = jnp.concatenate(
        [expert_up.reshape(local_experts * feat, wide), shared_up.T.reshape(-1, wide)]
    )
    flipped = expert_down.transpose(0, 2, 1)
    halves = [
        jnp.concatenate(
            [flipped[:, :, (i * TP + t) * wide : (i * TP + t + 1) * wide] for i in range(reps)],
            axis=2,
        )
        for t in range(TP)
    ]
    core_low = lax.axis_index("dp") % TP == 0
    mine = jnp.where(core_low, halves[0], halves[1])
    moved = swap_core(jnp.where(core_low, halves[1], halves[0]))
    downs = jnp.where(core_low, jnp.stack([mine, moved]), jnp.stack([moved, mine]))
    sdowns = shared_down.T.reshape(shared_cols, reps, TP, nz, shared_wide)
    sdowns = sdowns.transpose(2, 3, 0, 1, 4).reshape(1, members, shared_cols, reps * shared_wide)
    sdowns = jnp.broadcast_to(sdowns, (reps,) + sdowns.shape[1:])
    sdowns = sdowns.reshape(ndev, shared_cols, reps * shared_wide)
    gate_high, gate_low = two_parts(expert_gates)
    meta = jnp.stack(
        [
            routes[:, 0].astype(BF16),
            routes[:, 1].astype(BF16),
            gate_high[:, 0],
            gate_high[:, 1],
            gate_low[:, 0],
            gate_low[:, 1],
        ]
    )
    meta = jnp.pad(meta.reshape(-1, feat), ((0, HEAD - meta.size // feat), (0, 0)))
    early = jnp.concatenate([grad_out, meta])

    early_planes = lax.all_gather(early, "expert")
    order = (plane + jnp.array([0] + plane_steps(), jnp.int32)) % nz
    early_planes = jnp.take(early_planes, order, axis=0, mode="clip")
    early_core = swap_core(early_planes)

    pair = jnp.concatenate([qkv_weight.T, proj_weight.T])
    rq, rp = nz * qkv_cols, nz * proj_cols
    packed = ndp == 8 and rq % 16 == 0 and rp % 16 == 0
    if packed:
        line = jnp.stack([pair] + [from_plane(pair, step) for step in range(1, nz)])
        order = (jnp.arange(nz, dtype=jnp.int32) - plane) % nz
        line = jnp.take(line, order, axis=0, mode="clip")
        line = jnp.concatenate(
            [line[:, :qkv_cols].reshape(rq, feat), line[:, qkv_cols:].reshape(rp, feat)]
        )
        half = feat // 2
        left, right = line[None, :, :half], line[None, :, half:]
        left_x, right_y = swap_chip(left), swap_row(right)
    ids = jnp.concatenate([timestep, labels])[None]
    all_ids = exchange(jnp.broadcast_to(ids, (ndev, 2)))
    pick_time = all_ids[:, :1] == jnp.arange(time_table.shape[0], dtype=jnp.int32)[None]
    pick_class = all_ids[:, 1:] == jnp.arange(class_table.shape[0], dtype=jnp.int32)[None]
    cond_cols = dot_nn(pick_time.astype(BF16), time_table) + dot_nn(
        pick_class.astype(BF16), class_table
    )
    cond_all = exchange(jnp.broadcast_to(cond_cols[None], (ndev, ndev, table_cols)))
    if packed:
        left_x, right_y, cond_all = tie(left_x, right_y, cond_all)
        left_x, right_y = jnp.concatenate([left, left_x]), jnp.concatenate([right, right_y])
        left_y, right_x = swap_row(left_x), swap_chip(right_y)
    cond_all = cond_all.transpose(1, 0, 2).reshape(ndev, feat)
    silu_all = jax.nn.silu(cond_all).astype(BF16)
    my_index = lax.axis_index(AXES)
    cond_own = lax.dynamic_slice_in_dim(cond_all, my_index, 1, 0)
    mod_cols = dot_nn(silu_all, ada_weight) + ada_bias.astype(F32)[None]
    mod = exchange(mod_cols).reshape(6, feat)
    if packed:
        left_y, right_x, mod, ups, downs = tie(left_y, right_x, mod, ups, downs)
        left, right = jnp.concatenate([left_x, left_y]), jnp.concatenate([right_y, right_x])
        pieces = [left, swap_core(left), right, swap_core(right)]
        mine = lax.axis_index("dp")
        moves = [0, 2, 4, 6, 1, 3, 5, 7]
        where = jnp.stack([mine ^ m for m in moves]).astype(jnp.int32)
        spots = (
            (0, (0, 1, 2, 3), 0),
            (1, (4, 5, 6, 7), 0),
            (2, (0, 2, 1, 3), half),
            (3, (4, 6, 5, 7), half),
        )
        blocks = ndp
    else:
        pair = lax.all_gather(pair, AXES)
        pieces = [
            jnp.concatenate(
                [
                    pair[:, :qkv_cols].reshape(ndev * qkv_cols, feat),
                    pair[:, qkv_cols:].reshape(ndev * proj_cols, feat),
                ]
            )[None]
        ]
        where = jnp.zeros((1,), jnp.int32)
        spots = ((0, (0,), 0),)
        blocks = 0

    mod_rows = jnp.concatenate([mod, jnp.zeros((2, feat), F32)])
    late, *saved_attn = attend(tokens, mod_rows, where, pieces, spots)
    middle = saved_attn[0]

    if packed:
        ups = [ups, swap_chip(ups), swap_row(ups)]
        downs = [downs, swap_chip(downs), swap_row(downs)]
        late = gather_planes(late)
        late[1], late[2], late[3], *ups, downs[0], downs[1], downs[2] = tie(*late[1:], *ups, *downs)
        ups.append(swap_chip(ups[2]))
        downs.append(swap_row(downs[1]))
        place = lax.axis_index("dp") // TP
        sups = jnp.stack([up[local_experts * feat :].reshape(shared_wide, feat) for up in ups])
        order = place ^ jnp.arange(reps, dtype=jnp.int32)
        sup_t = jnp.take(sups, order, axis=0, mode="clip").reshape(reps * shared_wide, feat)
    else:
        late = gather_planes(late)
        place = jnp.zeros((), jnp.int32)
        ups, downs = gather_rows(ups), [gather_rows(downs)]
        sup_t = ups[:, local_experts * feat :].reshape(reps * shared_wide, feat)
        if wide % 128:
            ups = ups[:, : local_experts * feat].reshape(reps, local_experts * feat, wide)
            ups = ups.transpose(1, 0, 2).reshape(1, local_experts * feat, reps * wide)
        ups = [ups]
    sdown_t = exchange(sdowns).reshape(feat, reps * shared_wide)

    first = jnp.stack([plane * local_experts, place]).astype(jnp.int32)
    early = ((early_planes[:2], early_core[:2]), (early_planes[2:], early_core[2:]))
    d_normed_two, branch, y_moved, grads = run_mixture(
        late, early, (ups, downs, sup_t, sdown_t), first
    )

    g_mix, g_sup, g_sdown = grads
    if wide % 128:
        g_up = g_mix[0, 0].reshape(local_experts, feat, reps, wide).transpose(2, 0, 1, 3)
        g_down = g_mix[0, 1].reshape(local_experts, reps, TP * down_cols, reps, wide)
        g_down = g_down.transpose(1, 0, 3, 2, 4).reshape(g_up.shape)
        g_mix = jnp.stack([g_up, g_down], axis=1)
    g_mix = reduce_rows(g_mix)
    up_part = g_mix[0].astype(F32)
    g_down = g_mix[1].reshape(local_experts, reps, TP, down_cols, wide)
    kept = jnp.where(core_low, g_down[:, :, 0], g_down[:, :, 1])
    got = swap_core(jnp.where(core_low, g_down[:, :, 1], g_down[:, :, 0]))
    g_down = [jnp.where(core_low, kept, got), jnp.where(core_low, got, kept)]
    g_down = jnp.concatenate([g_down[t][:, i] for i in range(reps) for t in range(TP)], axis=2)
    down_part = g_down.transpose(0, 2, 1).astype(F32)

    g_sdown, d_normed_two = tie(g_sdown.astype(BF16), d_normed_two)
    g_sdown = exchange(g_sdown.reshape(ndev, shared_cols, reps * shared_wide))
    tokens_grad, sums, *g_small = attend_back(
        d_normed_two, grad_out, tokens, mod_rows, saved_attn, where, pieces, spots, blocks
    )
    g_sdown, *y_moved, tokens_grad, sums, g_small[0] = tie(
        g_sdown, *y_moved, tokens_grad, sums, g_small[0]
    )
    for m in y_moved:
        branch = branch + m.astype(F32)
    gates_grad = branch[rows, : 2 * rows].reshape(2, rows).T
    branch = branch[:rows]
    block_out = (middle + mod[5:6] * branch).astype(BF16)
    d_gate_two = jnp.sum(grad_out.astype(F32) * branch, axis=0, keepdims=True)

    d_mod = jnp.concatenate([sums[0:5], d_gate_two])
    d_mod = exchange(d_mod.astype(BF16).reshape(ndev, -1))
    if packed:
        half = feat // 2
        g_small = add(fold_bit(g_small[0].reshape((2, 2, 2) + g_small[0].shape[1:]), 2, 0))
        g_small, d_mod = tie(g_small, d_mod)
        left, right = fold_bit(g_small[..., :half], 1, 1), fold_bit(g_small[..., half:], 0, 2)
    else:
        g_small = jnp.concatenate(
            [g_small[0].reshape(ndev, qkv_cols, feat), g_small[1].reshape(ndev, proj_cols, feat)],
            axis=1,
        )
        g_small = lax.psum_scatter(g_small, AXES).astype(F32)
    d_cond = dot_nt(d_mod, ada_weight)
    d_cond_cols = exchange(d_cond.reshape(ndev, ndev, table_cols).transpose(1, 0, 2))
    if packed:
        left, right, d_cond_cols = tie(add(left), add(right), d_cond_cols)
        left, d_cond = tie(left, d_cond)
        left, right = fold_bit(left, 0, 2), fold_bit(right, 0, 1)
    d_cond_cols = local_grad(jax.nn.silu, cond_cols, jnp.sum(d_cond_cols, axis=0))
    d_cond_own = exchange(d_cond)
    if packed:
        left, right, d_cond_own = tie(add(left), add(right), d_cond_own)
        g_small = scatter_planes(jnp.concatenate([left, right], axis=-1), qkv_cols)
    cond_grad = local_grad(jax.nn.silu, cond_own, jnp.sum(d_cond_own, axis=0, keepdims=True))
    ada_part = dot_tn(silu_all, d_mod)
    bias_part = jnp.sum(d_mod.astype(F32), axis=0)
    g_sup, cond_grad = tie(g_sup, cond_grad)
    g_sup = g_sup.reshape((2,) * row_bits() + (shared_wide, feat))
    for bit in range(row_bits(), 0, -1):
        g_sup = add(fold_bit(g_sup, 0, bit))
    sup_part = g_sup.T
    g_sdown = g_sdown.reshape(reps, members, shared_cols, reps, shared_wide)
    g_sdown = jnp.sum(g_sdown.astype(F32), axis=0)
    sdown_part = g_sdown.transpose(2, 0, 3, 1).reshape(reps * members * shared_wide, shared_cols)

    def table_grad(pick):
        return lax.dot_general(
            pick.astype(F32),
            d_cond_cols,
            (((0,), (0,)), ((), ())),
            precision=lax.Precision.HIGHEST,
            preferred_element_type=F32,
        )

    time_part, class_part = table_grad(pick_time), table_grad(pick_class)

    qkv_part = g_small[:qkv_cols].T
    proj_part = g_small[qkv_cols:].T
    return (
        block_out,
        tokens_grad,
        cond_grad,
        gates_grad,
        ada_part,
        bias_part,
        qkv_part,
        proj_part,
        sup_part,
        sdown_part,
        up_part,
        down_part,
        time_part,
        class_part,
    )


def solution(mesh):
    both = ("dp", "expert")
    by_rows, by_cols, by_first = P(both, None), P(None, both), P(both)
    by_expert = P("expert", None, "dp")
    return jax.shard_map(
        local,
        mesh=mesh,
        in_specs=(
            by_rows,
            by_first,
            by_first,
            by_rows,
            by_rows,
            by_rows,
            by_cols,
            by_first,
            by_cols,
            by_cols,
            by_cols,
            by_cols,
            by_expert,
            by_expert,
            by_cols,
            by_cols,
        ),
        out_specs=(
            by_rows,
            by_rows,
            by_rows,
            by_rows,
            by_cols,
            by_first,
            by_cols,
            by_cols,
            by_cols,
            by_cols,
            by_expert,
            by_expert,
            by_cols,
            by_cols,
        ),
        check_vma=False,
    )
```

```python
import functools
import math

import jax
import jax.numpy as jnp
from jax import lax
from jax.experimental import pallas as pl
from jax.experimental.pallas import tpu as pltpu
from jax.sharding import PartitionSpec as P

H = 12
HD = 64
SEQ = 256
CAP = 128
TP = 2
AXES = ("dp", "expert")
F32 = jnp.float32
BF16 = jnp.bfloat16

HEAD = 16
BLOCKS = 4
GELU_A = math.sqrt(2.0 / math.pi)
GELU_B = 0.044715


def gelu_both(x):
    square = x * x
    t = jnp.tanh(GELU_A * x * (1.0 + GELU_B * square))
    half = 0.5 * (1.0 + t)
    slope = half + 0.5 * x * (1.0 - t * t) * (GELU_A + 3.0 * GELU_A * GELU_B * square)
    return x * half, slope


def mix_kernel(count, shared, more, before, final, first_ref, h_own, h_core, g_own, g_core, *refs):
    refs = list(refs)

    def take(number):
        taken = refs[:number]
        del refs[:number]
        return taken

    ups, downs = take(count), take(count)
    if shared:
        (sdown_ref,) = take(1)
        if count == 1:
            (sup_in,) = take(1)
    if more:
        keep_in, send_in = take(2)
    if before:
        (grads_in,) = take(1)
        if shared:
            gsup_in, gsdown_in = take(2)
    keep_out, send_out, grads = take(3)
    if shared:
        gsup, gsdown = take(2)
    rows_ref, act_ref, dpre_ref, dy_ref, hid_ref, ds_ref, meta, acc_y, acc_d, gg_acc = take(10)
    up_ref, down_ref, sup_ref, old_ref, new_ref, keep, send, sems = refs
    seq, feat = SEQ, h_own.shape[2]
    step = 256
    wide = up_ref.shape[1]
    blocks, part = new_ref.shape[0], new_ref.shape[3]

    copies = []
    if count == 1:
        copies.append(pltpu.make_async_copy(ups[0], up_ref, sems.at[0]))
        copies.append(pltpu.make_async_copy(downs[0], down_ref, sems.at[0]))
        if shared:
            copies.append(pltpu.make_async_copy(sup_in, sup_ref, sems.at[0]))
    else:
        per, swide = feat // count, sup_ref.shape[0] // count
        for i in range(count):
            place = first_ref[1] ^ i
            lanes = pl.ds(pl.multiple_of(place * part, 128), part)
            copies.append(
                pltpu.make_async_copy(ups[i].at[pl.ds(0, feat), :], up_ref.at[:, lanes], sems.at[0])
            )
            at = pl.ds(pl.multiple_of(place * per, 16), per)
            copies.append(pltpu.make_async_copy(downs[i], down_ref.at[at, :], sems.at[0]))
            if shared:
                at = pl.ds(pl.multiple_of(place * swide, 16), swide)
                for j in range(2):
                    copies.append(
                        pltpu.make_async_copy(
                            ups[i].at[pl.ds(feat + j * swide, swide), :],
                            sup_ref.at[at, pl.ds(j * part, part)],
                            sems.at[0],
                        )
                    )
    for copy in copies:
        copy.start()
    if more:
        came_copies = [
            pltpu.make_async_copy(keep_in, keep, sems.at[4]),
            pltpu.make_async_copy(send_in, send, sems.at[4]),
        ]
        for copy in came_copies:
            copy.start()
    if before:
        old = pltpu.make_async_copy(grads_in, old_ref, sems.at[1])
        old.start()

    hs = [h_own.at[0], h_own.at[1], h_core.at[0], h_core.at[1]]
    gs = [g_own.at[0], g_own.at[1], g_core.at[0], g_core.at[1]]
    half = BLOCKS // 2
    for b in range(BLOCKS):
        hid_ref[b] = hs[b][0:seq, :]
        tail = hs[b][seq : seq + HEAD, :].astype(F32)
        gate_two = tail[0:1] + tail[1:2]
        ds_ref[b] = (gate_two * gs[b][0:seq, :].astype(F32)).astype(BF16)
        meta[b] = gs[b][seq : seq + HEAD, :].astype(F32)

    name = first_ref[0].astype(F32)
    up_down = lax.broadcasted_iota(jnp.int32, (seq, seq), 0) <= lax.broadcasted_iota(
        jnp.int32, (seq, seq), 1
    )
    ones_tri = up_down.astype(F32).astype(BF16)
    slot = lax.broadcasted_iota(jnp.int32, (CAP, seq), 0).astype(F32)
    selects, back, gates = [], [], []
    for b in range(BLOCKS):
        m = meta[b]
        in0 = (m[0:1, 0:seq] == name).astype(F32)
        in1 = (m[0:1, seq : 2 * seq] == name).astype(F32)
        gate = in0 * (m[0:1, 2 * seq : 3 * seq] + m[1:2, seq : 2 * seq]) + in1 * (
            m[1:2, 0:seq] + m[1:2, 2 * seq : 3 * seq]
        )
        has = in0 + in1
        count_row = dot_nn(jnp.broadcast_to(has, (16, seq)).astype(BF16), ones_tri)[0:1]
        select = (count_row * has - 1.0 == slot).astype(F32)
        gates.append(jnp.sum(select * gate, axis=1, keepdims=True))
        back.append(select.T.astype(BF16))
        select = select.astype(BF16)
        selects.append(select)
        at = pl.ds(b * CAP, CAP)
        rows_ref[at, :] = dot_nn(select, hid_ref[b]).astype(BF16)
        dy_ref[at, :] = (gates[b] * dot_nn(select, ds_ref[b])).astype(BF16)

    for copy in copies:
        copy.wait()
    rows, dy = rows_ref[...], dy_ref[...]
    for c in range(0, wide, step):
        at = pl.ds(c, step)
        act, slope = gelu_both(dot_nn(rows, up_ref[:, at]))
        act_ref[:, at] = act.astype(BF16)
        dpre_ref[:, at] = (slope * dot_nn(dy, down_ref[:, at])).astype(BF16)
    act, dpre = act_ref[...], dpre_ref[...]
    if more:
        for copy in came_copies:
            copy.wait()
    for b in range(BLOCKS):
        if more:
            came = keep if b < half else send
            acc_d[b] = came[b % half, 0:seq, :].astype(F32)
            acc_y[b] = came[b % half, seq + HEAD : 2 * seq + HEAD, :].astype(F32)
            gg_acc[b] = came[b % half, 2 * seq + HEAD : 2 * (seq + HEAD), :].astype(F32)
        else:
            acc_d[b] = jnp.zeros((seq, feat), F32)
            acc_y[b] = jnp.zeros((seq, feat), F32)
            gg_acc[b] = jnp.zeros((HEAD, feat), F32)
    gg = [jnp.zeros((CAP, 1), F32)] * BLOCKS
    for c in range(0, feat, step):
        at = pl.ds(c, step)
        res = dot_nt(act, down_ref[at, :])
        dx = dot_nt(dpre, up_ref[at, :]).astype(BF16)
        for b in range(BLOCKS):
            value = res[b * CAP : (b + 1) * CAP]
            slots = pl.ds(b * CAP, CAP)
            gg[b] = gg[b] + jnp.sum(value * dy_ref[slots, at].astype(F32), axis=1, keepdims=True)
            acc_y[b, :, at] += dot_nn(back[b], (gates[b] * value).astype(BF16))
            acc_d[b, :, at] += dot_nn(back[b], dx[b * CAP : (b + 1) * CAP])
    for b in range(BLOCKS):
        m = meta[b]
        inverse = jnp.where(gates[b] > 0.0, 1.0 / jnp.where(gates[b] > 0.0, gates[b], 1.0), 0.0)
        token = jnp.sum(selects[b].astype(F32) * (gg[b] * inverse), axis=0, keepdims=True)
        in0 = (m[0:1, 0:seq] == name).astype(F32)
        in1 = (m[0:1, seq : 2 * seq] == name).astype(F32)
        gg_acc[b, 0:1, 0:seq] += in0 * token
        gg_acc[b, 0:1, seq : 2 * seq] += in1 * token

    if shared:
        hid = hid_ref[...].reshape(BLOCKS * seq, feat)
        ds = ds_ref[...].reshape(BLOCKS * seq, feat)
        act_s, slope = gelu_both(dot_nt(hid, sup_ref[...]))
        act_s = act_s.astype(BF16)
        dpre_s = (slope * dot_nn(ds, sdown_ref[...])).astype(BF16)
        g_one, g_two = dot_tn(dpre_s, hid), dot_tn(ds, act_s)
        gsup[...] = g_one + gsup_in[...] if before else g_one
        gsdown[...] = g_two + gsdown_in[...] if before else g_two
        for c in range(0, feat, step):
            at = pl.ds(c, step)
            acc_y[:, :, at] += dot_nt(act_s, sdown_ref[at, :]).reshape(BLOCKS, seq, step)
            acc_d[:, :, at] += dot_nn(dpre_s, sup_ref[:, at]).reshape(BLOCKS, seq, step)
    for b in range(BLOCKS):
        out = keep if b < half else send
        out[b % half, 0:seq, :] = acc_d[b].astype(BF16)
        gate_sum = jnp.zeros((HEAD, feat), F32)
        if final:
            gate_sum = jnp.sum(gs[b][0:seq, :].astype(F32) * acc_y[b], axis=0, keepdims=True)
            gate_sum = jnp.broadcast_to(gate_sum, (HEAD, feat))
        out[b % half, seq : seq + HEAD, :] = gate_sum.astype(BF16)
        out[b % half, seq + HEAD : 2 * seq + HEAD, :] = acc_y[b].astype(BF16)
        out[b % half, 2 * seq + HEAD : 2 * (seq + HEAD), :] = gg_acc[b].astype(BF16)

    sum_copies = [
        pltpu.make_async_copy(keep, keep_out, sems.at[5]),
        pltpu.make_async_copy(send, send_out, sems.at[5]),
    ]
    for copy in sum_copies:
        copy.start()
    if before:
        old.wait()
    per = feat // blocks

    def put(i, kind, start, value):
        at = pl.ds(start, value.shape[0])
        if before:
            value = value + old_ref[i, kind, at, :].astype(F32)
        new_ref[i, kind, at, :] = value.astype(BF16)

    for c in range(0, feat, step):
        total = dot_tn(rows_ref[:, c : c + step], dpre)
        for i in range(blocks):
            put(i, 0, c, total[:, i * part : (i + 1) * part])
    first_out = pltpu.make_async_copy(new_ref.at[:, 0], grads.at[:, 0], sems.at[2])
    first_out.start()
    chunk = 2 * per if blocks > 1 else step
    for c in range(0, feat, chunk):
        total = dot_tn(dy_ref[:, c : c + chunk], act)
        if blocks == 1:
            put(0, 1, c, total)
            continue
        for i in range(2):
            for q in range(blocks):
                value = total[i * per : (i + 1) * per, q * part : (q + 1) * part]
                put(c // per + i, 1, q * per, value)
    second_out = pltpu.make_async_copy(new_ref.at[:, 1], grads.at[:, 1], sems.at[3])
    second_out.start()
    first_out.wait()
    second_out.wait()
    for copy in sum_copies:
        copy.wait()


def mix(first, hid, grads, block, ups, downs, shared, more, before, final):
    full, feat = hid[0].shape[1:]
    rows = full - HEAD
    count = len(ups)
    half, total = BLOCKS // 2, BLOCKS * CAP
    wide = downs[0].shape[-1]
    blocks = count
    part = wide // blocks
    sds = jax.ShapeDtypeStruct
    given = [*hid, *grads, *ups, *downs]
    pair = lambda at: pl.BlockSpec((half, full, feat), lambda i: (at, 0, 0))
    specs = [pair(0), pair(0), pair(block), pair(block)] + [HBM_SPEC] * (2 * count)
    outs = [sds((half, 2 * full, feat), BF16)] * 2 + [sds((blocks, 2, feat, part), BF16)]
    out_specs = [HBM_SPEC] * 3
    swide = 16 * count
    if shared is not None:
        swide = shared[0].shape[1]
        given += shared
        specs += [VMEM_SPEC] + [HBM_SPEC] * (len(shared) - 1)
        outs += [sds((swide, feat), F32), sds((feat, swide), F32)]
        out_specs += [VMEM_SPEC] * 2
    if more is not None:
        given += more
        specs += [HBM_SPEC] * 2
    if before is not None:
        given += before
        specs += [HBM_SPEC] + [VMEM_SPEC] * (len(before) - 1)
    old_shape = (blocks, 2, feat, part) if before is not None else (1, 1, 16, 128)
    return pl.pallas_call(
        functools.partial(
            mix_kernel, count, shared is not None, more is not None, before is not None, final
        ),
        grid=(1,),
        in_specs=[SMEM_SPEC] + specs,
        out_specs=out_specs,
        out_shape=outs,
        scratch_shapes=[
            pltpu.VMEM((total, feat), BF16),
            pltpu.VMEM((total, wide), BF16),
            pltpu.VMEM((total, wide), BF16),
            pltpu.VMEM((total, feat), BF16),
            pltpu.VMEM((BLOCKS, rows, feat), BF16),
            pltpu.VMEM((BLOCKS, rows, feat), BF16),
            pltpu.VMEM((BLOCKS, HEAD, feat), F32),
            pltpu.VMEM((BLOCKS, rows, feat), F32),
            pltpu.VMEM((BLOCKS, rows, feat), F32),
            pltpu.VMEM((BLOCKS, HEAD, feat), F32),
            pltpu.VMEM((feat, wide), BF16),
            pltpu.VMEM((feat, wide), BF16),
            pltpu.VMEM((swide, feat), BF16),
            pltpu.VMEM(old_shape, BF16),
            pltpu.VMEM((blocks, 2, feat, part), BF16),
            pltpu.VMEM((half, 2 * full, feat), BF16),
            pltpu.VMEM((half, 2 * full, feat), BF16),
            pltpu.SemaphoreType.DMA((6,)),
        ],
        compiler_params=pltpu.CompilerParams(vmem_limit_bytes=58 * 2**20),
        cost_estimate=CHEAP,
    )(first, *given)


def norm_back(upstream, normed, inverse):
    mean_grad = jnp.mean(upstream, axis=-1, keepdims=True)
    mean_mix = jnp.mean(upstream * normed, axis=-1, keepdims=True)
    return inverse * (upstream - mean_grad - normed * mean_mix)


def dot_nn(left, right):
    return jnp.dot(left, right, preferred_element_type=F32)


def dot_tn(left, right):
    return lax.dot_general(left, right, (((0,), (0,)), ((), ())), preferred_element_type=F32)


def dot_nt(left, right):
    return lax.dot_general(left, right, (((1,), (1,)), ((), ())), preferred_element_type=F32)


def local_grad(function, inputs, upstream):
    unused, pull = jax.vjp(function, inputs)
    return pull(upstream)[0]


def row_norm(values):
    center = values - jnp.mean(values, axis=-1, keepdims=True)
    inverse = lax.rsqrt(jnp.mean(center * center, axis=-1, keepdims=True) + 1e-06)
    return center * inverse, inverse


def load_weights(where_ref, pieces, spots, wq, wp, sem):
    copies = []
    for ref, blocks, lane in spots:
        piece = pieces[ref]
        rq = wq.shape[0] // where_ref.shape[0]
        rp = wp.shape[0] // where_ref.shape[0]
        width = piece.shape[2]
        for j, block in enumerate(blocks):
            at = where_ref[block]
            lanes = pl.ds(lane, width)
            to_q = wq.at[pl.ds(pl.multiple_of(at * rq, 16), rq), lanes]
            to_p = wp.at[pl.ds(pl.multiple_of(at * rp, 16), rp), lanes]
            copies.append(pltpu.make_async_copy(piece.at[j, pl.ds(0, rq), :], to_q, sem))
            copies.append(pltpu.make_async_copy(piece.at[j, pl.ds(rq, rp), :], to_p, sem))
    for copy in copies:
        copy.start()
    return copies


def pair_masks():
    lane = lax.broadcasted_iota(jnp.int32, (1, 2 * HD), 1)
    return [(lane < HD).astype(F32).astype(BF16), (lane >= HD).astype(F32).astype(BF16)]


def head_probs(query, key, mask):
    scores = dot_nt(query * mask, key) * (1.0 / math.sqrt(HD))
    exp_scores = jnp.exp(scores - jnp.max(scores, axis=-1, keepdims=True))
    return exp_scores / jnp.sum(exp_scores, axis=-1, keepdims=True)


def attend_kernel(spots, where_ref, tok_ref, mod_ref, *refs):
    count = len({spot[0] for spot in spots})
    pieces = refs[:count]
    late_ref, x1_ref, projected_ref, h1_ref, qkv_ref, attn_ref, wq, wp, sem = refs[count:]
    copies = load_weights(where_ref, pieces, spots, wq, wp, sem)
    rows, feat = tok_ref.shape
    tokens = tok_ref[...].astype(F32)
    norm, unused = row_norm(tokens)
    h1_ref[...] = (norm * (1.0 + mod_ref[1:2, :]) + mod_ref[0:1, :]).astype(BF16)
    for copy in copies:
        copy.wait()
    h1 = h1_ref[...]
    for c in range(0, 3 * feat, 256):
        at = pl.ds(c, 256)
        qkv_ref[:, at] = dot_nt(h1, wq[at, :]).astype(BF16)
    low, high = pair_masks()
    for c in range(0, feat, 2 * HD):
        at = pl.ds(c, 2 * HD)
        query, key = qkv_ref[:, at], qkv_ref[:, pl.ds(feat + c, 2 * HD)]
        value = qkv_ref[:, pl.ds(2 * feat + c, 2 * HD)]
        first = head_probs(query, key, low).astype(BF16)
        second = head_probs(query, key, high).astype(BF16)
        attn_ref[:, at] = (dot_nn(first, value * low) + dot_nn(second, value * high)).astype(BF16)
    attn = attn_ref[...]
    for c in range(0, feat, 256):
        at = pl.ds(c, 256)
        projected_ref[:, at] = dot_nt(attn, wp[at, :])
    x1 = tokens + mod_ref[2:3, :] * projected_ref[...]
    x1_ref[...] = x1
    norm, unused = row_norm(x1)
    late_ref[0:rows, :] = (norm * (1.0 + mod_ref[4:5, :]) + mod_ref[3:4, :]).astype(BF16)
    gate = mod_ref[5:6, :]
    gate_high = gate.astype(BF16).astype(F32)
    line = lax.broadcasted_iota(jnp.int32, (HEAD, feat), 0)
    late_ref[rows : rows + HEAD, :] = jnp.where(
        line == 0, gate_high, jnp.where(line == 1, gate - gate_high, 0.0)
    ).astype(BF16)


VMEM_SPEC = pl.BlockSpec(memory_space=pltpu.VMEM)
SMEM_SPEC = pl.BlockSpec(memory_space=pltpu.SMEM)
HBM_SPEC = pl.BlockSpec(memory_space=pl.ANY)
CHEAP = pl.CostEstimate(flops=10**6, bytes_accessed=10**5, transcendentals=0)


def attend(tokens, mod, where, pieces, spots):
    rows, feat = tokens.shape
    sds = jax.ShapeDtypeStruct
    return pl.pallas_call(
        functools.partial(attend_kernel, spots),
        in_specs=[SMEM_SPEC, VMEM_SPEC, VMEM_SPEC] + [HBM_SPEC] * len(pieces),
        out_specs=[VMEM_SPEC] * 6,
        out_shape=[
            sds((rows + HEAD, feat), BF16),
            sds((rows, feat), F32),
            sds((rows, feat), F32),
            sds((rows, feat), BF16),
            sds((rows, 3 * feat), BF16),
            sds((rows, feat), BF16),
        ],
        scratch_shapes=[
            pltpu.VMEM((3 * feat, feat), BF16),
            pltpu.VMEM((feat, feat), BF16),
            pltpu.SemaphoreType.DMA,
        ],
        compiler_params=pltpu.CompilerParams(vmem_limit_bytes=40 * 2**20),
        cost_estimate=CHEAP,
    )(where, tokens, mod, *pieces)


def back_kernel(spots, blocks, where_ref, dh2_ref, grad_ref, tok_ref, mod_ref, x1_ref, projected_ref, h1_ref, qkv_ref, attn_ref, *refs):
    count = len({spot[0] for spot in spots})
    pieces = refs[:count]
    outs = refs[count:]
    tokens_out, sums_out = outs[0], outs[1]
    wq, wp, dqkv, dattn, sem = outs[-5:]
    grads = outs[2:-5]
    copies = load_weights(where_ref, pieces, spots, wq, wp, sem)
    rows, feat = tok_ref.shape
    norm_two, inverse_two = row_norm(x1_ref[...])
    dh2 = dh2_ref[...]
    d_x1 = grad_ref[...].astype(F32) + norm_back(dh2 * (1.0 + mod_ref[4:5, :]), norm_two, inverse_two)
    sums_out[3:4, :] = jnp.sum(dh2, axis=0, keepdims=True)
    sums_out[4:5, :] = jnp.sum(dh2 * norm_two, axis=0, keepdims=True)
    sums_out[2:3, :] = jnp.sum(d_x1 * projected_ref[...], axis=0, keepdims=True)
    sums_out[5:8, :] = jnp.zeros((3, feat), F32)
    dp = (mod_ref[2:3, :] * d_x1).astype(BF16)
    for copy in copies:
        copy.wait()

    def put(kind, start, size, value):
        if len(grads) == 2:
            grads[kind][start : start + size, :] = value.astype(BF16)
            return
        per = (3 * feat if kind == 0 else feat) // blocks
        base = 0 if kind == 0 else 3 * feat // blocks
        done = 0
        while done < size:
            block, inside = (start + done) // per, (start + done) % per
            take = min(size - done, per - inside)
            grads[0][block, base + inside : base + inside + take, :] = value[done : done + take].astype(BF16)
            done += take

    attn = attn_ref[...]
    for c in range(0, feat, 256):
        dattn[:, c : c + 256] = dot_nn(dp, wp[:, c : c + 256]).astype(BF16)
        put(1, c, 256, dot_tn(dp[:, c : c + 256], attn))
    low, high = pair_masks()
    scale = 1.0 / math.sqrt(HD)
    for c in range(0, feat, 2 * HD):
        at, at_key, at_value = pl.ds(c, 2 * HD), pl.ds(feat + c, 2 * HD), pl.ds(2 * feat + c, 2 * HD)
        query, key, value, d_out = qkv_ref[:, at], qkv_ref[:, at_key], qkv_ref[:, at_value], dattn[:, at]
        d_query, d_key, d_value = 0.0, 0.0, 0.0
        for mask in (low, high):
            probs = head_probs(query, key, mask)
            d_part = d_out * mask
            d_value = d_value + dot_tn(probs.astype(BF16), d_part)
            d_probs = dot_nt(d_part, value)
            delta = jnp.sum(probs * d_probs, axis=-1, keepdims=True)
            d_scores = (probs * (d_probs - delta)).astype(BF16)
            d_query = d_query + dot_nn(d_scores, key * mask)
            d_key = d_key + dot_tn(d_scores, query * mask)
        dqkv[:, at] = (d_query * scale).astype(BF16)
        dqkv[:, at_key] = (d_key * scale).astype(BF16)
        dqkv[:, at_value] = d_value.astype(BF16)
    h1 = h1_ref[...]
    d_all = dqkv[...]
    parts = []
    for c in range(0, feat, 256):
        parts.append(dot_nn(d_all, wq[:, c : c + 256]))
    d_h1 = jnp.concatenate(parts, axis=1)
    norm_one, inverse_one = row_norm(tok_ref[...].astype(F32))
    sums_out[0:1, :] = jnp.sum(d_h1, axis=0, keepdims=True)
    sums_out[1:2, :] = jnp.sum(d_h1 * norm_one, axis=0, keepdims=True)
    tokens_out[...] = d_x1 + norm_back(d_h1 * (1.0 + mod_ref[1:2, :]), norm_one, inverse_one)
    for c in range(0, 3 * feat, 256):
        put(0, c, 256, dot_tn(dqkv[:, c : c + 256], h1))


def attend_back(d_hid, grad_out, tokens, mod, saved, where, pieces, spots, blocks):
    rows, feat = tokens.shape
    sds = jax.ShapeDtypeStruct
    if blocks:
        shapes = [sds((blocks, 4 * feat // blocks, feat), BF16)]
    else:
        shapes = [sds((3 * feat, feat), BF16), sds((feat, feat), BF16)]
    return pl.pallas_call(
        functools.partial(back_kernel, spots, blocks),
        in_specs=[SMEM_SPEC] + [VMEM_SPEC] * (4 + len(saved)) + [HBM_SPEC] * len(pieces),
        out_specs=[VMEM_SPEC] * (2 + len(shapes)),
        out_shape=[sds((rows, feat), F32), sds((8, feat), F32)] + shapes,
        scratch_shapes=[
            pltpu.VMEM((3 * feat, feat), BF16),
            pltpu.VMEM((feat, feat), BF16),
            pltpu.VMEM((rows, 3 * feat), BF16),
            pltpu.VMEM((rows, feat), BF16),
            pltpu.SemaphoreType.DMA,
        ],
        compiler_params=pltpu.CompilerParams(vmem_limit_bytes=48 * 2**20),
        cost_estimate=CHEAP,
    )(where, d_hid, grad_out, tokens, mod, *saved, *pieces)


def swap(value, move):
    ndp, nz = lax.axis_size("dp"), lax.axis_size("expert")
    pairs = []
    for a in range(ndp):
        for b in range(nz):
            c, d = move(a, b)
            pairs.append((a * nz + b, c * nz + d))
    return lax.ppermute(value, AXES, pairs)


def swap_row(value):
    return swap(value, lambda a, b: (a ^ 4, b))


def swap_core(value):
    return swap(value, lambda a, b: (a ^ 1, b))


def swap_chip(value):
    return swap(value, lambda a, b: (a ^ 2, b))


def from_plane(value, step):
    nz = lax.axis_size("expert")
    return swap(value, lambda a, b: (a, (b - step) % nz))


def to_plane(value, step):
    nz = lax.axis_size("expert")
    return swap(value, lambda a, b: (a, (b + step) % nz))


def row_bits():
    return (lax.axis_size("dp") // TP).bit_length() - 1


def row_groups():
    ndp = lax.axis_size("dp")
    return [list(range(i, ndp, TP)) for i in range(TP)]


def gather_rows(value):
    return lax.all_gather(value, "dp", axis_index_groups=row_groups())


def reduce_rows(value):
    flat = value.astype(BF16).reshape(-1, value.shape[-1])
    flat = lax.psum_scatter(flat, "dp", tiled=True, axis_index_groups=row_groups())
    return flat.reshape(value.shape[1:])


def tie(*values):
    return lax.optimization_barrier(values)


def plane_steps():
    nz = lax.axis_size("expert")
    return sorted(range(1, nz), key=lambda step: (min(step, nz - step), step))


def gather_planes(block):
    return [block] + [from_plane(block, step) for step in plane_steps()]


def run_mixture(planes, early, weights, shared, first, send_shared):
    steps = plane_steps()
    rows = SEQ + HEAD
    far, near = jnp.stack(planes[2:]), jnp.stack(planes[:2])
    far_core = swap_core(far)
    near, far_core = tie(near, far_core)
    near_core = swap_core(near)
    far_sums, near_sums, done, shared_grads = None, None, [], None
    for i, (ups, downs) in enumerate(weights):
        name = jnp.stack([first[0] + i, first[1]]).astype(jnp.int32)
        both = shared if i == 0 else None
        following = weights[i + 1] if i + 1 < len(weights) else None
        split = following is not None and len(following[0]) == 3
        outs = mix(name, (far, far_core), early, 1, ups, downs, both, far_sums, None, following is None)
        if i == 0:
            near_core, *outs = tie(near_core, *outs)
        if following is None:
            shared_grads[0], shared_grads[1], *outs = tie(*shared_grads, *outs)
        if split:
            up, down = following
            up[1], up[2], down[1], down[2], *outs = tie(*up[1:], *down[1:], *outs)
            up.append(swap_chip(up[2]))
            down.append(swap_row(down[1]))
        far_sums, grads = list(outs[:2]), list(outs[2:])
        if following is None:
            total = far_sums[0].astype(F32) + swap_core(far_sums[1]).astype(F32)
            sent = [total[j, :rows].astype(BF16) for j in range(2)]
            *sent, near = tie(*sent, near)
            moved = [to_plane(part, step) for part, step in zip(sent, steps[1:])]
        final = following is None
        outs = mix(name, (near, near_core), early, 0, ups, downs, both, near_sums, grads, final)
        if split:
            up[3], down[3], *outs = tie(up[3], down[3], *outs)
        if following is None:
            moved[0], moved[1], *outs = tie(*moved, *outs)
        near_sums, grads = list(outs[:2]), list(outs[2:])
        done.append(grads[0])
        if i == 0:
            shared_grads = send_shared(*grads[1:])
    near = near_sums[0].astype(F32) + swap_core(near_sums[1]).astype(F32)
    d_hid = near[0][:rows]
    for part in moved:
        d_hid = d_hid + part.astype(F32)
    y_sent = [near[1, rows:].astype(BF16)] + [total[j, rows:].astype(BF16) for j in range(2)]
    dx_moved = to_plane(near[1, :rows].astype(BF16), steps[0])
    dx_moved, *y_sent = tie(dx_moved, *y_sent)
    y_moved = [to_plane(part, step) for part, step in zip(y_sent, steps)]
    return d_hid + dx_moved.astype(F32), near[0][rows:], y_moved, done, shared_grads


def fold_bit(part, axis, bit):
    send, keep = halves_of(part, axis, bit)
    return keep, swap_bit(send, bit)


def halves_of(part, axis, bit):
    at = (lax.axis_index("dp") >> bit) & 1
    send = lax.dynamic_index_in_dim(part, 1 - at, axis, False).astype(BF16)
    return send, lax.dynamic_index_in_dim(part, at, axis, False)


def swap_bit(value, bit):
    return swap(value, lambda a, b: (a ^ (1 << bit), b))


def add(pair):
    return pair[0].astype(F32) + pair[1].astype(F32)


def scatter_planes(part, split):
    nz = lax.axis_size("expert")
    z = lax.axis_index("expert")
    cut_q = split * nz
    cut_p = (part.shape[0] - cut_q) // nz

    def rows_of(plane):
        return jnp.concatenate(
            [
                lax.dynamic_slice_in_dim(part, plane * split, split, 0),
                lax.dynamic_slice_in_dim(part, cut_q + plane * cut_p, cut_p, 0),
            ]
        )

    total = rows_of(z)
    for step in range(1, nz):
        total = total + to_plane(rows_of((z + step) % nz).astype(BF16), step).astype(F32)
    return total


def two_parts(value):
    high = value.astype(BF16)
    return high, (value - high.astype(F32)).astype(BF16)


def local(
    tokens,
    timestep,
    labels,
    routes,
    expert_gates,
    grad_out,
    ada_weight,
    ada_bias,
    qkv_weight,
    proj_weight,
    shared_up,
    shared_down,
    expert_up,
    expert_down,
    time_table,
    class_table,
):
    rows, feat = tokens.shape
    ndp, nz = lax.axis_size("dp"), lax.axis_size("expert")
    reps = ndp // TP
    ndev = ndp * nz
    members = TP * nz
    local_experts = expert_up.shape[0]
    wide = expert_up.shape[2]
    down_cols = expert_down.shape[2]
    shared_wide = shared_up.shape[1]
    shared_cols = shared_down.shape[1]
    qkv_cols = qkv_weight.shape[1]
    proj_cols = proj_weight.shape[1]
    table_cols = time_table.shape[1]
    plane = lax.axis_index("expert")

    def exchange(value):
        return lax.all_to_all(value, AXES, 0, 0, tiled=True)

    if reps == 4 and wide % 128 == 0 and 2 * wide == feat:
        tail = shared_up.T
        tail = jnp.concatenate([tail[:, :wide], tail[:, wide:]])
    else:
        tail = shared_up.T[:, :wide]
    ups = [expert_up[e] for e in range(local_experts)]
    ups[0] = jnp.concatenate([ups[0], tail])
    flipped = expert_down.transpose(0, 2, 1)
    halves = [
        jnp.concatenate(
            [flipped[:, :, (i * TP + t) * wide : (i * TP + t + 1) * wide] for i in range(reps)],
            axis=2,
        )
        for t in range(TP)
    ]
    core_low = lax.axis_index("dp") % TP == 0
    mine = jnp.where(core_low, halves[0], halves[1])
    moved = swap_core(jnp.where(core_low, halves[1], halves[0]))
    downs = jnp.where(
        core_low, jnp.concatenate([mine, moved], axis=1), jnp.concatenate([moved, mine], axis=1)
    )
    downs = [downs[e] for e in range(local_experts)]
    sdowns = shared_down.T.reshape(shared_cols, reps, TP, nz, shared_wide)
    sdowns = sdowns.transpose(2, 3, 0, 1, 4).reshape(1, members, shared_cols, reps * shared_wide)
    sdowns = jnp.broadcast_to(sdowns, (reps,) + sdowns.shape[1:])
    sdowns = sdowns.reshape(ndev, shared_cols, reps * shared_wide)
    gate_high, gate_low = two_parts(expert_gates)
    meta = jnp.stack(
        [
            routes[:, 0].astype(BF16),
            routes[:, 1].astype(BF16),
            gate_high[:, 0],
            gate_high[:, 1],
            gate_low[:, 0],
            gate_low[:, 1],
        ]
    )
    meta = jnp.pad(meta.reshape(-1, feat), ((0, HEAD - meta.size // feat), (0, 0)))
    early = jnp.concatenate([grad_out, meta])

    early_planes = lax.all_gather(early, "expert")
    order = (plane + jnp.array([0] + plane_steps(), jnp.int32)) % nz
    early_planes = jnp.take(early_planes, order, axis=0, mode="clip")
    early_core = swap_core(early_planes)

    pair = jnp.concatenate([qkv_weight.T, proj_weight.T])
    rq, rp = nz * qkv_cols, nz * proj_cols
    packed = ndp == 8 and rq % 16 == 0 and rp % 16 == 0
    ids = jnp.concatenate([timestep, labels])[None]
    all_ids = exchange(jnp.broadcast_to(ids, (ndev, 2)))
    if packed:
        line = jnp.stack([pair] + [from_plane(pair, step) for step in range(1, nz)])
        order = (jnp.arange(nz, dtype=jnp.int32) - plane) % nz
        line = jnp.take(line, order, axis=0, mode="clip")
        line = jnp.concatenate(
            [line[:, :qkv_cols].reshape(rq, feat), line[:, qkv_cols:].reshape(rp, feat)]
        )
        half = feat // 2
        left, right = line[None, :, :half], line[None, :, half:]
        left_x, right_y = swap_chip(left), swap_row(right)
    pick_time = all_ids[:, :1] == jnp.arange(time_table.shape[0], dtype=jnp.int32)[None]
    pick_class = all_ids[:, 1:] == jnp.arange(class_table.shape[0], dtype=jnp.int32)[None]
    cond_cols = dot_nn(pick_time.astype(BF16), time_table) + dot_nn(
        pick_class.astype(BF16), class_table
    )
    cond_all = exchange(jnp.broadcast_to(cond_cols[None], (ndev, ndev, table_cols)))
    if packed:
        left_x, right_y, cond_all = tie(left_x, right_y, cond_all)
        left_x, right_y = jnp.concatenate([left, left_x]), jnp.concatenate([right, right_y])
        left_y, right_x = swap_row(left_x), swap_chip(right_y)
        left_core, right_core = swap_core(left_x), swap_core(right_y)
    cond_all = cond_all.transpose(1, 0, 2).reshape(ndev, feat)
    silu_all = jax.nn.silu(cond_all).astype(BF16)
    my_index = lax.axis_index(AXES)
    cond_own = lax.dynamic_slice_in_dim(cond_all, my_index, 1, 0)
    mod_cols = dot_nn(silu_all, ada_weight) + ada_bias.astype(F32)[None]
    mod = exchange(mod_cols).reshape(6, feat)
    if packed:
        sdowns, mod = tie(sdowns, mod)
        sdown_t = exchange(sdowns).reshape(feat, reps * shared_wide)
        pieces = [left_x, left_y, left_core, swap_core(left_y)]
        pieces += [right_y, right_x, right_core, swap_core(right_x)]
        mine = lax.axis_index("dp")
        moves = [0, 2, 4, 6, 1, 3, 5, 7]
        where = jnp.stack([mine ^ m for m in moves]).astype(jnp.int32)
        spots = (
            (0, (0, 1), 0),
            (1, (2, 3), 0),
            (2, (4, 5), 0),
            (3, (6, 7), 0),
            (4, (0, 2), half),
            (5, (1, 3), half),
            (6, (4, 6), half),
            (7, (5, 7), half),
        )
        blocks = ndp
    else:
        pair = lax.all_gather(pair, AXES)
        pieces = [
            jnp.concatenate(
                [
                    pair[:, :qkv_cols].reshape(ndev * qkv_cols, feat),
                    pair[:, qkv_cols:].reshape(ndev * proj_cols, feat),
                ]
            )[None]
        ]
        where = jnp.zeros((1,), jnp.int32)
        spots = ((0, (0,), 0),)
        blocks = 0

    if packed:
        weights = []
        for e in range(local_experts):
            up, down = ups[e], downs[e]
            if e:
                up, down, weights[-1][0][1] = tie(up, down, weights[-1][0][1])
            else:
                up, down, mod = tie(up, down, mod)
            up = [up, swap_chip(up), swap_row(up)]
            down = [down, swap_chip(down), swap_row(down)]
            weights.append([up, down])
        shared = [sdown_t]
        place = lax.axis_index("dp") // TP

    mod_rows = jnp.concatenate([mod, jnp.zeros((2, feat), F32)])
    late, *saved_attn = attend(tokens, mod_rows, where, pieces, spots)
    middle = saved_attn[0]

    if packed:
        up, down = weights[0]
        late, up[2], down[1] = tie(late, up[2], down[1])
        up.append(swap_chip(up[2]))
        down.append(swap_row(down[1]))
    planes = gather_planes(late)
    if packed:
        *planes, up[1], up[3], down[2], down[3] = tie(*planes, up[1], up[3], down[2], down[3])
    if not packed:
        place = jnp.zeros((), jnp.int32)
        weights = []
        for e in range(local_experts):
            up = gather_rows(ups[e][:feat]).transpose(1, 0, 2).reshape(feat, reps * wide)
            weights.append([[up], [gather_rows(downs[e]).reshape(feat, reps * wide)]])
        sup_t = gather_rows(shared_up.T).reshape(reps * shared_wide, feat)
        shared = [exchange(sdowns).reshape(feat, reps * shared_wide), sup_t]

    first = jnp.stack([plane * local_experts, place]).astype(jnp.int32)
    early = (early_planes, early_core)
    def send_shared(g_sup, g_sdown):
        g_sup = g_sup.reshape((2,) * row_bits() + (shared_wide, feat))
        for bit in range(row_bits(), 1, -1):
            g_sup = add(fold_bit(g_sup, 0, bit))
        g_sdown = g_sdown.astype(BF16).reshape(ndev, shared_cols, reps * shared_wide)
        return [g_sup, exchange(g_sdown)]

    d_normed_two, branch, y_moved, done, shared_grads = run_mixture(
        planes, early, weights, shared, first, send_shared
    )
    d_normed_two, d_gate_two = d_normed_two[:rows], d_normed_two[rows : rows + 1]

    g_sup, g_sdown = shared_grads
    reduced = []
    for g_mix in done:
        if g_mix.shape[0] == 1:
            g_up = g_mix[0, 0].reshape(feat, reps, wide).transpose(1, 0, 2)
            g_down = g_mix[0, 1].reshape(reps, TP * down_cols, reps, wide).transpose(0, 2, 1, 3)
            g_mix = jnp.stack([g_up, g_down.reshape(reps, feat, wide)], axis=1)
        reduced.append(reduce_rows(g_mix))

    def finish_expert(pair):
        g_up, g_down = pair[0].astype(F32), pair[1].reshape(reps, TP, down_cols, wide)
        kept = jnp.where(core_low, g_down[:, 0], g_down[:, 1])
        got = swap_core(jnp.where(core_low, g_down[:, 1], g_down[:, 0]))
        g_down = [jnp.where(core_low, kept, got), jnp.where(core_low, got, kept)]
        g_down = jnp.concatenate([g_down[t][i] for i in range(reps) for t in range(TP)], axis=1)
        return g_up, g_down.T.astype(F32)

    up_part, down_part = [], []
    for pair in reduced[:-1]:
        g_up, g_down = finish_expert(pair)
        g_up, g_down, d_normed_two = tie(g_up, g_down, d_normed_two)
        up_part.append(g_up)
        down_part.append(g_down)

    tokens_grad, sums, *g_small = attend_back(
        d_normed_two, grad_out, tokens, mod_rows, saved_attn, where, pieces, spots, blocks
    )
    d_mod = jnp.concatenate([sums[0:5], d_gate_two]).astype(BF16).reshape(ndev, -1)
    d_mod = exchange(d_mod)
    if packed:
        half = feat // 2
        kept, got = fold_bit(g_small[0].reshape((2, 2, 2) + g_small[0].shape[1:]), 2, 0)
        d_mod, kept, got, reduced[-1] = tie(d_mod, kept, got, reduced[-1])
        g_small = add((kept, got))
        left, right = halves_of(g_small[..., :half], 1, 1), halves_of(g_small[..., half:], 0, 2)
        left_sent, right_sent, d_mod = tie(left[0], right[0], d_mod)
        left, right = (left[1], swap_bit(left_sent, 1)), (right[1], swap_bit(right_sent, 2))
    else:
        g_small = jnp.concatenate(
            [g_small[0].reshape(ndev, qkv_cols, feat), g_small[1].reshape(ndev, proj_cols, feat)],
            axis=1,
        )
        g_small = lax.psum_scatter(g_small, AXES).astype(F32)
    d_cond = dot_nt(d_mod, ada_weight)
    d_cond_cols = d_cond.reshape(ndev, ndev, table_cols).transpose(1, 0, 2).reshape(ndev, -1)
    d_cond = exchange(jnp.concatenate([d_cond, d_cond_cols], axis=1))
    sup_part = add(fold_bit(g_sup, 0, 1)).T
    last_up, last_down = finish_expert(reduced[-1])
    if packed:
        left, right, d_cond, g_sdown, *y_moved = tie(
            add(left), add(right), d_cond, g_sdown, *y_moved
        )
        left, right = fold_bit(left, 0, 2), fold_bit(right, 0, 1)
        left, right, last_up, last_down, sup_part = tie(
            add(left), add(right), last_up, last_down, sup_part
        )
        g_small = scatter_planes(jnp.concatenate([left, right], axis=-1), qkv_cols)
    up_part = jnp.stack(up_part + [last_up])
    down_part = jnp.stack(down_part + [last_down])
    for part in y_moved:
        branch = branch + part.astype(F32)
    gates_grad = branch[rows, : 2 * rows].reshape(2, rows).T
    block_out = (middle + mod[5:6] * branch[:rows]).astype(BF16)
    d_cond = jnp.sum(d_cond, axis=0, keepdims=True)
    cond_grad = local_grad(jax.nn.silu, cond_own, d_cond[:, :feat])
    d_cond_cols = d_cond[:, feat:].reshape(ndev, table_cols)
    d_cond_cols = local_grad(jax.nn.silu, cond_cols, d_cond_cols)
    ada_part = dot_tn(silu_all, d_mod)
    bias_part = jnp.sum(d_mod.astype(F32), axis=0)
    g_sdown = g_sdown.reshape(reps, members, shared_cols, reps, shared_wide)
    g_sdown = jnp.sum(g_sdown.astype(F32), axis=0)
    sdown_part = g_sdown.transpose(2, 0, 3, 1).reshape(reps * members * shared_wide, shared_cols)

    def table_grad(pick):
        return lax.dot_general(
            pick.astype(F32),
            d_cond_cols,
            (((0,), (0,)), ((), ())),
            precision=lax.Precision.HIGHEST,
            preferred_element_type=F32,
        )

    time_part, class_part = table_grad(pick_time), table_grad(pick_class)

    qkv_part = g_small[:qkv_cols].T
    proj_part = g_small[qkv_cols:].T
    return (
        block_out,
        tokens_grad,
        cond_grad,
        gates_grad,
        ada_part,
        bias_part,
        qkv_part,
        proj_part,
        sup_part,
        sdown_part,
        up_part,
        down_part,
        time_part,
        class_part,
    )


def solution(mesh):
    both = ("dp", "expert")
    by_rows, by_cols, by_first = P(both, None), P(None, both), P(both)
    by_expert = P("expert", None, "dp")
    return jax.shard_map(
        local,
        mesh=mesh,
        in_specs=(
            by_rows,
            by_first,
            by_first,
            by_rows,
            by_rows,
            by_rows,
            by_cols,
            by_first,
            by_cols,
            by_cols,
            by_cols,
            by_cols,
            by_expert,
            by_expert,
            by_cols,
            by_cols,
        ),
        out_specs=(
            by_rows,
            by_rows,
            by_rows,
            by_rows,
            by_cols,
            by_first,
            by_cols,
            by_cols,
            by_cols,
            by_cols,
            by_expert,
            by_expert,
            by_cols,
            by_cols,
        ),
        check_vma=False,
    )
```

```python
import functools
import math

import jax
import jax.numpy as jnp
from jax import lax
from jax.experimental import pallas as pl
from jax.experimental.pallas import tpu as pltpu
from jax.sharding import PartitionSpec as P

H = 12
HD = 64
SEQ = 256
CAP = 128
TP = 2
AXES = ("dp", "expert")
F32 = jnp.float32
BF16 = jnp.bfloat16

HEAD = 16
BLOCKS = 4
GELU_A = math.sqrt(2.0 / math.pi)
GELU_B = 0.044715


def gelu_both(x):
    square = x * x
    t = jnp.tanh(GELU_A * x * (1.0 + GELU_B * square))
    half = 0.5 * (1.0 + t)
    slope = half + 0.5 * x * (1.0 - t * t) * (GELU_A + 3.0 * GELU_A * GELU_B * square)
    return x * half, slope


def mix_kernel(count, shared, more, before, final, first_ref, h_own, h_core, g_own, g_core, *refs):
    refs = list(refs)

    def take(number):
        taken = refs[:number]
        del refs[:number]
        return taken

    ups, downs = take(count), take(count)
    if shared:
        (sdown_ref,) = take(1)
        if count == 1:
            (sup_in,) = take(1)
    if more:
        sums_in = take(4)
    if before:
        (grads_in,) = take(1)
        if shared:
            gsup_in, gsdown_in = take(2)
    sums_out = take(4)
    (grads,) = take(1)
    if shared:
        gsup, gsdown = take(2)
    rows_ref, act_ref, dpre_ref, dy_ref, hid_ref, ds_ref, meta, acc_y, acc_d, gg_acc = take(10)
    up_ref, down_ref, sup_ref, old_ref, new_ref, *sums, sems = refs
    (keep_d, keep_y, send_d, send_y) = sums
    seq, feat = SEQ, h_own.shape[2]
    step = 256
    wide = up_ref.shape[1]
    blocks, part = new_ref.shape[0], new_ref.shape[3]

    copies = []
    if count == 1:
        copies.append(pltpu.make_async_copy(ups[0], up_ref, sems.at[0]))
        copies.append(pltpu.make_async_copy(downs[0], down_ref, sems.at[0]))
        if shared:
            copies.append(pltpu.make_async_copy(sup_in, sup_ref, sems.at[0]))
    else:
        per, swide = feat // count, sup_ref.shape[0] // count
        for i in range(count):
            place = first_ref[1] ^ i
            lanes = pl.ds(pl.multiple_of(place * part, 128), part)
            copies.append(
                pltpu.make_async_copy(ups[i].at[pl.ds(0, feat), :], up_ref.at[:, lanes], sems.at[0])
            )
            at = pl.ds(pl.multiple_of(place * per, 16), per)
            copies.append(pltpu.make_async_copy(downs[i], down_ref.at[at, :], sems.at[0]))
            if shared:
                at = pl.ds(pl.multiple_of(place * swide, 16), swide)
                for j in range(2):
                    copies.append(
                        pltpu.make_async_copy(
                            ups[i].at[pl.ds(feat + j * swide, swide), :],
                            sup_ref.at[at, pl.ds(j * part, part)],
                            sems.at[0],
                        )
                    )
    for copy in copies:
        copy.start()
    if more:
        came_copies = [pltpu.make_async_copy(a, b, sems.at[4]) for a, b in zip(sums_in, sums)]
        for copy in came_copies:
            copy.start()
    if before:
        old = pltpu.make_async_copy(grads_in, old_ref, sems.at[1])
        old.start()

    hs = [h_own.at[0], h_own.at[1], h_core.at[0], h_core.at[1]]
    gs = [g_own.at[0], g_own.at[1], g_core.at[0], g_core.at[1]]
    half = BLOCKS // 2
    for b in range(BLOCKS):
        hid_ref[b] = hs[b][0:seq, :]
        tail = hs[b][seq : seq + HEAD, :].astype(F32)
        gate_two = tail[0:1] + tail[1:2]
        ds_ref[b] = (gate_two * gs[b][0:seq, :].astype(F32)).astype(BF16)
        meta[b] = gs[b][seq : seq + HEAD, :].astype(F32)

    name = first_ref[0].astype(F32)
    up_down = lax.broadcasted_iota(jnp.int32, (seq, seq), 0) <= lax.broadcasted_iota(
        jnp.int32, (seq, seq), 1
    )
    ones_tri = up_down.astype(F32).astype(BF16)
    slot = lax.broadcasted_iota(jnp.int32, (CAP, seq), 0).astype(F32)
    selects, back, gates = [], [], []
    for b in range(BLOCKS):
        m = meta[b]
        in0 = (m[0:1, 0:seq] == name).astype(F32)
        in1 = (m[0:1, seq : 2 * seq] == name).astype(F32)
        gate = in0 * (m[0:1, 2 * seq : 3 * seq] + m[1:2, seq : 2 * seq]) + in1 * (
            m[1:2, 0:seq] + m[1:2, 2 * seq : 3 * seq]
        )
        has = in0 + in1
        count_row = dot_nn(jnp.broadcast_to(has, (16, seq)).astype(BF16), ones_tri)[0:1]
        select = (count_row * has - 1.0 == slot).astype(F32)
        gates.append(jnp.sum(select * gate, axis=1, keepdims=True))
        back.append(select.T.astype(BF16))
        select = select.astype(BF16)
        selects.append(select)
        at = pl.ds(b * CAP, CAP)
        rows_ref[at, :] = dot_nn(select, hid_ref[b]).astype(BF16)
        dy_ref[at, :] = (gates[b] * dot_nn(select, ds_ref[b])).astype(BF16)

    for copy in copies:
        copy.wait()
    rows, dy = rows_ref[...], dy_ref[...]
    for c in range(0, wide, step):
        at = pl.ds(c, step)
        act, slope = gelu_both(dot_nn(rows, up_ref[:, at]))
        act_ref[:, at] = act.astype(BF16)
        dpre_ref[:, at] = (slope * dot_nn(dy, down_ref[:, at])).astype(BF16)
    act, dpre = act_ref[...], dpre_ref[...]
    if more:
        for copy in came_copies:
            copy.wait()
    for b in range(BLOCKS):
        if more:
            came_d, came_y = (keep_d, keep_y) if b < half else (send_d, send_y)
            acc_d[b] = came_d[b % half, 0:seq, :].astype(F32)
            acc_y[b] = came_y[b % half, 0:seq, :].astype(F32)
            gg_acc[b] = came_y[b % half, seq : seq + HEAD, :].astype(F32)
        else:
            acc_d[b] = jnp.zeros((seq, feat), F32)
            acc_y[b] = jnp.zeros((seq, feat), F32)
            gg_acc[b] = jnp.zeros((HEAD, feat), F32)
    gg = [jnp.zeros((CAP, 1), F32)] * BLOCKS
    for c in range(0, feat, step):
        at = pl.ds(c, step)
        res = dot_nt(act, down_ref[at, :])
        dx = dot_nt(dpre, up_ref[at, :]).astype(BF16)
        for b in range(BLOCKS):
            value = res[b * CAP : (b + 1) * CAP]
            slots = pl.ds(b * CAP, CAP)
            gg[b] = gg[b] + jnp.sum(value * dy_ref[slots, at].astype(F32), axis=1, keepdims=True)
            acc_y[b, :, at] += dot_nn(back[b], (gates[b] * value).astype(BF16))
            acc_d[b, :, at] += dot_nn(back[b], dx[b * CAP : (b + 1) * CAP])
    for b in range(BLOCKS):
        m = meta[b]
        inverse = jnp.where(gates[b] > 0.0, 1.0 / jnp.where(gates[b] > 0.0, gates[b], 1.0), 0.0)
        token = jnp.sum(selects[b].astype(F32) * (gg[b] * inverse), axis=0, keepdims=True)
        in0 = (m[0:1, 0:seq] == name).astype(F32)
        in1 = (m[0:1, seq : 2 * seq] == name).astype(F32)
        gg_acc[b, 0:1, 0:seq] += in0 * token
        gg_acc[b, 0:1, seq : 2 * seq] += in1 * token

    if shared:
        hid = hid_ref[...].reshape(BLOCKS * seq, feat)
        ds = ds_ref[...].reshape(BLOCKS * seq, feat)
        act_s, slope = gelu_both(dot_nt(hid, sup_ref[...]))
        act_s = act_s.astype(BF16)
        dpre_s = (slope * dot_nn(ds, sdown_ref[...])).astype(BF16)
        g_one, g_two = dot_tn(dpre_s, hid), dot_tn(ds, act_s)
        if before:
            g_one, g_two = g_one + gsup_in[...], g_two + gsdown_in[...]
        gsup[...] = g_one.astype(gsup.dtype)
        gsdown[...] = g_two.astype(gsdown.dtype)
        for c in range(0, feat, step):
            at = pl.ds(c, step)
            acc_y[:, :, at] += dot_nt(act_s, sdown_ref[at, :]).reshape(BLOCKS, seq, step)
            acc_d[:, :, at] += dot_nn(dpre_s, sup_ref[:, at]).reshape(BLOCKS, seq, step)
    for b in range(BLOCKS):
        out_d, out_y = (keep_d, keep_y) if b < half else (send_d, send_y)
        out_d[b % half, 0:seq, :] = acc_d[b].astype(BF16)
        gate_sum = jnp.zeros((HEAD, feat), F32)
        if final:
            gate_sum = jnp.sum(gs[b][0:seq, :].astype(F32) * acc_y[b], axis=0, keepdims=True)
            gate_sum = jnp.broadcast_to(gate_sum, (HEAD, feat))
        out_d[b % half, seq : seq + HEAD, :] = gate_sum.astype(BF16)
        out_y[b % half, 0:seq, :] = acc_y[b].astype(BF16)
        out_y[b % half, seq : seq + HEAD, :] = gg_acc[b].astype(BF16)

    sum_copies = [pltpu.make_async_copy(a, b, sems.at[5]) for a, b in zip(sums, sums_out)]
    for copy in sum_copies:
        copy.start()
    if before:
        old.wait()
    per = feat // blocks

    def put(i, kind, start, value):
        at = pl.ds(start, value.shape[0])
        if before:
            value = value + old_ref[i, kind, at, :].astype(F32)
        new_ref[i, kind, at, :] = value.astype(BF16)

    for c in range(0, feat, step):
        total = dot_tn(rows_ref[:, c : c + step], dpre)
        for i in range(blocks):
            put(i, 0, c, total[:, i * part : (i + 1) * part])
    first_out = pltpu.make_async_copy(new_ref.at[:, 0], grads.at[:, 0], sems.at[2])
    first_out.start()
    chunk = 2 * per if blocks > 1 else step
    for c in range(0, feat, chunk):
        total = dot_tn(dy_ref[:, c : c + chunk], act)
        if blocks == 1:
            put(0, 1, c, total)
            continue
        for i in range(2):
            for q in range(blocks):
                value = total[i * per : (i + 1) * per, q * part : (q + 1) * part]
                put(c // per + i, 1, q * per, value)
    second_out = pltpu.make_async_copy(new_ref.at[:, 1], grads.at[:, 1], sems.at[3])
    second_out.start()
    first_out.wait()
    second_out.wait()
    for copy in sum_copies:
        copy.wait()


def mix(first, hid, grads, block, ups, downs, shared, more, before, final):
    full, feat = hid[0].shape[1:]
    rows = full - HEAD
    count = len(ups)
    half, total = BLOCKS // 2, BLOCKS * CAP
    wide = downs[0].shape[-1]
    blocks = count
    part = wide // blocks
    sds = jax.ShapeDtypeStruct
    given = [*hid, *grads, *ups, *downs]
    pair = lambda at: pl.BlockSpec((half, full, feat), lambda i: (at, 0, 0))
    specs = [pair(0), pair(0), pair(block), pair(block)] + [HBM_SPEC] * (2 * count)
    outs = [sds((half, full, feat), BF16)] * 4 + [sds((blocks, 2, feat, part), BF16)]
    out_specs = [HBM_SPEC] * 5
    swide = 16 * count
    if shared is not None:
        swide = shared[0].shape[1]
        given += shared
        specs += [VMEM_SPEC] + [HBM_SPEC] * (len(shared) - 1)
        kind = F32 if before is None else BF16
        outs += [sds((swide, feat), kind), sds((feat, swide), kind)]
        out_specs += [VMEM_SPEC] * 2
    if more is not None:
        given += more
        specs += [HBM_SPEC] * 4
    if before is not None:
        given += before
        specs += [HBM_SPEC] + [VMEM_SPEC] * (len(before) - 1)
    old_shape = (blocks, 2, feat, part) if before is not None else (1, 1, 16, 128)
    return pl.pallas_call(
        functools.partial(
            mix_kernel, count, shared is not None, more is not None, before is not None, final
        ),
        grid=(1,),
        in_specs=[SMEM_SPEC] + specs,
        out_specs=out_specs,
        out_shape=outs,
        scratch_shapes=[
            pltpu.VMEM((total, feat), BF16),
            pltpu.VMEM((total, wide), BF16),
            pltpu.VMEM((total, wide), BF16),
            pltpu.VMEM((total, feat), BF16),
            pltpu.VMEM((BLOCKS, rows, feat), BF16),
            pltpu.VMEM((BLOCKS, rows, feat), BF16),
            pltpu.VMEM((BLOCKS, HEAD, feat), F32),
            pltpu.VMEM((BLOCKS, rows, feat), F32),
            pltpu.VMEM((BLOCKS, rows, feat), F32),
            pltpu.VMEM((BLOCKS, HEAD, feat), F32),
            pltpu.VMEM((feat, wide), BF16),
            pltpu.VMEM((feat, wide), BF16),
            pltpu.VMEM((swide, feat), BF16),
            pltpu.VMEM(old_shape, BF16),
            pltpu.VMEM((blocks, 2, feat, part), BF16),
            pltpu.VMEM((half, full, feat), BF16),
            pltpu.VMEM((half, full, feat), BF16),
            pltpu.VMEM((half, full, feat), BF16),
            pltpu.VMEM((half, full, feat), BF16),
            pltpu.SemaphoreType.DMA((6,)),
        ],
        compiler_params=pltpu.CompilerParams(vmem_limit_bytes=58 * 2**20),
        cost_estimate=CHEAP,
    )(first, *given)


def norm_back(upstream, normed, inverse):
    mean_grad = jnp.mean(upstream, axis=-1, keepdims=True)
    mean_mix = jnp.mean(upstream * normed, axis=-1, keepdims=True)
    return inverse * (upstream - mean_grad - normed * mean_mix)


def dot_nn(left, right):
    return jnp.dot(left, right, preferred_element_type=F32)


def dot_tn(left, right):
    return lax.dot_general(left, right, (((0,), (0,)), ((), ())), preferred_element_type=F32)


def dot_nt(left, right):
    return lax.dot_general(left, right, (((1,), (1,)), ((), ())), preferred_element_type=F32)


def local_grad(function, inputs, upstream):
    unused, pull = jax.vjp(function, inputs)
    return pull(upstream)[0]


def row_norm(values):
    center = values - jnp.mean(values, axis=-1, keepdims=True)
    inverse = lax.rsqrt(jnp.mean(center * center, axis=-1, keepdims=True) + 1e-06)
    return center * inverse, inverse


def load_weights(where_ref, pieces, spots, wq, wp, sem):
    copies = []
    for ref, blocks, lane in spots:
        piece = pieces[ref]
        rq = wq.shape[0] // where_ref.shape[0]
        rp = wp.shape[0] // where_ref.shape[0]
        width = piece.shape[2]
        for j, block in enumerate(blocks):
            at = where_ref[block]
            lanes = pl.ds(lane, width)
            to_q = wq.at[pl.ds(pl.multiple_of(at * rq, 16), rq), lanes]
            to_p = wp.at[pl.ds(pl.multiple_of(at * rp, 16), rp), lanes]
            copies.append(pltpu.make_async_copy(piece.at[j, pl.ds(0, rq), :], to_q, sem))
            copies.append(pltpu.make_async_copy(piece.at[j, pl.ds(rq, rp), :], to_p, sem))
    for copy in copies:
        copy.start()
    return copies


def pair_masks():
    lane = lax.broadcasted_iota(jnp.int32, (1, 2 * HD), 1)
    return [(lane < HD).astype(F32).astype(BF16), (lane >= HD).astype(F32).astype(BF16)]


def head_probs(query, key, mask):
    scores = dot_nt(query * mask, key) * (1.0 / math.sqrt(HD))
    exp_scores = jnp.exp(scores - jnp.max(scores, axis=-1, keepdims=True))
    return exp_scores / jnp.sum(exp_scores, axis=-1, keepdims=True)


def attend_kernel(spots, where_ref, tok_ref, mod_ref, *refs):
    count = len({spot[0] for spot in spots})
    pieces = refs[:count]
    late_ref, x1_ref, projected_ref, h1_ref, qkv_ref, attn_ref, wq, wp, sem = refs[count:]
    copies = load_weights(where_ref, pieces, spots, wq, wp, sem)
    rows, feat = tok_ref.shape
    tokens = tok_ref[...].astype(F32)
    norm, unused = row_norm(tokens)
    h1_ref[...] = (norm * (1.0 + mod_ref[1:2, :]) + mod_ref[0:1, :]).astype(BF16)
    for copy in copies:
        copy.wait()
    h1 = h1_ref[...]
    for c in range(0, 3 * feat, 256):
        at = pl.ds(c, 256)
        qkv_ref[:, at] = dot_nt(h1, wq[at, :]).astype(BF16)
    low, high = pair_masks()
    for c in range(0, feat, 2 * HD):
        at = pl.ds(c, 2 * HD)
        query, key = qkv_ref[:, at], qkv_ref[:, pl.ds(feat + c, 2 * HD)]
        value = qkv_ref[:, pl.ds(2 * feat + c, 2 * HD)]
        first = head_probs(query, key, low).astype(BF16)
        second = head_probs(query, key, high).astype(BF16)
        attn_ref[:, at] = (dot_nn(first, value * low) + dot_nn(second, value * high)).astype(BF16)
    attn = attn_ref[...]
    for c in range(0, feat, 256):
        at = pl.ds(c, 256)
        projected_ref[:, at] = dot_nt(attn, wp[at, :])
    x1 = tokens + mod_ref[2:3, :] * projected_ref[...]
    x1_ref[...] = x1
    norm, unused = row_norm(x1)
    late_ref[0:rows, :] = (norm * (1.0 + mod_ref[4:5, :]) + mod_ref[3:4, :]).astype(BF16)
    gate = mod_ref[5:6, :]
    gate_high = gate.astype(BF16).astype(F32)
    line = lax.broadcasted_iota(jnp.int32, (HEAD, feat), 0)
    late_ref[rows : rows + HEAD, :] = jnp.where(
        line == 0, gate_high, jnp.where(line == 1, gate - gate_high, 0.0)
    ).astype(BF16)


VMEM_SPEC = pl.BlockSpec(memory_space=pltpu.VMEM)
SMEM_SPEC = pl.BlockSpec(memory_space=pltpu.SMEM)
HBM_SPEC = pl.BlockSpec(memory_space=pl.ANY)
CHEAP = pl.CostEstimate(flops=10**6, bytes_accessed=10**5, transcendentals=0)


def attend(tokens, mod, where, pieces, spots):
    rows, feat = tokens.shape
    sds = jax.ShapeDtypeStruct
    return pl.pallas_call(
        functools.partial(attend_kernel, spots),
        in_specs=[SMEM_SPEC, VMEM_SPEC, VMEM_SPEC] + [HBM_SPEC] * len(pieces),
        out_specs=[VMEM_SPEC] * 6,
        out_shape=[
            sds((rows + HEAD, feat), BF16),
            sds((rows, feat), F32),
            sds((rows, feat), F32),
            sds((rows, feat), BF16),
            sds((rows, 3 * feat), BF16),
            sds((rows, feat), BF16),
        ],
        scratch_shapes=[
            pltpu.VMEM((3 * feat, feat), BF16),
            pltpu.VMEM((feat, feat), BF16),
            pltpu.SemaphoreType.DMA,
        ],
        compiler_params=pltpu.CompilerParams(vmem_limit_bytes=40 * 2**20),
        cost_estimate=CHEAP,
    )(where, tokens, mod, *pieces)


def back_kernel(spots, blocks, where_ref, dh2_ref, grad_ref, tok_ref, mod_ref, x1_ref, projected_ref, h1_ref, qkv_ref, attn_ref, *refs):
    count = len({spot[0] for spot in spots})
    pieces = refs[:count]
    outs = refs[count:]
    tokens_out, sums_out = outs[0], outs[1]
    wq, wp, dqkv, dattn, sem = outs[-5:]
    grads = outs[2:-5]
    copies = load_weights(where_ref, pieces, spots, wq, wp, sem)
    rows, feat = tok_ref.shape
    norm_two, inverse_two = row_norm(x1_ref[...])
    dh2 = dh2_ref[...]
    d_x1 = grad_ref[...].astype(F32) + norm_back(dh2 * (1.0 + mod_ref[4:5, :]), norm_two, inverse_two)
    sums_out[3:4, :] = jnp.sum(dh2, axis=0, keepdims=True)
    sums_out[4:5, :] = jnp.sum(dh2 * norm_two, axis=0, keepdims=True)
    sums_out[2:3, :] = jnp.sum(d_x1 * projected_ref[...], axis=0, keepdims=True)
    sums_out[5:8, :] = jnp.zeros((3, feat), F32)
    dp = (mod_ref[2:3, :] * d_x1).astype(BF16)
    for copy in copies:
        copy.wait()

    def put(kind, start, size, value):
        if not blocks:
            grads[kind][start : start + size, :] = value.astype(BF16)
            return
        per = (3 * feat if kind == 0 else feat) // blocks
        base = 0 if kind == 0 else 3 * feat // blocks
        core = where_ref[0] % 2
        done = 0
        while done < size:
            block, inside = (start + done) // per, (start + done) % per
            take = min(size - done, per - inside)
            part = value[done : done + take].astype(BF16)
            for ref, same in ((grads[0], True), (grads[1], False)):

                @pl.when((core == block % 2) == same)
                def _(ref=ref, block=block, inside=inside, take=take, part=part):
                    ref[block // 2, base + inside : base + inside + take, :] = part

            done += take

    attn = attn_ref[...]
    for c in range(0, feat, 256):
        dattn[:, c : c + 256] = dot_nn(dp, wp[:, c : c + 256]).astype(BF16)
        put(1, c, 256, dot_tn(dp[:, c : c + 256], attn))
    low, high = pair_masks()
    scale = 1.0 / math.sqrt(HD)
    for c in range(0, feat, 2 * HD):
        at, at_key, at_value = pl.ds(c, 2 * HD), pl.ds(feat + c, 2 * HD), pl.ds(2 * feat + c, 2 * HD)
        query, key, value, d_out = qkv_ref[:, at], qkv_ref[:, at_key], qkv_ref[:, at_value], dattn[:, at]
        d_query, d_key, d_value = 0.0, 0.0, 0.0
        for mask in (low, high):
            probs = head_probs(query, key, mask)
            d_part = d_out * mask
            d_value = d_value + dot_tn(probs.astype(BF16), d_part)
            d_probs = dot_nt(d_part, value)
            delta = jnp.sum(probs * d_probs, axis=-1, keepdims=True)
            d_scores = (probs * (d_probs - delta)).astype(BF16)
            d_query = d_query + dot_nn(d_scores, key * mask)
            d_key = d_key + dot_tn(d_scores, query * mask)
        dqkv[:, at] = (d_query * scale).astype(BF16)
        dqkv[:, at_key] = (d_key * scale).astype(BF16)
        dqkv[:, at_value] = d_value.astype(BF16)
    h1 = h1_ref[...]
    d_all = dqkv[...]
    parts = []
    for c in range(0, feat, 256):
        parts.append(dot_nn(d_all, wq[:, c : c + 256]))
    d_h1 = jnp.concatenate(parts, axis=1)
    norm_one, inverse_one = row_norm(tok_ref[...].astype(F32))
    sums_out[0:1, :] = jnp.sum(d_h1, axis=0, keepdims=True)
    sums_out[1:2, :] = jnp.sum(d_h1 * norm_one, axis=0, keepdims=True)
    tokens_out[...] = d_x1 + norm_back(d_h1 * (1.0 + mod_ref[1:2, :]), norm_one, inverse_one)
    for c in range(0, 3 * feat, 256):
        put(0, c, 256, dot_tn(dqkv[:, c : c + 256], h1))


def attend_back(d_hid, grad_out, tokens, mod, saved, where, pieces, spots, blocks):
    rows, feat = tokens.shape
    sds = jax.ShapeDtypeStruct
    if blocks:
        shapes = [sds((blocks // 2, 4 * feat // blocks, feat), BF16)] * 2
    else:
        shapes = [sds((3 * feat, feat), BF16), sds((feat, feat), BF16)]
    return pl.pallas_call(
        functools.partial(back_kernel, spots, blocks),
        in_specs=[SMEM_SPEC] + [VMEM_SPEC] * (4 + len(saved)) + [HBM_SPEC] * len(pieces),
        out_specs=[VMEM_SPEC] * (2 + len(shapes)),
        out_shape=[sds((rows, feat), F32), sds((8, feat), F32)] + shapes,
        scratch_shapes=[
            pltpu.VMEM((3 * feat, feat), BF16),
            pltpu.VMEM((feat, feat), BF16),
            pltpu.VMEM((rows, 3 * feat), BF16),
            pltpu.VMEM((rows, feat), BF16),
            pltpu.SemaphoreType.DMA,
        ],
        compiler_params=pltpu.CompilerParams(vmem_limit_bytes=48 * 2**20),
        cost_estimate=CHEAP,
    )(where, d_hid, grad_out, tokens, mod, *saved, *pieces)


def swap(value, move):
    ndp, nz = lax.axis_size("dp"), lax.axis_size("expert")
    pairs = []
    for a in range(ndp):
        for b in range(nz):
            c, d = move(a, b)
            pairs.append((a * nz + b, c * nz + d))
    return lax.ppermute(value, AXES, pairs)


def swap_row(value):
    return swap(value, lambda a, b: (a ^ 4, b))


def swap_core(value):
    return swap(value, lambda a, b: (a ^ 1, b))


def swap_chip(value):
    return swap(value, lambda a, b: (a ^ 2, b))


def from_plane(value, step):
    nz = lax.axis_size("expert")
    return swap(value, lambda a, b: (a, (b - step) % nz))


def to_plane(value, step):
    nz = lax.axis_size("expert")
    return swap(value, lambda a, b: (a, (b + step) % nz))


def row_bits():
    return (lax.axis_size("dp") // TP).bit_length() - 1


def row_groups():
    ndp = lax.axis_size("dp")
    return [list(range(i, ndp, TP)) for i in range(TP)]


def gather_rows(value):
    return lax.all_gather(value, "dp", axis_index_groups=row_groups())


def reduce_rows(value):
    flat = value.astype(BF16).reshape(-1, value.shape[-1])
    flat = lax.psum_scatter(flat, "dp", tiled=True, axis_index_groups=row_groups())
    return flat.reshape(value.shape[1:])


def tie(*values):
    return lax.optimization_barrier(values)


def plane_steps():
    nz = lax.axis_size("expert")
    return sorted(range(1, nz), key=lambda step: (min(step, nz - step), step))


def gather_planes(block):
    return [block] + [from_plane(block, step) for step in plane_steps()]


def run_mixture(planes, early, weights, shared, first, send_shared):
    steps = plane_steps()
    rows = SEQ + HEAD
    far, near = jnp.stack(planes[2:]), jnp.stack(planes[:2])
    far_core = swap_core(far)
    near, far_core = tie(near, far_core)
    near_core = swap_core(near)
    far_sums, near_sums, done, shared_grads = None, None, [], None
    for i, (ups, downs) in enumerate(weights):
        name = jnp.stack([first[0] + i, first[1]]).astype(jnp.int32)
        both = shared if i == 0 else None
        following = weights[i + 1] if i + 1 < len(weights) else None
        split = following is not None and len(following[0]) == 3
        outs = mix(name, (far, far_core), early, 1, ups, downs, both, far_sums, None, following is None)
        if i == 0:
            near_core, *outs = tie(near_core, *outs)
        if following is None:
            shared_grads[1], *outs = tie(shared_grads[1], *outs)
        if split:
            up, down = following
            up[1], up[2], down[1], down[2], *outs = tie(*up[1:], *down[1:], *outs)
            up.append(swap_chip(up[2]))
            down.append(swap_row(down[1]))
        far_sums, grads = list(outs[:4]), list(outs[4:])
        if following is None:
            total = far_sums[0].astype(F32) + swap_core(far_sums[2]).astype(F32)
            sent = [total[j].astype(BF16) for j in range(2)]
            *sent, near = tie(*sent, near)
            moved = [to_plane(part, step) for part, step in zip(sent, steps[1:])]
        final = following is None
        outs = list(mix(name, (near, near_core), early, 0, ups, downs, both, near_sums, grads, final))
        if split:
            up[3], down[3], *outs = tie(up[3], down[3], *outs)
        if following is None:
            moved[0], moved[1], *outs = tie(*moved, *outs)
        near_sums, grads = list(outs[:4]), list(outs[4:])
        done.append(grads[0])
        if i == 0:
            shared_grads = send_shared(*grads[1:])
    dx = near_sums[0].astype(F32) + swap_core(near_sums[2]).astype(F32)
    dx_sent, far_sums[3], near_sums[3] = tie(dx[1].astype(BF16), far_sums[3], near_sums[3])
    dx_moved = to_plane(dx_sent, steps[0])
    d_hid = dx[0]
    for part in moved:
        d_hid = d_hid + part.astype(F32)
    far = far_sums[1].astype(F32) + swap_core(far_sums[3]).astype(F32)
    near = near_sums[1].astype(F32) + swap_core(near_sums[3]).astype(F32)
    y_sent = [near[1].astype(BF16)] + [far[j].astype(BF16) for j in range(2)]
    dx_moved, *y_sent = tie(dx_moved, *y_sent)
    return d_hid + dx_moved.astype(F32), near[0], y_sent, done, shared_grads


def fold_bit(part, axis, bit):
    send, keep = halves_of(part, axis, bit)
    return keep, swap_bit(send, bit)


def halves_of(part, axis, bit):
    at = (lax.axis_index("dp") >> bit) & 1
    send = lax.dynamic_index_in_dim(part, 1 - at, axis, False).astype(BF16)
    return send, lax.dynamic_index_in_dim(part, at, axis, False)


def swap_bit(value, bit):
    return swap(value, lambda a, b: (a ^ (1 << bit), b))


def add(pair):
    return pair[0].astype(F32) + pair[1].astype(F32)


def scatter_planes(part, split):
    nz = lax.axis_size("expert")
    z = lax.axis_index("expert")
    cut_q = split * nz
    cut_p = (part.shape[0] - cut_q) // nz

    def rows_of(plane):
        return jnp.concatenate(
            [
                lax.dynamic_slice_in_dim(part, plane * split, split, 0),
                lax.dynamic_slice_in_dim(part, cut_q + plane * cut_p, cut_p, 0),
            ]
        )

    moved = [to_plane(rows_of((z + step) % nz).astype(BF16), step) for step in range(1, nz)]
    return rows_of(z), moved


def two_parts(value):
    high = value.astype(BF16)
    return high, (value - high.astype(F32)).astype(BF16)


def local(
    tokens,
    timestep,
    labels,
    routes,
    expert_gates,
    grad_out,
    ada_weight,
    ada_bias,
    qkv_weight,
    proj_weight,
    shared_up,
    shared_down,
    expert_up,
    expert_down,
    time_table,
    class_table,
):
    rows, feat = tokens.shape
    ndp, nz = lax.axis_size("dp"), lax.axis_size("expert")
    reps = ndp // TP
    ndev = ndp * nz
    members = TP * nz
    local_experts = expert_up.shape[0]
    wide = expert_up.shape[2]
    down_cols = expert_down.shape[2]
    shared_wide = shared_up.shape[1]
    shared_cols = shared_down.shape[1]
    qkv_cols = qkv_weight.shape[1]
    proj_cols = proj_weight.shape[1]
    table_cols = time_table.shape[1]
    plane = lax.axis_index("expert")

    def exchange(value):
        return lax.all_to_all(value, AXES, 0, 0, tiled=True)

    if reps == 4 and wide % 128 == 0 and 2 * wide == feat:
        tail = shared_up.T
        tail = jnp.concatenate([tail[:, :wide], tail[:, wide:]])
    else:
        tail = shared_up.T[:, :wide]
    ups = [expert_up[e] for e in range(local_experts)]
    ups[0] = jnp.concatenate([ups[0], tail])
    flipped = expert_down.transpose(0, 2, 1)
    halves = [
        jnp.concatenate(
            [flipped[:, :, (i * TP + t) * wide : (i * TP + t + 1) * wide] for i in range(reps)],
            axis=2,
        )
        for t in range(TP)
    ]
    core_low = lax.axis_index("dp") % TP == 0
    mine = jnp.where(core_low, halves[0], halves[1])
    moved = swap_core(jnp.where(core_low, halves[1], halves[0]))
    downs = jnp.where(
        core_low, jnp.concatenate([mine, moved], axis=1), jnp.concatenate([moved, mine], axis=1)
    )
    sdowns = shared_down.T.reshape(shared_cols, reps, TP, nz, shared_wide)
    sdowns = sdowns.transpose(2, 3, 0, 1, 4).reshape(1, members, shared_cols, reps * shared_wide)
    sdowns = jnp.broadcast_to(sdowns, (reps,) + sdowns.shape[1:])
    sdowns = sdowns.reshape(ndev, shared_cols, reps * shared_wide)
    gate_high, gate_low = two_parts(expert_gates)
    meta = jnp.stack(
        [
            routes[:, 0].astype(BF16),
            routes[:, 1].astype(BF16),
            gate_high[:, 0],
            gate_high[:, 1],
            gate_low[:, 0],
            gate_low[:, 1],
        ]
    )
    meta = jnp.pad(meta.reshape(-1, feat), ((0, HEAD - meta.size // feat), (0, 0)))
    early = jnp.concatenate([grad_out, meta])

    early_planes = lax.all_gather(early, "expert")
    order = (plane + jnp.array([0] + plane_steps(), jnp.int32)) % nz
    early_planes = jnp.take(early_planes, order, axis=0, mode="clip")
    early_core = swap_core(early_planes)

    pair = jnp.concatenate([qkv_weight.T, proj_weight.T])
    rq, rp = nz * qkv_cols, nz * proj_cols
    packed = ndp == 8 and rq % 16 == 0 and rp % 16 == 0
    ids = jnp.concatenate([timestep, labels])[None]
    all_ids = exchange(jnp.broadcast_to(ids, (ndev, 2)))
    if packed:
        line = jnp.stack([pair] + [from_plane(pair, step) for step in range(1, nz)])
        order = (jnp.arange(nz, dtype=jnp.int32) - plane) % nz
        line = jnp.take(line, order, axis=0, mode="clip")
        line = jnp.concatenate(
            [line[:, :qkv_cols].reshape(rq, feat), line[:, qkv_cols:].reshape(rp, feat)]
        )
        half = feat // 2
        left, right = line[None, :, :half], line[None, :, half:]
        left_x, right_y = swap_chip(left), swap_row(right)
    pick_time = all_ids[:, :1] == jnp.arange(time_table.shape[0], dtype=jnp.int32)[None]
    pick_class = all_ids[:, 1:] == jnp.arange(class_table.shape[0], dtype=jnp.int32)[None]
    cond_cols = dot_nn(pick_time.astype(BF16), time_table) + dot_nn(
        pick_class.astype(BF16), class_table
    )
    cond_all = exchange(jnp.broadcast_to(cond_cols[None], (ndev, ndev, table_cols)))
    downs, cond_all = tie(downs, cond_all)
    downs = [downs[e] for e in range(local_experts)]
    if packed:
        left_x, right_y, cond_all = tie(left_x, right_y, cond_all)
        left_x, right_y = jnp.concatenate([left, left_x]), jnp.concatenate([right, right_y])
        left_y, right_x = swap_row(left_x), swap_chip(right_y)
        left_core, right_core = swap_core(left_x), swap_core(right_y)
    cond_all = cond_all.transpose(1, 0, 2).reshape(ndev, feat)
    silu_all = jax.nn.silu(cond_all).astype(BF16)
    my_index = lax.axis_index(AXES)
    cond_own = lax.dynamic_slice_in_dim(cond_all, my_index, 1, 0)
    mod_cols = dot_nn(silu_all, ada_weight) + ada_bias.astype(F32)[None]
    mod = exchange(mod_cols).reshape(6, feat)
    if packed:
        sdowns, mod = tie(sdowns, mod)
        sdown_t = exchange(sdowns).reshape(feat, reps * shared_wide)
        pieces = [left_x, left_y, left_core, swap_core(left_y)]
        pieces += [right_y, right_x, right_core, swap_core(right_x)]
        mine = lax.axis_index("dp")
        moves = [0, 2, 4, 6, 1, 3, 5, 7]
        where = jnp.stack([mine ^ m for m in moves]).astype(jnp.int32)
        spots = (
            (0, (0, 1), 0),
            (1, (2, 3), 0),
            (2, (4, 5), 0),
            (3, (6, 7), 0),
            (4, (0, 2), half),
            (5, (1, 3), half),
            (6, (4, 6), half),
            (7, (5, 7), half),
        )
        blocks = ndp
    else:
        pair = lax.all_gather(pair, AXES)
        pieces = [
            jnp.concatenate(
                [
                    pair[:, :qkv_cols].reshape(ndev * qkv_cols, feat),
                    pair[:, qkv_cols:].reshape(ndev * proj_cols, feat),
                ]
            )[None]
        ]
        where = jnp.zeros((1,), jnp.int32)
        spots = ((0, (0,), 0),)
        blocks = 0

    if packed:
        weights = []
        for e in range(local_experts):
            up, down = ups[e], downs[e]
            if e:
                up, down, weights[-1][0][1] = tie(up, down, weights[-1][0][1])
            else:
                up, down, mod = tie(up, down, mod)
            up = [up, swap_chip(up), swap_row(up)]
            down = [down, swap_chip(down), swap_row(down)]
            weights.append([up, down])
        shared = [sdown_t]
        place = lax.axis_index("dp") // TP

    mod_rows = jnp.concatenate([mod, jnp.zeros((2, feat), F32)])
    late, *saved_attn = attend(tokens, mod_rows, where, pieces, spots)
    middle = saved_attn[0]

    if packed:
        up, down = weights[0]
        late, up[2], down[1] = tie(late, up[2], down[1])
        up.append(swap_chip(up[2]))
        down.append(swap_row(down[1]))
    planes = gather_planes(late)
    if packed:
        *planes, sdown_t, up[1], up[3], down[2], down[3] = tie(
            *planes, sdown_t, up[1], up[3], down[2], down[3]
        )
        shared = [sdown_t]
    if not packed:
        place = jnp.zeros((), jnp.int32)
        weights = []
        for e in range(local_experts):
            up = gather_rows(ups[e][:feat]).transpose(1, 0, 2).reshape(feat, reps * wide)
            weights.append([[up], [gather_rows(downs[e]).reshape(feat, reps * wide)]])
        sup_t = gather_rows(shared_up.T).reshape(reps * shared_wide, feat)
        shared = [exchange(sdowns).reshape(feat, reps * shared_wide), sup_t]

    first = jnp.stack([plane * local_experts, place]).astype(jnp.int32)
    early = (early_planes, early_core)
    def send_shared(g_sup, g_sdown):
        g_sup = g_sup.reshape(reps, shared_wide, feat)
        g_sdown = g_sdown.reshape(ndev, shared_cols, reps * shared_wide)
        return [g_sup, exchange(g_sdown)]

    d_normed_two, branch, y_sent, done, shared_grads = run_mixture(
        planes, early, weights, shared, first, send_shared
    )
    d_normed_two, d_gate_two = d_normed_two[:rows], d_normed_two[rows : rows + 1]

    g_sup, g_sdown = shared_grads
    reduced = []
    for g_mix in done:
        if g_mix.shape[0] == 1:
            g_up = g_mix[0, 0].reshape(feat, reps, wide).transpose(1, 0, 2)
            g_down = g_mix[0, 1].reshape(reps, TP * down_cols, reps, wide).transpose(0, 2, 1, 3)
            g_mix = jnp.stack([g_up, g_down.reshape(reps, feat, wide)], axis=1)
        reduced.append(reduce_rows(g_mix))

    def finish_expert(pair):
        g_up, g_down = pair[0].astype(F32), pair[1].reshape(reps, TP, down_cols, wide)
        kept = jnp.where(core_low, g_down[:, 0], g_down[:, 1])
        got = swap_core(jnp.where(core_low, g_down[:, 1], g_down[:, 0]))
        g_down = [jnp.where(core_low, kept, got), jnp.where(core_low, got, kept)]
        g_down = jnp.concatenate([g_down[t][i] for i in range(reps) for t in range(TP)], axis=1)
        return g_up, g_down.T.astype(F32)

    up_part, down_part = [], []
    for pair in reduced[:-1]:
        g_up, g_down = finish_expert(pair)
        g_up, g_down, d_normed_two = tie(g_up, g_down, d_normed_two)
        up_part.append(g_up)
        down_part.append(g_down)

    tokens_grad, sums, *g_small = attend_back(
        d_normed_two, grad_out, tokens, mod_rows, saved_attn, where, pieces, spots, blocks
    )
    y_moved = [to_plane(part, step) for part, step in zip(y_sent[:2], plane_steps())]
    *y_moved, tokens_grad, sums, g_small[0], g_small[1] = tie(
        *y_moved, tokens_grad, sums, *g_small
    )
    d_mod = jnp.concatenate([sums[0:5], d_gate_two]).astype(BF16).reshape(ndev, -1)
    d_mod = exchange(d_mod)
    if packed:
        half = feat // 2
        kept, got = g_small[0], swap_core(g_small[1])
        d_mod, kept, got = tie(d_mod, kept, got)
        g_small = add((kept, got)).reshape((2, 2) + kept.shape[1:])
        left, right = halves_of(g_small[..., :half], 1, 1), halves_of(g_small[..., half:], 0, 2)
        left_sent, right_sent, d_mod = tie(left[0], right[0], d_mod)
        right_sent, y_sent[2] = tie(right_sent, y_sent[2])
        left, right = [left[1], swap_bit(left_sent, 1)], [right[1], swap_bit(right_sent, 2)]
        reduced[-1], left[1], right[1], d_mod = tie(reduced[-1], left[1], right[1], d_mod)
    else:
        g_small = jnp.concatenate(
            [g_small[0].reshape(ndev, qkv_cols, feat), g_small[1].reshape(ndev, proj_cols, feat)],
            axis=1,
        )
        g_small = lax.psum_scatter(g_small, AXES).astype(F32)
    reduced[-1], g_sup = tie(reduced[-1], g_sup)
    sup_part = reduce_rows(g_sup).T.astype(F32)
    y_moved.append(to_plane(y_sent[2], plane_steps()[2]))
    d_cond = dot_nt(d_mod, ada_weight)
    d_cond_cols = d_cond.reshape(ndev, ndev, table_cols).transpose(1, 0, 2).reshape(ndev, -1)
    d_cond = jnp.concatenate([d_cond, d_cond_cols], axis=1)
    if packed:
        left, right = list(fold_bit(add(left), 0, 2)), list(fold_bit(add(right), 0, 1))
        left[1], right[1], d_cond, *y_moved = tie(left[1], right[1], d_cond, *y_moved)
    d_cond = exchange(d_cond)
    last_up, last_down = finish_expert(reduced[-1])
    if packed:
        left, right, last_up, last_down = tie(add(left), add(right), last_up, last_down)
        g_small, g_moved = scatter_planes(jnp.concatenate([left, right], axis=-1), qkv_cols)
    else:
        g_moved = []
    d_cond, g_sdown, *y_moved = tie(d_cond, g_sdown, *y_moved)
    up_part = jnp.stack(up_part + [last_up])
    down_part = jnp.stack(down_part + [last_down])
    for part in y_moved:
        branch = branch + part.astype(F32)
    gates_grad = branch[rows, : 2 * rows].reshape(2, rows).T
    block_out = (middle + mod[5:6] * branch[:rows]).astype(BF16)
    d_cond = jnp.sum(d_cond, axis=0, keepdims=True)
    cond_grad = local_grad(jax.nn.silu, cond_own, d_cond[:, :feat])
    d_cond_cols = d_cond[:, feat:].reshape(ndev, table_cols)
    d_cond_cols = local_grad(jax.nn.silu, cond_cols, d_cond_cols)
    ada_part = dot_tn(silu_all, d_mod)
    bias_part = jnp.sum(d_mod.astype(F32), axis=0)
    g_sdown = g_sdown.reshape(reps, members, shared_cols, reps, shared_wide)
    g_sdown = jnp.sum(g_sdown.astype(F32), axis=0)
    sdown_part = g_sdown.transpose(2, 0, 3, 1).reshape(reps * members * shared_wide, shared_cols)

    def table_grad(pick):
        return lax.dot_general(
            pick.astype(F32),
            d_cond_cols,
            (((0,), (0,)), ((), ())),
            precision=lax.Precision.HIGHEST,
            preferred_element_type=F32,
        )

    time_part, class_part = table_grad(pick_time), table_grad(pick_class)

    outs = [block_out, cond_grad, gates_grad, ada_part, bias_part, sup_part, sdown_part]
    outs += [up_part, down_part, time_part, class_part]
    if g_moved:
        *g_moved, outs = lax.optimization_barrier((*g_moved, outs))
    block_out, cond_grad, gates_grad, ada_part, bias_part, sup_part, sdown_part = outs[:7]
    up_part, down_part, time_part, class_part = outs[7:]
    for part in g_moved:
        g_small = g_small + part.astype(F32)
    qkv_part = g_small[:qkv_cols].T
    proj_part = g_small[qkv_cols:].T
    return (
        block_out,
        tokens_grad,
        cond_grad,
        gates_grad,
        ada_part,
        bias_part,
        qkv_part,
        proj_part,
        sup_part,
        sdown_part,
        up_part,
        down_part,
        time_part,
        class_part,
    )


def solution(mesh):
    both = ("dp", "expert")
    by_rows, by_cols, by_first = P(both, None), P(None, both), P(both)
    by_expert = P("expert", None, "dp")
    return jax.shard_map(
        local,
        mesh=mesh,
        in_specs=(
            by_rows,
            by_first,
            by_first,
            by_rows,
            by_rows,
            by_rows,
            by_cols,
            by_first,
            by_cols,
            by_cols,
            by_cols,
            by_cols,
            by_expert,
            by_expert,
            by_cols,
            by_cols,
        ),
        out_specs=(
            by_rows,
            by_rows,
            by_rows,
            by_rows,
            by_cols,
            by_first,
            by_cols,
            by_cols,
            by_cols,
            by_cols,
            by_expert,
            by_expert,
            by_cols,
            by_cols,
        ),
        check_vma=False,
    )
```

```python
import functools
import math

import jax
import jax.numpy as jnp
from jax import lax
from jax.experimental import pallas as pl
from jax.experimental.pallas import tpu as pltpu
from jax.sharding import PartitionSpec as P

H = 12
HD = 64
SEQ = 256
CAP = 128
TP = 2
AXES = ("dp", "expert")
F32 = jnp.float32
BF16 = jnp.bfloat16

HEAD = 16
BLOCKS = 4
GELU_A = math.sqrt(2.0 / math.pi)
GELU_B = 0.044715


def gelu_both(x):
    square = x * x
    t = jnp.tanh(GELU_A * x * (1.0 + GELU_B * square))
    half = 0.5 * (1.0 + t)
    slope = half + 0.5 * x * (1.0 - t * t) * (GELU_A + 3.0 * GELU_A * GELU_B * square)
    return x * half, slope


def mix_kernel(count, shared, more, before, final, first_ref, h_own, h_core, g_own, g_core, *refs):
    refs = list(refs)

    def take(number):
        taken = refs[:number]
        del refs[:number]
        return taken

    ups, downs = take(count), take(count)
    if shared:
        (sdown_ref,) = take(1)
        if count == 1:
            (sup_in,) = take(1)
    if more:
        sums_in = take(4)
    if before:
        (grads_in,) = take(1)
        if shared:
            gsup_in, gsdown_in = take(2)
    sums_out = take(4)
    (grads,) = take(1)
    if shared:
        gsup, gsdown = take(2)
    rows_ref, act_ref, dpre_ref, dy_ref, hid_ref, ds_ref, meta, acc_y, acc_d, gg_acc = take(10)
    up_ref, down_ref, sup_ref, old_ref, new_ref, *sums, sems = refs
    (keep_d, keep_y, send_d, send_y) = sums
    seq, feat = SEQ, h_own.shape[2]
    step = 256
    wide = up_ref.shape[1]
    blocks, part = new_ref.shape[0], new_ref.shape[3]

    copies = []
    if count == 1:
        copies.append(pltpu.make_async_copy(ups[0], up_ref, sems.at[0]))
        copies.append(pltpu.make_async_copy(downs[0], down_ref, sems.at[0]))
        if shared:
            copies.append(pltpu.make_async_copy(sup_in, sup_ref, sems.at[0]))
    else:
        per, swide = feat // count, sup_ref.shape[0] // count
        for i in range(count):
            place = first_ref[1] ^ i
            lanes = pl.ds(pl.multiple_of(place * part, 128), part)
            copies.append(
                pltpu.make_async_copy(ups[i].at[pl.ds(0, feat), :], up_ref.at[:, lanes], sems.at[0])
            )
            at = pl.ds(pl.multiple_of(place * per, 16), per)
            copies.append(pltpu.make_async_copy(downs[i], down_ref.at[at, :], sems.at[0]))
            if shared:
                at = pl.ds(pl.multiple_of(place * swide, 16), swide)
                for j in range(2):
                    copies.append(
                        pltpu.make_async_copy(
                            ups[i].at[pl.ds(feat + j * swide, swide), :],
                            sup_ref.at[at, pl.ds(j * part, part)],
                            sems.at[0],
                        )
                    )
    for copy in copies:
        copy.start()
    if more:
        came_copies = [pltpu.make_async_copy(a, b, sems.at[4]) for a, b in zip(sums_in, sums)]
        for copy in came_copies:
            copy.start()
    if before:
        old = pltpu.make_async_copy(grads_in, old_ref, sems.at[1])
        old.start()

    hs = [h_own.at[0], h_own.at[1], h_core.at[0], h_core.at[1]]
    gs = [g_own.at[0], g_own.at[1], g_core.at[0], g_core.at[1]]
    half = BLOCKS // 2
    for b in range(BLOCKS):
        hid_ref[b] = hs[b][0:seq, :]
        tail = hs[b][seq : seq + HEAD, :].astype(F32)
        gate_two = tail[0:1] + tail[1:2]
        ds_ref[b] = (gate_two * gs[b][0:seq, :].astype(F32)).astype(BF16)
        meta[b] = gs[b][seq : seq + HEAD, :].astype(F32)

    name = first_ref[0].astype(F32)
    up_down = lax.broadcasted_iota(jnp.int32, (seq, seq), 0) <= lax.broadcasted_iota(
        jnp.int32, (seq, seq), 1
    )
    ones_tri = up_down.astype(F32).astype(BF16)
    slot = lax.broadcasted_iota(jnp.int32, (CAP, seq), 0).astype(F32)
    selects, back, gates = [], [], []
    for b in range(BLOCKS):
        m = meta[b]
        in0 = (m[0:1, 0:seq] == name).astype(F32)
        in1 = (m[0:1, seq : 2 * seq] == name).astype(F32)
        gate = in0 * (m[0:1, 2 * seq : 3 * seq] + m[1:2, seq : 2 * seq]) + in1 * (
            m[1:2, 0:seq] + m[1:2, 2 * seq : 3 * seq]
        )
        has = in0 + in1
        count_row = dot_nn(jnp.broadcast_to(has, (16, seq)).astype(BF16), ones_tri)[0:1]
        select = (count_row * has - 1.0 == slot).astype(F32)
        gates.append(jnp.sum(select * gate, axis=1, keepdims=True))
        back.append(select.T.astype(BF16))
        select = select.astype(BF16)
        selects.append(select)
        at = pl.ds(b * CAP, CAP)
        rows_ref[at, :] = dot_nn(select, hid_ref[b]).astype(BF16)
        dy_ref[at, :] = (gates[b] * dot_nn(select, ds_ref[b])).astype(BF16)

    for copy in copies:
        copy.wait()
    rows, dy = rows_ref[...], dy_ref[...]
    for c in range(0, wide, step):
        at = pl.ds(c, step)
        act, slope = gelu_both(dot_nn(rows, up_ref[:, at]))
        act_ref[:, at] = act.astype(BF16)
        dpre_ref[:, at] = (slope * dot_nn(dy, down_ref[:, at])).astype(BF16)
    act, dpre = act_ref[...], dpre_ref[...]
    if more:
        for copy in came_copies:
            copy.wait()
    for b in range(BLOCKS):
        if more:
            came_d, came_y = (keep_d, keep_y) if b < half else (send_d, send_y)
            acc_d[b] = came_d[b % half, 0:seq, :].astype(F32)
            acc_y[b] = came_y[b % half, 0:seq, :].astype(F32)
            gg_acc[b] = came_y[b % half, seq : seq + HEAD, :].astype(F32)
        else:
            acc_d[b] = jnp.zeros((seq, feat), F32)
            acc_y[b] = jnp.zeros((seq, feat), F32)
            gg_acc[b] = jnp.zeros((HEAD, feat), F32)
    gg = [jnp.zeros((CAP, 1), F32)] * BLOCKS
    for c in range(0, feat, step):
        at = pl.ds(c, step)
        res = dot_nt(act, down_ref[at, :])
        dx = dot_nt(dpre, up_ref[at, :]).astype(BF16)
        for b in range(BLOCKS):
            value = res[b * CAP : (b + 1) * CAP]
            slots = pl.ds(b * CAP, CAP)
            gg[b] = gg[b] + jnp.sum(value * dy_ref[slots, at].astype(F32), axis=1, keepdims=True)
            acc_y[b, :, at] += dot_nn(back[b], (gates[b] * value).astype(BF16))
            acc_d[b, :, at] += dot_nn(back[b], dx[b * CAP : (b + 1) * CAP])
    for b in range(BLOCKS):
        m = meta[b]
        inverse = jnp.where(gates[b] > 0.0, 1.0 / jnp.where(gates[b] > 0.0, gates[b], 1.0), 0.0)
        token = jnp.sum(selects[b].astype(F32) * (gg[b] * inverse), axis=0, keepdims=True)
        in0 = (m[0:1, 0:seq] == name).astype(F32)
        in1 = (m[0:1, seq : 2 * seq] == name).astype(F32)
        gg_acc[b, 0:1, 0:seq] += in0 * token
        gg_acc[b, 0:1, seq : 2 * seq] += in1 * token

    if shared:
        hid = hid_ref[...].reshape(BLOCKS * seq, feat)
        ds = ds_ref[...].reshape(BLOCKS * seq, feat)
        act_s, slope = gelu_both(dot_nt(hid, sup_ref[...]))
        act_s = act_s.astype(BF16)
        dpre_s = (slope * dot_nn(ds, sdown_ref[...])).astype(BF16)
        g_one, g_two = dot_tn(dpre_s, hid), dot_tn(ds, act_s)
        if before:
            g_one, g_two = g_one + gsup_in[...], g_two + gsdown_in[...]
        gsup[...] = g_one.astype(gsup.dtype)
        gsdown[...] = g_two.astype(gsdown.dtype)
        for c in range(0, feat, step):
            at = pl.ds(c, step)
            acc_y[:, :, at] += dot_nt(act_s, sdown_ref[at, :]).reshape(BLOCKS, seq, step)
            acc_d[:, :, at] += dot_nn(dpre_s, sup_ref[:, at]).reshape(BLOCKS, seq, step)
    for b in range(BLOCKS):
        out_d, out_y = (keep_d, keep_y) if b < half else (send_d, send_y)
        out_d[b % half, 0:seq, :] = acc_d[b].astype(BF16)
        gate_sum = jnp.zeros((HEAD, feat), F32)
        if final:
            gate_sum = jnp.sum(gs[b][0:seq, :].astype(F32) * acc_y[b], axis=0, keepdims=True)
            gate_sum = jnp.broadcast_to(gate_sum, (HEAD, feat))
        out_d[b % half, seq : seq + HEAD, :] = gate_sum.astype(BF16)
        out_y[b % half, 0:seq, :] = acc_y[b].astype(BF16)
        out_y[b % half, seq : seq + HEAD, :] = gg_acc[b].astype(BF16)

    sum_copies = [pltpu.make_async_copy(a, b, sems.at[5]) for a, b in zip(sums, sums_out)]
    for copy in sum_copies:
        copy.start()
    if before:
        old.wait()
    per = feat // blocks

    def put(i, kind, start, value):
        at = pl.ds(start, value.shape[0])
        if before:
            value = value + old_ref[i, kind, at, :].astype(F32)
        new_ref[i, kind, at, :] = value.astype(BF16)

    for c in range(0, feat, step):
        total = dot_tn(rows_ref[:, c : c + step], dpre)
        for i in range(blocks):
            put(i, 0, c, total[:, i * part : (i + 1) * part])
    first_out = pltpu.make_async_copy(new_ref.at[:, 0], grads.at[:, 0], sems.at[2])
    first_out.start()
    chunk = 2 * per if blocks > 1 else step
    for c in range(0, feat, chunk):
        total = dot_tn(dy_ref[:, c : c + chunk], act)
        if blocks == 1:
            put(0, 1, c, total)
            continue
        for i in range(2):
            for q in range(blocks):
                value = total[i * per : (i + 1) * per, q * part : (q + 1) * part]
                put(c // per + i, 1, q * per, value)
    second_out = pltpu.make_async_copy(new_ref.at[:, 1], grads.at[:, 1], sems.at[3])
    second_out.start()
    first_out.wait()
    second_out.wait()
    for copy in sum_copies:
        copy.wait()


def mix(first, hid, grads, block, ups, downs, shared, more, before, final):
    full, feat = hid[0].shape[1:]
    rows = full - HEAD
    count = len(ups)
    half, total = BLOCKS // 2, BLOCKS * CAP
    wide = downs[0].shape[-1]
    blocks = count
    part = wide // blocks
    sds = jax.ShapeDtypeStruct
    given = [*hid, *grads, *ups, *downs]
    pair = lambda at: pl.BlockSpec((half, full, feat), lambda i: (at, 0, 0))
    specs = [pair(0), pair(0), pair(block), pair(block)] + [HBM_SPEC] * (2 * count)
    outs = [sds((half, full, feat), BF16)] * 4 + [sds((blocks, 2, feat, part), BF16)]
    out_specs = [HBM_SPEC] * 5
    swide = 16 * count
    if shared is not None:
        swide = shared[0].shape[1]
        given += shared
        specs += [VMEM_SPEC] + [HBM_SPEC] * (len(shared) - 1)
        kind = F32 if before is None else BF16
        outs += [sds((swide, feat), kind), sds((feat, swide), kind)]
        out_specs += [VMEM_SPEC] * 2
    if more is not None:
        given += more
        specs += [HBM_SPEC] * 4
    if before is not None:
        given += before
        specs += [HBM_SPEC] + [VMEM_SPEC] * (len(before) - 1)
    old_shape = (blocks, 2, feat, part) if before is not None else (1, 1, 16, 128)
    return pl.pallas_call(
        functools.partial(
            mix_kernel, count, shared is not None, more is not None, before is not None, final
        ),
        grid=(1,),
        in_specs=[SMEM_SPEC] + specs,
        out_specs=out_specs,
        out_shape=outs,
        scratch_shapes=[
            pltpu.VMEM((total, feat), BF16),
            pltpu.VMEM((total, wide), BF16),
            pltpu.VMEM((total, wide), BF16),
            pltpu.VMEM((total, feat), BF16),
            pltpu.VMEM((BLOCKS, rows, feat), BF16),
            pltpu.VMEM((BLOCKS, rows, feat), BF16),
            pltpu.VMEM((BLOCKS, HEAD, feat), F32),
            pltpu.VMEM((BLOCKS, rows, feat), F32),
            pltpu.VMEM((BLOCKS, rows, feat), F32),
            pltpu.VMEM((BLOCKS, HEAD, feat), F32),
            pltpu.VMEM((feat, wide), BF16),
            pltpu.VMEM((feat, wide), BF16),
            pltpu.VMEM((swide, feat), BF16),
            pltpu.VMEM(old_shape, BF16),
            pltpu.VMEM((blocks, 2, feat, part), BF16),
            pltpu.VMEM((half, full, feat), BF16),
            pltpu.VMEM((half, full, feat), BF16),
            pltpu.VMEM((half, full, feat), BF16),
            pltpu.VMEM((half, full, feat), BF16),
            pltpu.SemaphoreType.DMA((6,)),
        ],
        compiler_params=pltpu.CompilerParams(vmem_limit_bytes=58 * 2**20),
        cost_estimate=CHEAP,
    )(first, *given)


def norm_back(upstream, normed, inverse):
    mean_grad = jnp.mean(upstream, axis=-1, keepdims=True)
    mean_mix = jnp.mean(upstream * normed, axis=-1, keepdims=True)
    return inverse * (upstream - mean_grad - normed * mean_mix)


def dot_nn(left, right):
    return jnp.dot(left, right, preferred_element_type=F32)


def dot_tn(left, right):
    return lax.dot_general(left, right, (((0,), (0,)), ((), ())), preferred_element_type=F32)


def dot_nt(left, right):
    return lax.dot_general(left, right, (((1,), (1,)), ((), ())), preferred_element_type=F32)


def local_grad(function, inputs, upstream):
    unused, pull = jax.vjp(function, inputs)
    return pull(upstream)[0]


def row_norm(values):
    center = values - jnp.mean(values, axis=-1, keepdims=True)
    inverse = lax.rsqrt(jnp.mean(center * center, axis=-1, keepdims=True) + 1e-06)
    return center * inverse, inverse


def load_weights(where_ref, pieces, spots, wq, wp, sem):
    copies = []
    for ref, blocks, lane in spots:
        piece = pieces[ref]
        rq = wq.shape[0] // where_ref.shape[0]
        rp = wp.shape[0] // where_ref.shape[0]
        width = piece.shape[2]
        for j, block in enumerate(blocks):
            at = where_ref[block]
            lanes = pl.ds(lane, width)
            to_q = wq.at[pl.ds(pl.multiple_of(at * rq, 16), rq), lanes]
            to_p = wp.at[pl.ds(pl.multiple_of(at * rp, 16), rp), lanes]
            copies.append(pltpu.make_async_copy(piece.at[j, pl.ds(0, rq), :], to_q, sem))
            copies.append(pltpu.make_async_copy(piece.at[j, pl.ds(rq, rp), :], to_p, sem))
    for copy in copies:
        copy.start()
    return copies


def pair_masks():
    lane = lax.broadcasted_iota(jnp.int32, (1, 2 * HD), 1)
    return [(lane < HD).astype(F32).astype(BF16), (lane >= HD).astype(F32).astype(BF16)]


def head_probs(query, key, mask):
    scores = dot_nt(query * mask, key) * (1.0 / math.sqrt(HD))
    exp_scores = jnp.exp(scores - jnp.max(scores, axis=-1, keepdims=True))
    return exp_scores / jnp.sum(exp_scores, axis=-1, keepdims=True)


def attend_kernel(spots, where_ref, tok_ref, mod_ref, *refs):
    count = len({spot[0] for spot in spots})
    pieces = refs[:count]
    late_ref, x1_ref, projected_ref, h1_ref, qkv_ref, attn_ref, wq, wp, sem = refs[count:]
    copies = load_weights(where_ref, pieces, spots, wq, wp, sem)
    rows, feat = tok_ref.shape
    tokens = tok_ref[...].astype(F32)
    norm, unused = row_norm(tokens)
    h1_ref[...] = (norm * (1.0 + mod_ref[1:2, :]) + mod_ref[0:1, :]).astype(BF16)
    for copy in copies:
        copy.wait()
    h1 = h1_ref[...]
    for c in range(0, 3 * feat, 256):
        at = pl.ds(c, 256)
        qkv_ref[:, at] = dot_nt(h1, wq[at, :]).astype(BF16)
    low, high = pair_masks()
    for c in range(0, feat, 2 * HD):
        at = pl.ds(c, 2 * HD)
        query, key = qkv_ref[:, at], qkv_ref[:, pl.ds(feat + c, 2 * HD)]
        value = qkv_ref[:, pl.ds(2 * feat + c, 2 * HD)]
        first = head_probs(query, key, low).astype(BF16)
        second = head_probs(query, key, high).astype(BF16)
        attn_ref[:, at] = (dot_nn(first, value * low) + dot_nn(second, value * high)).astype(BF16)
    attn = attn_ref[...]
    for c in range(0, feat, 256):
        at = pl.ds(c, 256)
        projected_ref[:, at] = dot_nt(attn, wp[at, :])
    x1 = tokens + mod_ref[2:3, :] * projected_ref[...]
    x1_ref[...] = x1
    norm, unused = row_norm(x1)
    late_ref[0:rows, :] = (norm * (1.0 + mod_ref[4:5, :]) + mod_ref[3:4, :]).astype(BF16)
    gate = mod_ref[5:6, :]
    gate_high = gate.astype(BF16).astype(F32)
    line = lax.broadcasted_iota(jnp.int32, (HEAD, feat), 0)
    late_ref[rows : rows + HEAD, :] = jnp.where(
        line == 0, gate_high, jnp.where(line == 1, gate - gate_high, 0.0)
    ).astype(BF16)


VMEM_SPEC = pl.BlockSpec(memory_space=pltpu.VMEM)
SMEM_SPEC = pl.BlockSpec(memory_space=pltpu.SMEM)
HBM_SPEC = pl.BlockSpec(memory_space=pl.ANY)
CHEAP = pl.CostEstimate(flops=10**6, bytes_accessed=10**5, transcendentals=0)


def attend(tokens, mod, where, pieces, spots):
    rows, feat = tokens.shape
    sds = jax.ShapeDtypeStruct
    return pl.pallas_call(
        functools.partial(attend_kernel, spots),
        in_specs=[SMEM_SPEC, VMEM_SPEC, VMEM_SPEC] + [HBM_SPEC] * len(pieces),
        out_specs=[VMEM_SPEC] * 6,
        out_shape=[
            sds((rows + HEAD, feat), BF16),
            sds((rows, feat), F32),
            sds((rows, feat), F32),
            sds((rows, feat), BF16),
            sds((rows, 3 * feat), BF16),
            sds((rows, feat), BF16),
        ],
        scratch_shapes=[
            pltpu.VMEM((3 * feat, feat), BF16),
            pltpu.VMEM((feat, feat), BF16),
            pltpu.SemaphoreType.DMA,
        ],
        compiler_params=pltpu.CompilerParams(vmem_limit_bytes=40 * 2**20),
        cost_estimate=CHEAP,
    )(where, tokens, mod, *pieces)


def back_kernel(spots, blocks, where_ref, dh2_ref, grad_ref, tok_ref, mod_ref, x1_ref, projected_ref, h1_ref, qkv_ref, attn_ref, *refs):
    count = len({spot[0] for spot in spots})
    pieces = refs[:count]
    outs = refs[count:]
    tokens_out, sums_out = outs[0], outs[1]
    wq, wp, dqkv, dattn, g_ref, sem, sems = outs[-7:]
    grads = outs[2:-7]
    copies = load_weights(where_ref, pieces, spots, wq, wp, sem)
    rows, feat = tok_ref.shape
    norm_two, inverse_two = row_norm(x1_ref[...])
    dh2 = dh2_ref[...]
    d_x1 = grad_ref[...].astype(F32) + norm_back(dh2 * (1.0 + mod_ref[4:5, :]), norm_two, inverse_two)
    sums_out[3:4, :] = jnp.sum(dh2, axis=0, keepdims=True)
    sums_out[4:5, :] = jnp.sum(dh2 * norm_two, axis=0, keepdims=True)
    sums_out[2:3, :] = jnp.sum(d_x1 * projected_ref[...], axis=0, keepdims=True)
    sums_out[5:8, :] = jnp.zeros((3, feat), F32)
    dp = (mod_ref[2:3, :] * d_x1).astype(BF16)
    for copy in copies:
        copy.wait()

    def put(kind, start, size, value):
        if not blocks:
            grads[kind][start : start + size, :] = value.astype(BF16)
            return
        per = (3 * feat if kind == 0 else feat) // blocks
        base = 0 if kind == 0 else 3 * feat // blocks
        done = 0
        while done < size:
            block, inside = (start + done) // per, (start + done) % per
            take = min(size - done, per - inside)
            g_ref[block, base + inside : base + inside + take, :] = value[done : done + take].astype(BF16)
            done += take

    attn = attn_ref[...]
    for c in range(0, feat, 256):
        dattn[:, c : c + 256] = dot_nn(dp, wp[:, c : c + 256]).astype(BF16)
        put(1, c, 256, dot_tn(dp[:, c : c + 256], attn))
    low, high = pair_masks()
    scale = 1.0 / math.sqrt(HD)
    for c in range(0, feat, 2 * HD):
        at, at_key, at_value = pl.ds(c, 2 * HD), pl.ds(feat + c, 2 * HD), pl.ds(2 * feat + c, 2 * HD)
        query, key, value, d_out = qkv_ref[:, at], qkv_ref[:, at_key], qkv_ref[:, at_value], dattn[:, at]
        d_query, d_key, d_value = 0.0, 0.0, 0.0
        for mask in (low, high):
            probs = head_probs(query, key, mask)
            d_part = d_out * mask
            d_value = d_value + dot_tn(probs.astype(BF16), d_part)
            d_probs = dot_nt(d_part, value)
            delta = jnp.sum(probs * d_probs, axis=-1, keepdims=True)
            d_scores = (probs * (d_probs - delta)).astype(BF16)
            d_query = d_query + dot_nn(d_scores, key * mask)
            d_key = d_key + dot_tn(d_scores, query * mask)
        dqkv[:, at] = (d_query * scale).astype(BF16)
        dqkv[:, at_key] = (d_key * scale).astype(BF16)
        dqkv[:, at_value] = d_value.astype(BF16)
    h1 = h1_ref[...]
    d_all = dqkv[...]
    parts = []
    for c in range(0, feat, 256):
        parts.append(dot_nn(d_all, wq[:, c : c + 256]))
    d_h1 = jnp.concatenate(parts, axis=1)
    norm_one, inverse_one = row_norm(tok_ref[...].astype(F32))
    sums_out[0:1, :] = jnp.sum(d_h1, axis=0, keepdims=True)
    sums_out[1:2, :] = jnp.sum(d_h1 * norm_one, axis=0, keepdims=True)
    tokens_out[...] = d_x1 + norm_back(d_h1 * (1.0 + mod_ref[1:2, :]), norm_one, inverse_one)
    for c in range(0, 3 * feat, 256):
        put(0, c, 256, dot_tn(dqkv[:, c : c + 256], h1))
    core = where_ref[0] % 2

    def blocks_out(action):
        for block in range(blocks):
            for ref, same in ((grads[0], True), (grads[1], False)):

                @pl.when((core == block % 2) == same)
                def _(ref=ref, block=block):
                    copy = pltpu.make_async_copy(g_ref.at[block], ref.at[block // 2], sems.at[block])
                    copy.start() if action == "start" else copy.wait()

    if blocks:
        blocks_out("start")
        blocks_out("wait")


def attend_back(d_hid, grad_out, tokens, mod, saved, where, pieces, spots, blocks):
    rows, feat = tokens.shape
    sds = jax.ShapeDtypeStruct
    if blocks:
        shapes = [sds((blocks // 2, 4 * feat // blocks, feat), BF16)] * 2
    else:
        shapes = [sds((3 * feat, feat), BF16), sds((feat, feat), BF16)]
    return pl.pallas_call(
        functools.partial(back_kernel, spots, blocks),
        in_specs=[SMEM_SPEC] + [VMEM_SPEC] * (4 + len(saved)) + [HBM_SPEC] * len(pieces),
        out_specs=[VMEM_SPEC] * 2 + [HBM_SPEC if blocks else VMEM_SPEC] * 2,
        out_shape=[sds((rows, feat), F32), sds((8, feat), F32)] + shapes,
        scratch_shapes=[
            pltpu.VMEM((3 * feat, feat), BF16),
            pltpu.VMEM((feat, feat), BF16),
            pltpu.VMEM((rows, 3 * feat), BF16),
            pltpu.VMEM((rows, feat), BF16),
            pltpu.VMEM((blocks, 4 * feat // blocks, feat) if blocks else (1, 16, 128), BF16),
            pltpu.SemaphoreType.DMA,
            pltpu.SemaphoreType.DMA((max(1, blocks),)),
        ],
        compiler_params=pltpu.CompilerParams(vmem_limit_bytes=48 * 2**20),
        cost_estimate=CHEAP,
    )(where, d_hid, grad_out, tokens, mod, *saved, *pieces)


def swap(value, move):
    ndp, nz = lax.axis_size("dp"), lax.axis_size("expert")
    pairs = []
    for a in range(ndp):
        for b in range(nz):
            c, d = move(a, b)
            pairs.append((a * nz + b, c * nz + d))
    return lax.ppermute(value, AXES, pairs)


def swap_row(value):
    return swap(value, lambda a, b: (a ^ 4, b))


def swap_core(value):
    return swap(value, lambda a, b: (a ^ 1, b))


def swap_chip(value):
    return swap(value, lambda a, b: (a ^ 2, b))


def from_plane(value, step):
    nz = lax.axis_size("expert")
    return swap(value, lambda a, b: (a, (b - step) % nz))


def to_plane(value, step):
    nz = lax.axis_size("expert")
    return swap(value, lambda a, b: (a, (b + step) % nz))


def row_bits():
    return (lax.axis_size("dp") // TP).bit_length() - 1


def row_groups():
    ndp = lax.axis_size("dp")
    return [list(range(i, ndp, TP)) for i in range(TP)]


def gather_rows(value):
    return lax.all_gather(value, "dp", axis_index_groups=row_groups())


def reduce_rows(value):
    flat = value.astype(BF16).reshape(-1, value.shape[-1])
    flat = lax.psum_scatter(flat, "dp", tiled=True, axis_index_groups=row_groups())
    return flat.reshape(value.shape[1:])


def tie(*values):
    return lax.optimization_barrier(values)


def plane_steps():
    nz = lax.axis_size("expert")
    return sorted(range(1, nz), key=lambda step: (min(step, nz - step), step))


def gather_planes(block):
    return [block] + [from_plane(block, step) for step in plane_steps()]


def run_mixture(planes, early, weights, shared, first, send_shared):
    steps = plane_steps()
    rows = SEQ + HEAD
    blocks = [jnp.stack(planes[:2]), None]
    cores = [swap_core(blocks[0]), None]
    if len(weights[0][0]) > 1:
        up, down = weights[0]
        cores[0], shared[0], up[1], up[3], down[2], down[3] = tie(
            cores[0], shared[0], up[1], up[3], down[2], down[3]
        )
    sums, done, shared_grads = [None, None], [], None
    for i, (ups, downs) in enumerate(weights):
        name = jnp.stack([first[0] + i, first[1]]).astype(jnp.int32)
        both = shared if i == 0 else None
        following = weights[i + 1] if i + 1 < len(weights) else None
        split = following is not None and len(following[0]) == 3
        final = following is None
        grads = None
        for turn, pair in enumerate((1, 0) if final else (0, 1)):
            hid = (blocks[pair], cores[pair])
            outs = list(mix(name, hid, early, pair, ups, downs, both, sums[pair], grads, final))
            if i == 0 and turn == 0:
                planes[2], planes[3], *outs = tie(*planes[2:], *outs)
                blocks[1] = jnp.stack(planes[2:])
                cores[1] = swap_core(blocks[1])
            if split and turn == 0:
                up, down = following
                up[1], up[2], down[1], down[2], *outs = tie(*up[1:], *down[1:], *outs)
                up.append(swap_chip(up[2]))
                down.append(swap_row(down[1]))
            elif split:
                up[3], down[3], *outs = tie(up[3], down[3], *outs)
            if final and turn == 0:
                shared_grads[1], *outs = tie(shared_grads[1], *outs)
                total = outs[0].astype(F32) + swap_core(outs[2]).astype(F32)
                sent = [total[j].astype(BF16) for j in range(2)]
                *sent, blocks[0] = tie(*sent, blocks[0])
                moved = [to_plane(part, step) for part, step in zip(sent, steps[1:])]
            elif final:
                moved[0], moved[1], *outs = tie(*moved, *outs)
            sums[pair], grads = list(outs[:4]), list(outs[4:])
        done.append(grads[0])
        if i == 0:
            shared_grads = send_shared(*grads[1:])
    near_sums, far_sums = sums
    dx = near_sums[0].astype(F32) + swap_core(near_sums[2]).astype(F32)
    dx_sent, far_sums[3], near_sums[3] = tie(dx[1].astype(BF16), far_sums[3], near_sums[3])
    dx_moved = to_plane(dx_sent, steps[0])
    d_hid = dx[0]
    for part in moved:
        d_hid = d_hid + part.astype(F32)
    far = far_sums[1].astype(F32) + swap_core(far_sums[3]).astype(F32)
    near = near_sums[1].astype(F32) + swap_core(near_sums[3]).astype(F32)
    y_sent = [near[1].astype(BF16)] + [far[j].astype(BF16) for j in range(2)]
    dx_moved, *y_sent = tie(dx_moved, *y_sent)
    return d_hid + dx_moved.astype(F32), near[0], y_sent, done, shared_grads


def fold_bit(part, axis, bit):
    send, keep = halves_of(part, axis, bit)
    return keep, swap_bit(send, bit)


def halves_of(part, axis, bit):
    at = (lax.axis_index("dp") >> bit) & 1
    send = lax.dynamic_index_in_dim(part, 1 - at, axis, False).astype(BF16)
    return send, lax.dynamic_index_in_dim(part, at, axis, False)


def swap_bit(value, bit):
    return swap(value, lambda a, b: (a ^ (1 << bit), b))


def add(pair):
    return pair[0].astype(F32) + pair[1].astype(F32)


def scatter_planes(part, split):
    nz = lax.axis_size("expert")
    z = lax.axis_index("expert")
    cut_q = split * nz
    cut_p = (part.shape[0] - cut_q) // nz

    def rows_of(plane):
        return jnp.concatenate(
            [
                lax.dynamic_slice_in_dim(part, plane * split, split, 0),
                lax.dynamic_slice_in_dim(part, cut_q + plane * cut_p, cut_p, 0),
            ]
        )

    moved = [to_plane(rows_of((z + step) % nz).astype(BF16), step) for step in range(1, nz)]
    return rows_of(z), moved


def two_parts(value):
    high = value.astype(BF16)
    return high, (value - high.astype(F32)).astype(BF16)


def local(
    tokens,
    timestep,
    labels,
    routes,
    expert_gates,
    grad_out,
    ada_weight,
    ada_bias,
    qkv_weight,
    proj_weight,
    shared_up,
    shared_down,
    expert_up,
    expert_down,
    time_table,
    class_table,
):
    rows, feat = tokens.shape
    ndp, nz = lax.axis_size("dp"), lax.axis_size("expert")
    reps = ndp // TP
    ndev = ndp * nz
    members = TP * nz
    local_experts = expert_up.shape[0]
    wide = expert_up.shape[2]
    down_cols = expert_down.shape[2]
    shared_wide = shared_up.shape[1]
    shared_cols = shared_down.shape[1]
    qkv_cols = qkv_weight.shape[1]
    proj_cols = proj_weight.shape[1]
    table_cols = time_table.shape[1]
    plane = lax.axis_index("expert")

    def exchange(value):
        return lax.all_to_all(value, AXES, 0, 0, tiled=True)

    if reps == 4 and wide % 128 == 0 and 2 * wide == feat:
        tail = shared_up.T
        tail = jnp.concatenate([tail[:, :wide], tail[:, wide:]])
    else:
        tail = shared_up.T[:, :wide]
    ups = [expert_up[e] for e in range(local_experts)]
    ups[0] = jnp.concatenate([ups[0], tail])
    flipped = expert_down.transpose(0, 2, 1)
    halves = [
        jnp.concatenate(
            [flipped[:, :, (i * TP + t) * wide : (i * TP + t + 1) * wide] for i in range(reps)],
            axis=2,
        )
        for t in range(TP)
    ]
    core_low = lax.axis_index("dp") % TP == 0
    mine = jnp.where(core_low, halves[0], halves[1])
    moved = swap_core(jnp.where(core_low, halves[1], halves[0]))
    downs = jnp.where(
        core_low, jnp.concatenate([mine, moved], axis=1), jnp.concatenate([moved, mine], axis=1)
    )
    sdowns = shared_down.T.reshape(shared_cols, reps, TP, nz, shared_wide)
    sdowns = sdowns.transpose(2, 3, 0, 1, 4).reshape(1, members, shared_cols, reps * shared_wide)
    sdowns = jnp.broadcast_to(sdowns, (reps,) + sdowns.shape[1:])
    sdowns = sdowns.reshape(ndev, shared_cols, reps * shared_wide)
    gate_high, gate_low = two_parts(expert_gates)
    meta = jnp.stack(
        [
            routes[:, 0].astype(BF16),
            routes[:, 1].astype(BF16),
            gate_high[:, 0],
            gate_high[:, 1],
            gate_low[:, 0],
            gate_low[:, 1],
        ]
    )
    meta = jnp.pad(meta.reshape(-1, feat), ((0, HEAD - meta.size // feat), (0, 0)))
    early = jnp.concatenate([grad_out, meta])

    early_planes = lax.all_gather(early, "expert")
    order = (plane + jnp.array([0] + plane_steps(), jnp.int32)) % nz
    early_planes = jnp.take(early_planes, order, axis=0, mode="clip")
    early_core = swap_core(early_planes)

    pair = jnp.concatenate([qkv_weight.T, proj_weight.T])
    rq, rp = nz * qkv_cols, nz * proj_cols
    packed = ndp == 8 and rq % 16 == 0 and rp % 16 == 0
    ids = jnp.concatenate([timestep, labels])[None]
    all_ids = exchange(jnp.broadcast_to(ids, (ndev, 2)))
    if packed:
        line = jnp.stack([pair] + [from_plane(pair, step) for step in range(1, nz)])
        order = (jnp.arange(nz, dtype=jnp.int32) - plane) % nz
        line = jnp.take(line, order, axis=0, mode="clip")
        line = jnp.concatenate(
            [line[:, :qkv_cols].reshape(rq, feat), line[:, qkv_cols:].reshape(rp, feat)]
        )
        half = feat // 2
        left, right = line[None, :, :half], line[None, :, half:]
        left_x, right_y = swap_chip(left), swap_row(right)
    pick_time = all_ids[:, :1] == jnp.arange(time_table.shape[0], dtype=jnp.int32)[None]
    pick_class = all_ids[:, 1:] == jnp.arange(class_table.shape[0], dtype=jnp.int32)[None]
    cond_cols = dot_nn(pick_time.astype(BF16), time_table) + dot_nn(
        pick_class.astype(BF16), class_table
    )
    cond_all = exchange(jnp.broadcast_to(cond_cols[None], (ndev, ndev, table_cols)))
    downs, cond_all = tie(downs, cond_all)
    downs = [downs[e] for e in range(local_experts)]
    if packed:
        left_x, right_y, cond_all = tie(left_x, right_y, cond_all)
        left_x, right_y = jnp.concatenate([left, left_x]), jnp.concatenate([right, right_y])
        left_y, right_x = swap_row(left_x), swap_chip(right_y)
        left_core, right_core = swap_core(left_x), swap_core(right_y)
    cond_all = cond_all.transpose(1, 0, 2).reshape(ndev, feat)
    silu_all = jax.nn.silu(cond_all).astype(BF16)
    my_index = lax.axis_index(AXES)
    cond_own = lax.dynamic_slice_in_dim(cond_all, my_index, 1, 0)
    mod_cols = dot_nn(silu_all, ada_weight) + ada_bias.astype(F32)[None]
    mod = exchange(mod_cols).reshape(6, feat)
    if packed:
        sdowns, mod = tie(sdowns, mod)
        sdown_t = exchange(sdowns).reshape(feat, reps * shared_wide)
        pieces = [left_x, left_y, left_core, swap_core(left_y)]
        pieces += [right_y, right_x, right_core, swap_core(right_x)]
        mine = lax.axis_index("dp")
        moves = [0, 2, 4, 6, 1, 3, 5, 7]
        where = jnp.stack([mine ^ m for m in moves]).astype(jnp.int32)
        spots = (
            (0, (0, 1), 0),
            (1, (2, 3), 0),
            (2, (4, 5), 0),
            (3, (6, 7), 0),
            (4, (0, 2), half),
            (5, (1, 3), half),
            (6, (4, 6), half),
            (7, (5, 7), half),
        )
        blocks = ndp
    else:
        pair = lax.all_gather(pair, AXES)
        pieces = [
            jnp.concatenate(
                [
                    pair[:, :qkv_cols].reshape(ndev * qkv_cols, feat),
                    pair[:, qkv_cols:].reshape(ndev * proj_cols, feat),
                ]
            )[None]
        ]
        where = jnp.zeros((1,), jnp.int32)
        spots = ((0, (0,), 0),)
        blocks = 0

    if packed:
        weights = []
        for e in range(local_experts):
            up, down = ups[e], downs[e]
            if e:
                up, down, weights[-1][0][1] = tie(up, down, weights[-1][0][1])
            else:
                up, down, mod = tie(up, down, mod)
            up = [up, swap_chip(up), swap_row(up)]
            down = [down, swap_chip(down), swap_row(down)]
            weights.append([up, down])
        shared = [sdown_t]
        place = lax.axis_index("dp") // TP

    mod_rows = jnp.concatenate([mod, jnp.zeros((2, feat), F32)])
    late, *saved_attn = attend(tokens, mod_rows, where, pieces, spots)
    middle = saved_attn[0]

    if packed:
        up, down = weights[0]
        late, up[2], down[1] = tie(late, up[2], down[1])
        up.append(swap_chip(up[2]))
        down.append(swap_row(down[1]))
    steps = plane_steps()
    if packed:
        second = from_plane(late, steps[0])
        second, late, up[1], down[2] = tie(second, late, up[1], down[2])
        planes = [late, second] + [from_plane(late, step) for step in steps[1:]]
        shared = [sdown_t]
    else:
        planes = gather_planes(late)
    if not packed:
        place = jnp.zeros((), jnp.int32)
        weights = []
        for e in range(local_experts):
            up = gather_rows(ups[e][:feat]).transpose(1, 0, 2).reshape(feat, reps * wide)
            weights.append([[up], [gather_rows(downs[e]).reshape(feat, reps * wide)]])
        sup_t = gather_rows(shared_up.T).reshape(reps * shared_wide, feat)
        shared = [exchange(sdowns).reshape(feat, reps * shared_wide), sup_t]

    first = jnp.stack([plane * local_experts, place]).astype(jnp.int32)
    early = (early_planes, early_core)
    def send_shared(g_sup, g_sdown):
        g_sup = g_sup.reshape(reps, shared_wide, feat)
        g_sdown = g_sdown.reshape(ndev, shared_cols, reps * shared_wide)
        return [g_sup, exchange(g_sdown)]

    d_normed_two, branch, y_sent, done, shared_grads = run_mixture(
        planes, early, weights, shared, first, send_shared
    )
    d_normed_two, d_gate_two = d_normed_two[:rows], d_normed_two[rows : rows + 1]

    g_sup, g_sdown = shared_grads
    reduced = []
    for g_mix in done:
        if g_mix.shape[0] == 1:
            g_up = g_mix[0, 0].reshape(feat, reps, wide).transpose(1, 0, 2)
            g_down = g_mix[0, 1].reshape(reps, TP * down_cols, reps, wide).transpose(0, 2, 1, 3)
            g_mix = jnp.stack([g_up, g_down.reshape(reps, feat, wide)], axis=1)
        reduced.append(reduce_rows(g_mix))

    def finish_expert(pair):
        g_up, g_down = pair[0].astype(F32), pair[1].reshape(reps, TP, down_cols, wide)
        kept = jnp.where(core_low, g_down[:, 0], g_down[:, 1])
        got = swap_core(jnp.where(core_low, g_down[:, 1], g_down[:, 0]))
        g_down = [jnp.where(core_low, kept, got), jnp.where(core_low, got, kept)]
        g_down = jnp.concatenate([g_down[t][i] for i in range(reps) for t in range(TP)], axis=1)
        return g_up, g_down.T.astype(F32)

    up_part, down_part = [], []
    for pair in reduced[:-1]:
        g_up, g_down = finish_expert(pair)
        g_up, g_down, d_normed_two = tie(g_up, g_down, d_normed_two)
        up_part.append(g_up)
        down_part.append(g_down)

    def finish_shared(grad):
        grad = grad.reshape(reps, members, shared_cols, reps, shared_wide)
        grad = jnp.sum(grad.astype(F32), axis=0)
        return grad.transpose(2, 0, 3, 1).reshape(reps * members * shared_wide, shared_cols)

    tokens_grad, sums, *g_small = attend_back(
        d_normed_two, grad_out, tokens, mod_rows, saved_attn, where, pieces, spots, blocks
    )
    y_moved = [to_plane(part, step) for part, step in zip(y_sent[:2], plane_steps())]
    *y_moved, tokens_grad, sums, g_small[0], g_small[1] = tie(
        *y_moved, tokens_grad, sums, *g_small
    )
    d_mod = jnp.concatenate([sums[0:5], d_gate_two]).astype(BF16).reshape(ndev, -1)
    d_mod = exchange(d_mod)
    if packed:
        half = feat // 2
        kept, got = g_small[0], swap_core(g_small[1])
        d_mod, kept, got = tie(d_mod, kept, got)
        g_small = add((kept, got)).reshape((2, 2) + kept.shape[1:])
        left, right = halves_of(g_small[..., :half], 1, 1), halves_of(g_small[..., half:], 0, 2)
        left_sent, right_sent, d_mod = tie(left[0], right[0], d_mod)
        right_sent, y_sent[2] = tie(right_sent, y_sent[2])
        left, right = [left[1], swap_bit(left_sent, 1)], [right[1], swap_bit(right_sent, 2)]
        left[1], right[1], g_sdown = tie(left[1], right[1], finish_shared(g_sdown))
        left, right = halves_of(add(left), 0, 2), halves_of(add(right), 0, 1)
        left_sent, right_sent, d_mod, reduced[-1] = tie(left[0], right[0], d_mod, reduced[-1])
        left, right = [left[1], swap_bit(left_sent, 2)], [right[1], swap_bit(right_sent, 1)]
    else:
        g_small = jnp.concatenate(
            [g_small[0].reshape(ndev, qkv_cols, feat), g_small[1].reshape(ndev, proj_cols, feat)],
            axis=1,
        )
        g_small = lax.psum_scatter(g_small, AXES).astype(F32)
        g_sdown = finish_shared(g_sdown)
    reduced[-1], g_sup = tie(reduced[-1], g_sup)
    sup_part = reduce_rows(g_sup).T.astype(F32)
    y_moved.append(to_plane(y_sent[2], plane_steps()[2]))
    d_cond = dot_nt(d_mod, ada_weight)
    d_cond_cols = d_cond.reshape(ndev, ndev, table_cols).transpose(1, 0, 2).reshape(ndev, -1)
    d_cond = jnp.concatenate([d_cond, d_cond_cols], axis=1)
    if packed:
        left[1], right[1], d_cond, *y_moved = tie(left[1], right[1], d_cond, *y_moved)
    d_cond = exchange(d_cond)
    last_up, last_down = finish_expert(reduced[-1])
    if packed:
        left, right, last_up, last_down = tie(add(left), add(right), last_up, last_down)
        g_small, g_moved = scatter_planes(jnp.concatenate([left, right], axis=-1), qkv_cols)
    else:
        g_moved = []
    d_cond, g_sdown, *y_moved = tie(d_cond, g_sdown, *y_moved)
    up_part = jnp.stack(up_part + [last_up])
    down_part = jnp.stack(down_part + [last_down])
    for part in y_moved:
        branch = branch + part.astype(F32)
    gates_grad = branch[rows, : 2 * rows].reshape(2, rows).T
    block_out = (middle + mod[5:6] * branch[:rows]).astype(BF16)
    d_cond = jnp.sum(d_cond, axis=0, keepdims=True)
    cond_grad = local_grad(jax.nn.silu, cond_own, d_cond[:, :feat])
    d_cond_cols = d_cond[:, feat:].reshape(ndev, table_cols)
    d_cond_cols = local_grad(jax.nn.silu, cond_cols, d_cond_cols)
    ada_part = dot_tn(silu_all, d_mod)
    bias_part = jnp.sum(d_mod.astype(F32), axis=0)
    sdown_part = g_sdown

    def table_grad(pick):
        return lax.dot_general(
            pick.astype(F32),
            d_cond_cols,
            (((0,), (0,)), ((), ())),
            precision=lax.Precision.HIGHEST,
            preferred_element_type=F32,
        )

    time_part, class_part = table_grad(pick_time), table_grad(pick_class)

    outs = [block_out, cond_grad, gates_grad, ada_part, bias_part, sup_part, sdown_part]
    outs += [up_part, down_part, time_part, class_part]
    if g_moved:
        *g_moved, outs = lax.optimization_barrier((*g_moved, outs))
    block_out, cond_grad, gates_grad, ada_part, bias_part, sup_part, sdown_part = outs[:7]
    up_part, down_part, time_part, class_part = outs[7:]
    for part in g_moved:
        g_small = g_small + part.astype(F32)
    qkv_part = g_small[:qkv_cols].T
    proj_part = g_small[qkv_cols:].T
    return (
        block_out,
        tokens_grad,
        cond_grad,
        gates_grad,
        ada_part,
        bias_part,
        qkv_part,
        proj_part,
        sup_part,
        sdown_part,
        up_part,
        down_part,
        time_part,
        class_part,
    )


def solution(mesh):
    both = ("dp", "expert")
    by_rows, by_cols, by_first = P(both, None), P(None, both), P(both)
    by_expert = P("expert", None, "dp")
    return jax.shard_map(
        local,
        mesh=mesh,
        in_specs=(
            by_rows,
            by_first,
            by_first,
            by_rows,
            by_rows,
            by_rows,
            by_cols,
            by_first,
            by_cols,
            by_cols,
            by_cols,
            by_cols,
            by_expert,
            by_expert,
            by_cols,
            by_cols,
        ),
        out_specs=(
            by_rows,
            by_rows,
            by_rows,
            by_rows,
            by_cols,
            by_first,
            by_cols,
            by_cols,
            by_cols,
            by_cols,
            by_expert,
            by_expert,
            by_cols,
            by_cols,
        ),
        check_vma=False,
    )
```

```python
import functools
import math

import jax
import jax.numpy as jnp
from jax import lax
from jax.experimental import pallas as pl
from jax.experimental.pallas import tpu as pltpu
from jax.sharding import PartitionSpec as P

H = 12
HD = 64
SEQ = 256
CAP = 128
TP = 2
AXES = ("dp", "expert")
F32 = jnp.float32
BF16 = jnp.bfloat16

HEAD = 16
BLOCKS = 4
GELU_A = math.sqrt(2.0 / math.pi)
GELU_B = 0.044715


def gelu_both(x):
    square = x * x
    t = jnp.tanh(GELU_A * x * (1.0 + GELU_B * square))
    half = 0.5 * (1.0 + t)
    slope = half + 0.5 * x * (1.0 - t * t) * (GELU_A + 3.0 * GELU_A * GELU_B * square)
    return x * half, slope


def mix_kernel(count, shared, more, before, final, first_ref, h_own, h_core, g_own, g_core, *refs):
    refs = list(refs)

    def take(number):
        taken = refs[:number]
        del refs[:number]
        return taken

    ups, downs = take(count), take(count)
    if shared:
        (sdown_ref,) = take(1)
        if count == 1:
            (sup_in,) = take(1)
    if more:
        sums_in = take(4)
    if before:
        (grads_in,) = take(1)
        if shared:
            gsup_in, gsdown_in = take(2)
    sums_out = take(4)
    (grads,) = take(1)
    if shared:
        gsup, gsdown = take(2)
    rows_ref, act_ref, dpre_ref, dy_ref, hid_ref, ds_ref, meta, acc_y, acc_d, gg_acc = take(10)
    up_ref, down_ref, sup_ref, old_ref, new_ref, *sums, sems = refs
    (keep_d, keep_y, send_d, send_y) = sums
    seq, feat = SEQ, h_own.shape[2]
    step = 256
    wide = up_ref.shape[1]
    blocks, part = new_ref.shape[0], new_ref.shape[3]

    copies = []
    if count == 1:
        copies.append(pltpu.make_async_copy(ups[0], up_ref, sems.at[0]))
        copies.append(pltpu.make_async_copy(downs[0], down_ref, sems.at[0]))
        if shared:
            copies.append(pltpu.make_async_copy(sup_in, sup_ref, sems.at[0]))
    else:
        per, swide = feat // count, sup_ref.shape[0] // count
        for i in range(count):
            place = first_ref[1] ^ i
            lanes = pl.ds(pl.multiple_of(place * part, 128), part)
            copies.append(
                pltpu.make_async_copy(ups[i].at[pl.ds(0, feat), :], up_ref.at[:, lanes], sems.at[0])
            )
            at = pl.ds(pl.multiple_of(place * per, 16), per)
            copies.append(pltpu.make_async_copy(downs[i], down_ref.at[at, :], sems.at[0]))
            if shared:
                at = pl.ds(pl.multiple_of(place * swide, 16), swide)
                for j in range(2):
                    copies.append(
                        pltpu.make_async_copy(
                            ups[i].at[pl.ds(feat + j * swide, swide), :],
                            sup_ref.at[at, pl.ds(j * part, part)],
                            sems.at[0],
                        )
                    )
    for copy in copies:
        copy.start()
    if more:
        came_copies = [pltpu.make_async_copy(a, b, sems.at[4]) for a, b in zip(sums_in, sums)]
        for copy in came_copies:
            copy.start()
    if before:
        old = pltpu.make_async_copy(grads_in, old_ref, sems.at[1])
        old.start()

    hs = [h_own.at[0], h_own.at[1], h_core.at[0], h_core.at[1]]
    gs = [g_own.at[0], g_own.at[1], g_core.at[0], g_core.at[1]]
    half = BLOCKS // 2
    for b in range(BLOCKS):
        hid_ref[b] = hs[b][0:seq, :]
        tail = hs[b][seq : seq + HEAD, :].astype(F32)
        gate_two = tail[0:1] + tail[1:2]
        ds_ref[b] = (gate_two * gs[b][0:seq, :].astype(F32)).astype(BF16)
        meta[b] = gs[b][seq : seq + HEAD, :].astype(F32)

    name = first_ref[0].astype(F32)
    up_down = lax.broadcasted_iota(jnp.int32, (seq, seq), 0) <= lax.broadcasted_iota(
        jnp.int32, (seq, seq), 1
    )
    ones_tri = up_down.astype(F32).astype(BF16)
    slot = lax.broadcasted_iota(jnp.int32, (CAP, seq), 0).astype(F32)
    selects, back, gates = [], [], []
    for b in range(BLOCKS):
        m = meta[b]
        in0 = (m[0:1, 0:seq] == name).astype(F32)
        in1 = (m[0:1, seq : 2 * seq] == name).astype(F32)
        gate = in0 * (m[0:1, 2 * seq : 3 * seq] + m[1:2, seq : 2 * seq]) + in1 * (
            m[1:2, 0:seq] + m[1:2, 2 * seq : 3 * seq]
        )
        has = in0 + in1
        count_row = dot_nn(jnp.broadcast_to(has, (16, seq)).astype(BF16), ones_tri)[0:1]
        select = (count_row * has - 1.0 == slot).astype(F32)
        gates.append(jnp.sum(select * gate, axis=1, keepdims=True))
        back.append(select.T.astype(BF16))
        select = select.astype(BF16)
        selects.append(select)
        at = pl.ds(b * CAP, CAP)
        rows_ref[at, :] = dot_nn(select, hid_ref[b]).astype(BF16)
        dy_ref[at, :] = (gates[b] * dot_nn(select, ds_ref[b])).astype(BF16)

    for copy in copies:
        copy.wait()
    rows, dy = rows_ref[...], dy_ref[...]
    for c in range(0, wide, step):
        at = pl.ds(c, step)
        act, slope = gelu_both(dot_nn(rows, up_ref[:, at]))
        act_ref[:, at] = act.astype(BF16)
        dpre_ref[:, at] = (slope * dot_nn(dy, down_ref[:, at])).astype(BF16)
    act, dpre = act_ref[...], dpre_ref[...]
    if more:
        for copy in came_copies:
            copy.wait()
    for b in range(BLOCKS):
        if more:
            came_d, came_y = (keep_d, keep_y) if b < half else (send_d, send_y)
            acc_d[b] = came_d[b % half, 0:seq, :].astype(F32)
            acc_y[b] = came_y[b % half, 0:seq, :].astype(F32)
            gg_acc[b] = came_y[b % half, seq : seq + HEAD, :].astype(F32)
        else:
            acc_d[b] = jnp.zeros((seq, feat), F32)
            acc_y[b] = jnp.zeros((seq, feat), F32)
            gg_acc[b] = jnp.zeros((HEAD, feat), F32)
    gg = [jnp.zeros((CAP, 1), F32)] * BLOCKS
    for c in range(0, feat, step):
        at = pl.ds(c, step)
        res = dot_nt(act, down_ref[at, :])
        dx = dot_nt(dpre, up_ref[at, :]).astype(BF16)
        for b in range(BLOCKS):
            value = res[b * CAP : (b + 1) * CAP]
            slots = pl.ds(b * CAP, CAP)
            gg[b] = gg[b] + jnp.sum(value * dy_ref[slots, at].astype(F32), axis=1, keepdims=True)
            acc_y[b, :, at] += dot_nn(back[b], (gates[b] * value).astype(BF16))
            acc_d[b, :, at] += dot_nn(back[b], dx[b * CAP : (b + 1) * CAP])
    for b in range(BLOCKS):
        m = meta[b]
        inverse = jnp.where(gates[b] > 0.0, 1.0 / jnp.where(gates[b] > 0.0, gates[b], 1.0), 0.0)
        token = jnp.sum(selects[b].astype(F32) * (gg[b] * inverse), axis=0, keepdims=True)
        in0 = (m[0:1, 0:seq] == name).astype(F32)
        in1 = (m[0:1, seq : 2 * seq] == name).astype(F32)
        gg_acc[b, 0:1, 0:seq] += in0 * token
        gg_acc[b, 0:1, seq : 2 * seq] += in1 * token

    if shared:
        hid = hid_ref[...].reshape(BLOCKS * seq, feat)
        ds = ds_ref[...].reshape(BLOCKS * seq, feat)
        act_s, slope = gelu_both(dot_nt(hid, sup_ref[...]))
        act_s = act_s.astype(BF16)
        dpre_s = (slope * dot_nn(ds, sdown_ref[...])).astype(BF16)
        g_one, g_two = dot_tn(dpre_s, hid), dot_tn(ds, act_s)
        if before:
            g_one, g_two = g_one + gsup_in[...], g_two + gsdown_in[...]
        gsup[...] = g_one.astype(gsup.dtype)
        gsdown[...] = g_two.astype(gsdown.dtype)
        for c in range(0, feat, step):
            at = pl.ds(c, step)
            acc_y[:, :, at] += dot_nt(act_s, sdown_ref[at, :]).reshape(BLOCKS, seq, step)
            acc_d[:, :, at] += dot_nn(dpre_s, sup_ref[:, at]).reshape(BLOCKS, seq, step)
    for b in range(BLOCKS):
        out_d, out_y = (keep_d, keep_y) if b < half else (send_d, send_y)
        out_d[b % half, 0:seq, :] = acc_d[b].astype(BF16)
        gate_sum = jnp.zeros((HEAD, feat), F32)
        if final:
            gate_sum = jnp.sum(gs[b][0:seq, :].astype(F32) * acc_y[b], axis=0, keepdims=True)
            gate_sum = jnp.broadcast_to(gate_sum, (HEAD, feat))
        out_d[b % half, seq : seq + HEAD, :] = gate_sum.astype(BF16)
        out_y[b % half, 0:seq, :] = acc_y[b].astype(BF16)
        out_y[b % half, seq : seq + HEAD, :] = gg_acc[b].astype(BF16)

    sum_copies = [pltpu.make_async_copy(a, b, sems.at[5]) for a, b in zip(sums, sums_out)]
    for copy in sum_copies:
        copy.start()
    if before:
        old.wait()
    per = feat // blocks

    def put(i, kind, start, value):
        at = pl.ds(start, value.shape[0])
        if before:
            value = value + old_ref[i, kind, at, :].astype(F32)
        new_ref[i, kind, at, :] = value.astype(BF16)

    for c in range(0, feat, step):
        total = dot_tn(rows_ref[:, c : c + step], dpre)
        for i in range(blocks):
            put(i, 0, c, total[:, i * part : (i + 1) * part])
    first_out = pltpu.make_async_copy(new_ref.at[:, 0], grads.at[:, 0], sems.at[2])
    first_out.start()
    chunk = 2 * per if blocks > 1 else step
    for c in range(0, feat, chunk):
        total = dot_tn(dy_ref[:, c : c + chunk], act)
        if blocks == 1:
            put(0, 1, c, total)
            continue
        for i in range(2):
            for q in range(blocks):
                value = total[i * per : (i + 1) * per, q * part : (q + 1) * part]
                put(c // per + i, 1, q * per, value)
    second_out = pltpu.make_async_copy(new_ref.at[:, 1], grads.at[:, 1], sems.at[3])
    second_out.start()
    first_out.wait()
    second_out.wait()
    for copy in sum_copies:
        copy.wait()


def mix(first, hid, grads, block, ups, downs, shared, more, before, final):
    full, feat = hid[0].shape[1:]
    rows = full - HEAD
    count = len(ups)
    half, total = BLOCKS // 2, BLOCKS * CAP
    wide = downs[0].shape[-1]
    blocks = count
    part = wide // blocks
    sds = jax.ShapeDtypeStruct
    given = [*hid, *grads, *ups, *downs]
    pair = lambda at: pl.BlockSpec((half, full, feat), lambda i: (at, 0, 0))
    specs = [pair(0), pair(0), pair(block), pair(block)] + [HBM_SPEC] * (2 * count)
    outs = [sds((half, full, feat), BF16)] * 4 + [sds((blocks, 2, feat, part), BF16)]
    out_specs = [HBM_SPEC] * 5
    swide = 16 * count
    if shared is not None:
        swide = shared[0].shape[1]
        given += shared
        specs += [VMEM_SPEC] + [HBM_SPEC] * (len(shared) - 1)
        kind = F32 if before is None else BF16
        outs += [sds((swide, feat), kind), sds((feat, swide), kind)]
        out_specs += [VMEM_SPEC] * 2
    if more is not None:
        given += more
        specs += [HBM_SPEC] * 4
    if before is not None:
        given += before
        specs += [HBM_SPEC] + [VMEM_SPEC] * (len(before) - 1)
    old_shape = (blocks, 2, feat, part) if before is not None else (1, 1, 16, 128)
    return pl.pallas_call(
        functools.partial(
            mix_kernel, count, shared is not None, more is not None, before is not None, final
        ),
        grid=(1,),
        in_specs=[SMEM_SPEC] + specs,
        out_specs=out_specs,
        out_shape=outs,
        scratch_shapes=[
            pltpu.VMEM((total, feat), BF16),
            pltpu.VMEM((total, wide), BF16),
            pltpu.VMEM((total, wide), BF16),
            pltpu.VMEM((total, feat), BF16),
            pltpu.VMEM((BLOCKS, rows, feat), BF16),
            pltpu.VMEM((BLOCKS, rows, feat), BF16),
            pltpu.VMEM((BLOCKS, HEAD, feat), F32),
            pltpu.VMEM((BLOCKS, rows, feat), F32),
            pltpu.VMEM((BLOCKS, rows, feat), F32),
            pltpu.VMEM((BLOCKS, HEAD, feat), F32),
            pltpu.VMEM((feat, wide), BF16),
            pltpu.VMEM((feat, wide), BF16),
            pltpu.VMEM((swide, feat), BF16),
            pltpu.VMEM(old_shape, BF16),
            pltpu.VMEM((blocks, 2, feat, part), BF16),
            pltpu.VMEM((half, full, feat), BF16),
            pltpu.VMEM((half, full, feat), BF16),
            pltpu.VMEM((half, full, feat), BF16),
            pltpu.VMEM((half, full, feat), BF16),
            pltpu.SemaphoreType.DMA((6,)),
        ],
        compiler_params=pltpu.CompilerParams(vmem_limit_bytes=58 * 2**20),
        cost_estimate=CHEAP,
    )(first, *given)


def norm_back(upstream, normed, inverse):
    mean_grad = jnp.mean(upstream, axis=-1, keepdims=True)
    mean_mix = jnp.mean(upstream * normed, axis=-1, keepdims=True)
    return inverse * (upstream - mean_grad - normed * mean_mix)


def dot_nn(left, right):
    return jnp.dot(left, right, preferred_element_type=F32)


def dot_tn(left, right):
    return lax.dot_general(left, right, (((0,), (0,)), ((), ())), preferred_element_type=F32)


def dot_nt(left, right):
    return lax.dot_general(left, right, (((1,), (1,)), ((), ())), preferred_element_type=F32)


def local_grad(function, inputs, upstream):
    unused, pull = jax.vjp(function, inputs)
    return pull(upstream)[0]


def row_norm(values):
    center = values - jnp.mean(values, axis=-1, keepdims=True)
    inverse = lax.rsqrt(jnp.mean(center * center, axis=-1, keepdims=True) + 1e-06)
    return center * inverse, inverse


def load_weights(where_ref, pieces, spots, wq, wp, sem):
    copies = []
    for ref, blocks, lane in spots:
        piece = pieces[ref]
        rq = wq.shape[0] // where_ref.shape[0]
        rp = wp.shape[0] // where_ref.shape[0]
        width = piece.shape[2]
        for j, block in enumerate(blocks):
            at = where_ref[block]
            lanes = pl.ds(lane, width)
            to_q = wq.at[pl.ds(pl.multiple_of(at * rq, 16), rq), lanes]
            to_p = wp.at[pl.ds(pl.multiple_of(at * rp, 16), rp), lanes]
            copies.append(pltpu.make_async_copy(piece.at[j, pl.ds(0, rq), :], to_q, sem))
            copies.append(pltpu.make_async_copy(piece.at[j, pl.ds(rq, rp), :], to_p, sem))
    for copy in copies:
        copy.start()
    return copies


def pair_masks():
    lane = lax.broadcasted_iota(jnp.int32, (1, 2 * HD), 1)
    return [(lane < HD).astype(F32).astype(BF16), (lane >= HD).astype(F32).astype(BF16)]


def head_probs(query, key, mask):
    scores = dot_nt(query * mask, key) * (1.0 / math.sqrt(HD))
    exp_scores = jnp.exp(scores - jnp.max(scores, axis=-1, keepdims=True))
    return exp_scores / jnp.sum(exp_scores, axis=-1, keepdims=True)


def attend_kernel(spots, where_ref, tok_ref, mod_ref, *refs):
    count = len({spot[0] for spot in spots})
    pieces = refs[:count]
    late_ref, x1_ref, projected_ref, h1_ref, qkv_ref, attn_ref, wq, wp, sem = refs[count:]
    copies = load_weights(where_ref, pieces, spots, wq, wp, sem)
    rows, feat = tok_ref.shape
    tokens = tok_ref[...].astype(F32)
    norm, unused = row_norm(tokens)
    h1_ref[...] = (norm * (1.0 + mod_ref[1:2, :]) + mod_ref[0:1, :]).astype(BF16)
    for copy in copies:
        copy.wait()
    h1 = h1_ref[...]
    for c in range(0, 3 * feat, 256):
        at = pl.ds(c, 256)
        qkv_ref[:, at] = dot_nt(h1, wq[at, :]).astype(BF16)
    low, high = pair_masks()
    for c in range(0, feat, 2 * HD):
        at = pl.ds(c, 2 * HD)
        query, key = qkv_ref[:, at], qkv_ref[:, pl.ds(feat + c, 2 * HD)]
        value = qkv_ref[:, pl.ds(2 * feat + c, 2 * HD)]
        first = head_probs(query, key, low).astype(BF16)
        second = head_probs(query, key, high).astype(BF16)
        attn_ref[:, at] = (dot_nn(first, value * low) + dot_nn(second, value * high)).astype(BF16)
    attn = attn_ref[...]
    for c in range(0, feat, 256):
        at = pl.ds(c, 256)
        projected_ref[:, at] = dot_nt(attn, wp[at, :])
    x1 = tokens + mod_ref[2:3, :] * projected_ref[...]
    x1_ref[...] = x1
    norm, unused = row_norm(x1)
    late_ref[0:rows, :] = (norm * (1.0 + mod_ref[4:5, :]) + mod_ref[3:4, :]).astype(BF16)
    gate = mod_ref[5:6, :]
    gate_high = gate.astype(BF16).astype(F32)
    line = lax.broadcasted_iota(jnp.int32, (HEAD, feat), 0)
    late_ref[rows : rows + HEAD, :] = jnp.where(
        line == 0, gate_high, jnp.where(line == 1, gate - gate_high, 0.0)
    ).astype(BF16)


VMEM_SPEC = pl.BlockSpec(memory_space=pltpu.VMEM)
SMEM_SPEC = pl.BlockSpec(memory_space=pltpu.SMEM)
HBM_SPEC = pl.BlockSpec(memory_space=pl.ANY)
CHEAP = pl.CostEstimate(flops=10**6, bytes_accessed=10**5, transcendentals=0)


def attend(tokens, mod, where, pieces, spots):
    rows, feat = tokens.shape
    sds = jax.ShapeDtypeStruct
    return pl.pallas_call(
        functools.partial(attend_kernel, spots),
        in_specs=[SMEM_SPEC, VMEM_SPEC, VMEM_SPEC] + [HBM_SPEC] * len(pieces),
        out_specs=[VMEM_SPEC] * 6,
        out_shape=[
            sds((rows + HEAD, feat), BF16),
            sds((rows, feat), F32),
            sds((rows, feat), F32),
            sds((rows, feat), BF16),
            sds((rows, 3 * feat), BF16),
            sds((rows, feat), BF16),
        ],
        scratch_shapes=[
            pltpu.VMEM((3 * feat, feat), BF16),
            pltpu.VMEM((feat, feat), BF16),
            pltpu.SemaphoreType.DMA,
        ],
        compiler_params=pltpu.CompilerParams(vmem_limit_bytes=40 * 2**20),
        cost_estimate=CHEAP,
    )(where, tokens, mod, *pieces)


def back_kernel(spots, blocks, where_ref, dh2_ref, grad_ref, tok_ref, mod_ref, x1_ref, projected_ref, h1_ref, qkv_ref, attn_ref, *refs):
    count = len({spot[0] for spot in spots})
    pieces = refs[:count]
    outs = refs[count:]
    tokens_out, sums_out = outs[0], outs[1]
    wq, wp, dqkv, dattn, g_ref, sem, sems = outs[-7:]
    grads = outs[2:-7]
    copies = load_weights(where_ref, pieces, spots, wq, wp, sem)
    rows, feat = tok_ref.shape
    norm_two, inverse_two = row_norm(x1_ref[...])
    dh2 = dh2_ref[0:rows, :]
    d_x1 = grad_ref[...].astype(F32) + norm_back(dh2 * (1.0 + mod_ref[4:5, :]), norm_two, inverse_two)
    sums_out[3:4, :] = jnp.sum(dh2, axis=0, keepdims=True)
    sums_out[4:5, :] = jnp.sum(dh2 * norm_two, axis=0, keepdims=True)
    sums_out[2:3, :] = jnp.sum(d_x1 * projected_ref[...], axis=0, keepdims=True)
    sums_out[5:8, :] = jnp.zeros((3, feat), F32)
    dp = (mod_ref[2:3, :] * d_x1).astype(BF16)
    for copy in copies:
        copy.wait()

    def put(kind, start, size, value):
        if not blocks:
            grads[kind][start : start + size, :] = value.astype(BF16)
            return
        per = (3 * feat if kind == 0 else feat) // blocks
        base = 0 if kind == 0 else 3 * feat // blocks
        done = 0
        while done < size:
            block, inside = (start + done) // per, (start + done) % per
            take = min(size - done, per - inside)
            g_ref[block, base + inside : base + inside + take, :] = value[done : done + take].astype(BF16)
            done += take

    attn = attn_ref[...]
    for c in range(0, feat, 256):
        dattn[:, c : c + 256] = dot_nn(dp, wp[:, c : c + 256]).astype(BF16)
        put(1, c, 256, dot_tn(dp[:, c : c + 256], attn))
    low, high = pair_masks()
    scale = 1.0 / math.sqrt(HD)
    for c in range(0, feat, 2 * HD):
        at, at_key, at_value = pl.ds(c, 2 * HD), pl.ds(feat + c, 2 * HD), pl.ds(2 * feat + c, 2 * HD)
        query, key, value, d_out = qkv_ref[:, at], qkv_ref[:, at_key], qkv_ref[:, at_value], dattn[:, at]
        d_query, d_key, d_value = 0.0, 0.0, 0.0
        for mask in (low, high):
            probs = head_probs(query, key, mask)
            d_part = d_out * mask
            d_value = d_value + dot_tn(probs.astype(BF16), d_part)
            d_probs = dot_nt(d_part, value)
            delta = jnp.sum(probs * d_probs, axis=-1, keepdims=True)
            d_scores = (probs * (d_probs - delta)).astype(BF16)
            d_query = d_query + dot_nn(d_scores, key * mask)
            d_key = d_key + dot_tn(d_scores, query * mask)
        dqkv[:, at] = (d_query * scale).astype(BF16)
        dqkv[:, at_key] = (d_key * scale).astype(BF16)
        dqkv[:, at_value] = d_value.astype(BF16)
    h1 = h1_ref[...]
    d_all = dqkv[...]
    parts = []
    for c in range(0, feat, 256):
        parts.append(dot_nn(d_all, wq[:, c : c + 256]))
    d_h1 = jnp.concatenate(parts, axis=1)
    norm_one, inverse_one = row_norm(tok_ref[...].astype(F32))
    sums_out[0:1, :] = jnp.sum(d_h1, axis=0, keepdims=True)
    sums_out[1:2, :] = jnp.sum(d_h1 * norm_one, axis=0, keepdims=True)
    tokens_out[...] = d_x1 + norm_back(d_h1 * (1.0 + mod_ref[1:2, :]), norm_one, inverse_one)
    for c in range(0, 3 * feat, 256):
        put(0, c, 256, dot_tn(dqkv[:, c : c + 256], h1))
    core = where_ref[0] % 2

    def blocks_out(action):
        for block in range(blocks):
            for ref, same in ((grads[0], True), (grads[1], False)):

                @pl.when((core == block % 2) == same)
                def _(ref=ref, block=block):
                    copy = pltpu.make_async_copy(g_ref.at[block], ref.at[block // 2], sems.at[block])
                    copy.start() if action == "start" else copy.wait()

    if blocks:
        blocks_out("start")
        blocks_out("wait")


def attend_back(d_hid, grad_out, tokens, mod, saved, where, pieces, spots, blocks):
    rows, feat = tokens.shape
    sds = jax.ShapeDtypeStruct
    if blocks:
        shapes = [sds((blocks // 2, 4 * feat // blocks, feat), BF16)] * 2
    else:
        shapes = [sds((3 * feat, feat), BF16), sds((feat, feat), BF16)]
    return pl.pallas_call(
        functools.partial(back_kernel, spots, blocks),
        in_specs=[SMEM_SPEC] + [VMEM_SPEC] * (4 + len(saved)) + [HBM_SPEC] * len(pieces),
        out_specs=[VMEM_SPEC] * 2 + [HBM_SPEC if blocks else VMEM_SPEC] * 2,
        out_shape=[sds((rows, feat), F32), sds((8, feat), F32)] + shapes,
        scratch_shapes=[
            pltpu.VMEM((3 * feat, feat), BF16),
            pltpu.VMEM((feat, feat), BF16),
            pltpu.VMEM((rows, 3 * feat), BF16),
            pltpu.VMEM((rows, feat), BF16),
            pltpu.VMEM((blocks, 4 * feat // blocks, feat) if blocks else (1, 16, 128), BF16),
            pltpu.SemaphoreType.DMA,
            pltpu.SemaphoreType.DMA((max(1, blocks),)),
        ],
        compiler_params=pltpu.CompilerParams(vmem_limit_bytes=48 * 2**20),
        cost_estimate=CHEAP,
    )(where, d_hid, grad_out, tokens, mod, *saved, *pieces)


def swap(value, move):
    ndp, nz = lax.axis_size("dp"), lax.axis_size("expert")
    pairs = []
    for a in range(ndp):
        for b in range(nz):
            c, d = move(a, b)
            pairs.append((a * nz + b, c * nz + d))
    return lax.ppermute(value, AXES, pairs)


def swap_row(value):
    return swap(value, lambda a, b: (a ^ 4, b))


def swap_core(value):
    return swap(value, lambda a, b: (a ^ 1, b))


def swap_chip(value):
    return swap(value, lambda a, b: (a ^ 2, b))


def from_plane(value, step):
    nz = lax.axis_size("expert")
    return swap(value, lambda a, b: (a, (b - step) % nz))


def to_plane(value, step):
    nz = lax.axis_size("expert")
    return swap(value, lambda a, b: (a, (b + step) % nz))


def row_bits():
    return (lax.axis_size("dp") // TP).bit_length() - 1


def row_groups():
    ndp = lax.axis_size("dp")
    return [list(range(i, ndp, TP)) for i in range(TP)]


def gather_rows(value):
    return lax.all_gather(value, "dp", axis_index_groups=row_groups())


def reduce_rows(value):
    flat = value.astype(BF16).reshape(-1, value.shape[-1])
    flat = lax.psum_scatter(flat, "dp", tiled=True, axis_index_groups=row_groups())
    return flat.reshape(value.shape[1:])


def tie(*values):
    return lax.optimization_barrier(values)


def plane_steps():
    nz = lax.axis_size("expert")
    return sorted(range(1, nz), key=lambda step: (min(step, nz - step), step))


def gather_planes(block):
    return [block] + [from_plane(block, step) for step in plane_steps()]


def run_mixture(planes, early, weights, shared, first, send_shared):
    steps = plane_steps()
    rows = SEQ + HEAD
    blocks = [jnp.stack(planes[:2]), None]
    cores = [swap_core(blocks[0]), None]
    if len(weights[0][0]) > 1:
        up, down = weights[0]
        cores[0], shared[0], up[1], up[3], down[2], down[3] = tie(
            cores[0], shared[0], up[1], up[3], down[2], down[3]
        )
    sums, done, shared_grads = [None, None], [], None
    for i, (ups, downs) in enumerate(weights):
        name = jnp.stack([first[0] + i, first[1]]).astype(jnp.int32)
        both = shared if i == 0 else None
        following = weights[i + 1] if i + 1 < len(weights) else None
        split = following is not None and len(following[0]) == 3
        final = following is None
        grads = None
        for turn, pair in enumerate((1, 0) if final else (0, 1)):
            hid = (blocks[pair], cores[pair])
            outs = list(mix(name, hid, early, pair, ups, downs, both, sums[pair], grads, final))
            if i == 0 and turn == 0:
                planes[2], planes[3], *outs = tie(*planes[2:], *outs)
                blocks[1] = jnp.stack(planes[2:])
                cores[1] = swap_core(blocks[1])
            if split and turn == 0:
                up, down = following
                up[1], up[2], down[1], down[2], *outs = tie(*up[1:], *down[1:], *outs)
                up.append(swap_chip(up[2]))
                down.append(swap_row(down[1]))
            elif split:
                up[3], down[3], *outs = tie(up[3], down[3], *outs)
            if final and turn == 0:
                shared_grads[1], *outs = tie(shared_grads[1], *outs)
                total = outs[0].astype(F32) + swap_core(outs[2]).astype(F32)
                sent = [total[j].astype(BF16) for j in range(2)]
                *sent, blocks[0] = tie(*sent, blocks[0])
                moved = [to_plane(part, step) for part, step in zip(sent, steps[1:])]
            elif final:
                moved[0], moved[1], *outs = tie(*moved, *outs)
            sums[pair], grads = list(outs[:4]), list(outs[4:])
        done.append(grads[0])
        if i == 0:
            shared_grads = send_shared(*grads[1:])
    near_sums, far_sums = sums
    dx = near_sums[0].astype(F32) + swap_core(near_sums[2]).astype(F32)
    dx_sent, far_sums[3], near_sums[3] = tie(dx[1].astype(BF16), far_sums[3], near_sums[3])
    dx_moved = to_plane(dx_sent, steps[0])
    d_hid = dx[0]
    for part in moved:
        d_hid = d_hid + part.astype(F32)
    far = far_sums[1].astype(F32) + swap_core(far_sums[3]).astype(F32)
    near = near_sums[1].astype(F32) + swap_core(near_sums[3]).astype(F32)
    y_sent = [near[1].astype(BF16)] + [far[j].astype(BF16) for j in range(2)]
    dx_moved, *y_sent = tie(dx_moved, *y_sent)
    return d_hid + dx_moved.astype(F32), near[0], y_sent, done, shared_grads


def fold_bit(part, axis, bit):
    send, keep = halves_of(part, axis, bit)
    return keep, swap_bit(send, bit)


def halves_of(part, axis, bit):
    at = (lax.axis_index("dp") >> bit) & 1
    send = lax.dynamic_index_in_dim(part, 1 - at, axis, False).astype(BF16)
    return send, lax.dynamic_index_in_dim(part, at, axis, False)


def swap_bit(value, bit):
    return swap(value, lambda a, b: (a ^ (1 << bit), b))


def add(pair):
    return pair[0].astype(F32) + pair[1].astype(F32)


def scatter_planes(part, split):
    nz = lax.axis_size("expert")
    z = lax.axis_index("expert")
    cut_q = split * nz
    cut_p = (part.shape[0] - cut_q) // nz

    def rows_of(plane):
        return jnp.concatenate(
            [
                lax.dynamic_slice_in_dim(part, plane * split, split, 0),
                lax.dynamic_slice_in_dim(part, cut_q + plane * cut_p, cut_p, 0),
            ]
        )

    moved = [to_plane(rows_of((z + step) % nz).astype(BF16), step) for step in range(1, nz)]
    return rows_of(z), moved


def two_parts(value):
    high = value.astype(BF16)
    return high, (value - high.astype(F32)).astype(BF16)


def local(
    tokens,
    timestep,
    labels,
    routes,
    expert_gates,
    grad_out,
    ada_weight,
    ada_bias,
    qkv_weight,
    proj_weight,
    shared_up,
    shared_down,
    expert_up,
    expert_down,
    time_table,
    class_table,
):
    rows, feat = tokens.shape
    ndp, nz = lax.axis_size("dp"), lax.axis_size("expert")
    reps = ndp // TP
    ndev = ndp * nz
    members = TP * nz
    local_experts = expert_up.shape[0]
    wide = expert_up.shape[2]
    down_cols = expert_down.shape[2]
    shared_wide = shared_up.shape[1]
    shared_cols = shared_down.shape[1]
    qkv_cols = qkv_weight.shape[1]
    proj_cols = proj_weight.shape[1]
    table_cols = time_table.shape[1]
    plane = lax.axis_index("expert")

    def exchange(value):
        return lax.all_to_all(value, AXES, 0, 0, tiled=True)

    if reps == 4 and wide % 128 == 0 and 2 * wide == feat:
        tail = shared_up.T
        tail = jnp.concatenate([tail[:, :wide], tail[:, wide:]])
    else:
        tail = shared_up.T[:, :wide]
    ups = [expert_up[e] for e in range(local_experts)]
    ups[0] = jnp.concatenate([ups[0], tail])
    flipped = expert_down.transpose(0, 2, 1)
    halves = [
        jnp.concatenate(
            [flipped[:, :, (i * TP + t) * wide : (i * TP + t + 1) * wide] for i in range(reps)],
            axis=2,
        )
        for t in range(TP)
    ]
    core_low = lax.axis_index("dp") % TP == 0
    mine = jnp.where(core_low, halves[0], halves[1])
    moved = swap_core(jnp.where(core_low, halves[1], halves[0]))
    downs = jnp.where(
        core_low, jnp.concatenate([mine, moved], axis=1), jnp.concatenate([moved, mine], axis=1)
    )
    sdowns = shared_down.T.reshape(shared_cols, reps, TP, nz, shared_wide)
    sdowns = sdowns.transpose(2, 3, 0, 1, 4).reshape(1, members, shared_cols, reps * shared_wide)
    sdowns = jnp.broadcast_to(sdowns, (reps,) + sdowns.shape[1:])
    sdowns = sdowns.reshape(ndev, shared_cols, reps * shared_wide)
    gate_high, gate_low = two_parts(expert_gates)
    meta = jnp.stack(
        [
            routes[:, 0].astype(BF16),
            routes[:, 1].astype(BF16),
            gate_high[:, 0],
            gate_high[:, 1],
            gate_low[:, 0],
            gate_low[:, 1],
        ]
    )
    meta = jnp.pad(meta.reshape(-1, feat), ((0, HEAD - meta.size // feat), (0, 0)))
    early = jnp.concatenate([grad_out, meta])

    early_planes = lax.all_gather(early, "expert")
    order = (plane + jnp.array([0] + plane_steps(), jnp.int32)) % nz
    early_planes = jnp.take(early_planes, order, axis=0, mode="clip")
    early_core = swap_core(early_planes)

    pair = jnp.concatenate([qkv_weight.T, proj_weight.T])
    rq, rp = nz * qkv_cols, nz * proj_cols
    packed = ndp == 8 and rq % 16 == 0 and rp % 16 == 0
    ids = jnp.concatenate([timestep, labels])[None]
    all_ids = exchange(jnp.broadcast_to(ids, (ndev, 2)))
    if packed:
        line = jnp.stack([pair] + [from_plane(pair, step) for step in range(1, nz)])
        order = (jnp.arange(nz, dtype=jnp.int32) - plane) % nz
        line = jnp.take(line, order, axis=0, mode="clip")
        line = jnp.concatenate(
            [line[:, :qkv_cols].reshape(rq, feat), line[:, qkv_cols:].reshape(rp, feat)]
        )
        half = feat // 2
        left, right = line[None, :, :half], line[None, :, half:]
        left_x, right_y = swap_chip(left), swap_row(right)
    pick_time = all_ids[:, :1] == jnp.arange(time_table.shape[0], dtype=jnp.int32)[None]
    pick_class = all_ids[:, 1:] == jnp.arange(class_table.shape[0], dtype=jnp.int32)[None]
    cond_cols = dot_nn(pick_time.astype(BF16), time_table) + dot_nn(
        pick_class.astype(BF16), class_table
    )
    cond_all = exchange(jnp.broadcast_to(cond_cols[None], (ndev, ndev, table_cols)))
    downs, cond_all = tie(downs, cond_all)
    downs = [downs[e] for e in range(local_experts)]
    if packed:
        left_x, right_y, cond_all = tie(left_x, right_y, cond_all)
        left_x, right_y = jnp.concatenate([left, left_x]), jnp.concatenate([right, right_y])
        left_y, right_x = swap_row(left_x), swap_chip(right_y)
        left_core, right_core = swap_core(left_x), swap_core(right_y)
    cond_all = cond_all.transpose(1, 0, 2).reshape(ndev, feat)
    silu_all = jax.nn.silu(cond_all).astype(BF16)
    my_index = lax.axis_index(AXES)
    cond_own = lax.dynamic_slice_in_dim(cond_all, my_index, 1, 0)
    mod_cols = dot_nn(silu_all, ada_weight) + ada_bias.astype(F32)[None]
    mod = exchange(mod_cols).reshape(6, feat)
    if packed:
        sdowns, mod = tie(sdowns, mod)
        sdown_t = exchange(sdowns).reshape(feat, reps * shared_wide)
        pieces = [left_x, left_y, left_core, swap_core(left_y)]
        pieces += [right_y, right_x, right_core, swap_core(right_x)]
        mine = lax.axis_index("dp")
        moves = [0, 2, 4, 6, 1, 3, 5, 7]
        where = jnp.stack([mine ^ m for m in moves]).astype(jnp.int32)
        spots = (
            (0, (0, 1), 0),
            (1, (2, 3), 0),
            (2, (4, 5), 0),
            (3, (6, 7), 0),
            (4, (0, 2), half),
            (5, (1, 3), half),
            (6, (4, 6), half),
            (7, (5, 7), half),
        )
        blocks = ndp
    else:
        pair = lax.all_gather(pair, AXES)
        pieces = [
            jnp.concatenate(
                [
                    pair[:, :qkv_cols].reshape(ndev * qkv_cols, feat),
                    pair[:, qkv_cols:].reshape(ndev * proj_cols, feat),
                ]
            )[None]
        ]
        where = jnp.zeros((1,), jnp.int32)
        spots = ((0, (0,), 0),)
        blocks = 0

    if packed:
        weights = []
        for e in range(local_experts):
            up, down = ups[e], downs[e]
            if e:
                up, down, weights[-1][0][1] = tie(up, down, weights[-1][0][1])
            else:
                up, down, mod = tie(up, down, mod)
            up = [up, swap_chip(up), swap_row(up)]
            down = [down, swap_chip(down), swap_row(down)]
            weights.append([up, down])
        shared = [sdown_t]
        place = lax.axis_index("dp") // TP

    mod_rows = jnp.concatenate([mod, jnp.zeros((2, feat), F32)])
    late, *saved_attn = attend(tokens, mod_rows, where, pieces, spots)
    middle = saved_attn[0]

    if packed:
        up, down = weights[0]
        late, up[2], down[1] = tie(late, up[2], down[1])
        up.append(swap_chip(up[2]))
        down.append(swap_row(down[1]))
    steps = plane_steps()
    if packed:
        second = from_plane(late, steps[0])
        second, late, up[1], down[2] = tie(second, late, up[1], down[2])
        planes = [late, second] + [from_plane(late, step) for step in steps[1:]]
        shared = [sdown_t]
    else:
        planes = gather_planes(late)
    if not packed:
        place = jnp.zeros((), jnp.int32)
        weights = []
        for e in range(local_experts):
            up = gather_rows(ups[e][:feat]).transpose(1, 0, 2).reshape(feat, reps * wide)
            weights.append([[up], [gather_rows(downs[e]).reshape(feat, reps * wide)]])
        sup_t = gather_rows(shared_up.T).reshape(reps * shared_wide, feat)
        shared = [exchange(sdowns).reshape(feat, reps * shared_wide), sup_t]

    first = jnp.stack([plane * local_experts, place]).astype(jnp.int32)
    early = (early_planes, early_core)
    def send_shared(g_sup, g_sdown):
        g_sup = g_sup.reshape(reps, shared_wide, feat)
        g_sdown = g_sdown.reshape(ndev, shared_cols, reps * shared_wide)
        return [g_sup, exchange(g_sdown)]

    d_normed_two, branch, y_sent, done, shared_grads = run_mixture(
        planes, early, weights, shared, first, send_shared
    )
    d_gate_two = d_normed_two[rows : rows + 1]

    g_sup, g_sdown = shared_grads
    reduced = []
    for g_mix in done:
        if g_mix.shape[0] == 1:
            g_up = g_mix[0, 0].reshape(feat, reps, wide).transpose(1, 0, 2)
            g_down = g_mix[0, 1].reshape(reps, TP * down_cols, reps, wide).transpose(0, 2, 1, 3)
            g_mix = jnp.stack([g_up, g_down.reshape(reps, feat, wide)], axis=1)
        reduced.append(reduce_rows(g_mix))

    def finish_expert(pair):
        g_up, g_down = pair[0].astype(F32), pair[1].reshape(reps, TP, down_cols, wide)
        kept = jnp.where(core_low, g_down[:, 0], g_down[:, 1])
        got = swap_core(jnp.where(core_low, g_down[:, 1], g_down[:, 0]))
        g_down = [jnp.where(core_low, kept, got), jnp.where(core_low, got, kept)]
        g_down = jnp.concatenate([g_down[t][i] for i in range(reps) for t in range(TP)], axis=1)
        return g_up, g_down.T.astype(F32)

    up_part, down_part = [], []
    for pair in reduced[:-1]:
        g_up, g_down = finish_expert(pair)
        g_up, g_down, d_normed_two = tie(g_up, g_down, d_normed_two)
        up_part.append(g_up)
        down_part.append(g_down)

    def finish_shared(grad):
        grad = grad.reshape(reps, members, shared_cols, reps, shared_wide)
        grad = jnp.sum(grad.astype(F32), axis=0)
        return grad.transpose(2, 0, 3, 1).reshape(reps * members * shared_wide, shared_cols)

    tokens_grad, sums, *g_small = attend_back(
        d_normed_two, grad_out, tokens, mod_rows, saved_attn, where, pieces, spots, blocks
    )
    y_moved = [to_plane(part, step) for part, step in zip(y_sent[:2], plane_steps())]
    *y_moved, tokens_grad, sums, g_small[0], g_small[1] = tie(
        *y_moved, tokens_grad, sums, *g_small
    )
    d_mod = jnp.concatenate([sums[0:5], d_gate_two]).astype(BF16).reshape(ndev, -1)
    d_mod = exchange(d_mod)
    if packed:
        half = feat // 2
        kept, got = g_small[0], swap_core(g_small[1])
        d_mod, kept, got = tie(d_mod, kept, got)
        g_small = add((kept, got)).reshape((2, 2) + kept.shape[1:])
        left, right = halves_of(g_small[..., :half], 1, 1), halves_of(g_small[..., half:], 0, 2)
        left_sent, right_sent, d_mod = tie(left[0], right[0], d_mod)
        right_sent, y_sent[2] = tie(right_sent, y_sent[2])
        left, right = [left[1], swap_bit(left_sent, 1)], [right[1], swap_bit(right_sent, 2)]
        left[1], right[1], g_sdown = tie(left[1], right[1], finish_shared(g_sdown))
        left, right = halves_of(add(left), 0, 2), halves_of(add(right), 0, 1)
        left_sent, right_sent, d_mod, reduced[-1] = tie(left[0], right[0], d_mod, reduced[-1])
        left, right = [left[1], swap_bit(left_sent, 2)], [right[1], swap_bit(right_sent, 1)]
    else:
        g_small = jnp.concatenate(
            [g_small[0].reshape(ndev, qkv_cols, feat), g_small[1].reshape(ndev, proj_cols, feat)],
            axis=1,
        )
        g_small = lax.psum_scatter(g_small, AXES).astype(F32)
        g_sdown = finish_shared(g_sdown)
    reduced[-1], g_sup = tie(reduced[-1], g_sup)
    sup_part = reduce_rows(g_sup).T.astype(F32)
    y_moved.append(to_plane(y_sent[2], plane_steps()[2]))
    d_cond = dot_nt(d_mod, ada_weight)
    d_cond_cols = d_cond.reshape(ndev, ndev, table_cols).transpose(1, 0, 2).reshape(ndev, -1)
    d_cond = jnp.concatenate([d_cond, d_cond_cols], axis=1)
    if packed:
        left[1], right[1], d_cond, *y_moved = tie(left[1], right[1], d_cond, *y_moved)
    d_cond = exchange(d_cond)
    last_up, last_down = finish_expert(reduced[-1])
    if packed:
        left, right, last_up, last_down = tie(add(left), add(right), last_up, last_down)
        g_small, g_moved = scatter_planes(jnp.concatenate([left, right], axis=-1), qkv_cols)
    else:
        g_moved = []
    d_cond, g_sdown, *y_moved = tie(d_cond, g_sdown, *y_moved)
    up_part = jnp.stack(up_part + [last_up])
    down_part = jnp.stack(down_part + [last_down])
    for part in y_moved:
        branch = branch + part.astype(F32)
    gates_grad = branch[rows, : 2 * rows].reshape(2, rows).T
    block_out = (middle + mod[5:6] * branch[:rows]).astype(BF16)
    d_cond = jnp.sum(d_cond, axis=0, keepdims=True)
    cond_grad = local_grad(jax.nn.silu, cond_own, d_cond[:, :feat])
    d_cond_cols = d_cond[:, feat:].reshape(ndev, table_cols)
    d_cond_cols = local_grad(jax.nn.silu, cond_cols, d_cond_cols)
    ada_part = dot_tn(silu_all, d_mod)
    bias_part = jnp.sum(d_mod.astype(F32), axis=0)
    sdown_part = g_sdown

    def table_grad(pick):
        return lax.dot_general(
            pick.astype(F32),
            d_cond_cols,
            (((0,), (0,)), ((), ())),
            precision=lax.Precision.HIGHEST,
            preferred_element_type=F32,
        )

    time_part, class_part = table_grad(pick_time), table_grad(pick_class)

    outs = [block_out, cond_grad, gates_grad, ada_part, bias_part, sup_part, sdown_part]
    outs += [up_part, down_part, time_part, class_part]
    if g_moved:
        *g_moved, outs = lax.optimization_barrier((*g_moved, outs))
    block_out, cond_grad, gates_grad, ada_part, bias_part, sup_part, sdown_part = outs[:7]
    up_part, down_part, time_part, class_part = outs[7:]
    for part in g_moved:
        g_small = g_small + part.astype(F32)
    qkv_part = g_small[:qkv_cols].T
    proj_part = g_small[qkv_cols:].T
    return (
        block_out,
        tokens_grad,
        cond_grad,
        gates_grad,
        ada_part,
        bias_part,
        qkv_part,
        proj_part,
        sup_part,
        sdown_part,
        up_part,
        down_part,
        time_part,
        class_part,
    )


def solution(mesh):
    both = ("dp", "expert")
    by_rows, by_cols, by_first = P(both, None), P(None, both), P(both)
    by_expert = P("expert", None, "dp")
    return jax.shard_map(
        local,
        mesh=mesh,
        in_specs=(
            by_rows,
            by_first,
            by_first,
            by_rows,
            by_rows,
            by_rows,
            by_cols,
            by_first,
            by_cols,
            by_cols,
            by_cols,
            by_cols,
            by_expert,
            by_expert,
            by_cols,
            by_cols,
        ),
        out_specs=(
            by_rows,
            by_rows,
            by_rows,
            by_rows,
            by_cols,
            by_first,
            by_cols,
            by_cols,
            by_cols,
            by_cols,
            by_expert,
            by_expert,
            by_cols,
            by_cols,
        ),
        check_vma=False,
    )
```
